256 devices in a mesh: gx: 16 (over z, core), gy: 16 (over x, y).
Axes of the slice: x: 4, y: 4, z: 8, core: 2. Of those that a mesh axis runs over, the one named last changes fastest.
Arguments:
- tables: float32 [4096, 32], P(('gx', 'gy')), may hold values from 0 to 8
- table_index: int32 [1024, 8192], P('gx', 'gy'), may hold values from 0 to 4095
- toggle: int32 [1024, 8192], P('gx', 'gy'), may hold values from 0 to 31
- tap_code: int32 [1024, 8192], P('gx', 'gy'), may hold values from 0 to 8
- capacitance: float32 [2, 1024, 8192], P(None, 'gx', 'gy'), may hold values from 0.02 to 0.2
- prior_drop: float32 [2, 1024, 8192], P(None, 'gx', 'gy'), may hold values from 0 to 0.5
Outputs:
- drop_first: float32 [2, 1024, 8192], P(None, 'gx', 'gy')
- drop_second: float32 [2, 1024, 8192], P(None, 'gx', 'gy')
The draws below stay inside these ranges and needn't reach their ends.
All inputs are finite; a program needn't handle non-finite values.
Results may differ from the reference program's by a relative error of at most 0.0003.
Values sent between devices are 32-bit elements; how exact they have to be, the bound alone decides.
No kernel may reach another device: no remote copies, remote signals or barrier semaphores. Data moves between devices by JAX's collectives and lax.ppermute only.
A program may use at most 64 MiB of HBM per device.

```python
import math
import jax
import jax.numpy as jnp
from jax import lax

SUBSTEPS = 32
STEPS = 2
ITERS = 3
NX = 1024
NY = 8192
NTAB = 4096


def touch_ends(values, rng, low, high):
    spot = [jax.random.randint(jax.random.fold_in(rng, axis), (), 0, length) for axis, length in enumerate(values.shape)]
    main_axis = values.shape.index(max(values.shape))
    next_to = spot[:main_axis] + [(spot[main_axis] + 1) % values.shape[main_axis]] + spot[main_axis + 1:]
    return values.at[tuple(spot)].set(low).at[tuple(next_to)].set(high)


def shard_levels(rng, extent, pieces, least, top_value):
    factor_of, own = 1.0, jax.random.fold_in(rng, 6)
    for axis_at, shards_of in pieces:
        draws = jnp.exp(jax.random.uniform(jax.random.fold_in(own, axis_at), (shards_of,), jnp.float32, least / len(pieces), top_value / len(pieces)))
        factor_of = factor_of * jnp.repeat(draws, extent[axis_at] // shards_of).reshape([-1 if axis == axis_at else 1 for axis in range(len(extent))])
    return factor_of


def setup_inputs(seed: int = 0) -> dict:
    streams_of = jax.random.split(jax.random.key(seed), 7)
    return {
        "tables": jnp.clip(8.0 * jax.random.uniform(streams_of[0], (NTAB, SUBSTEPS), jnp.float32) ** shard_levels(streams_of[0], (NTAB, SUBSTEPS), ((0, 256),), -0.2, 0.2), 0.0, 8.0),
        "table_index": touch_ends(jax.random.randint(streams_of[1], (NX, NY), 0, NTAB), jax.random.fold_in(streams_of[1], 1), 0, NTAB - 1).astype(jnp.int32),
        "toggle": touch_ends(jax.random.randint(streams_of[2], (NX, NY), 0, SUBSTEPS), jax.random.fold_in(streams_of[2], 1), 0, SUBSTEPS - 1).astype(jnp.int32),
        "tap_code": touch_ends(jax.random.randint(streams_of[3], (NX, NY), 0, 9), jax.random.fold_in(streams_of[3], 1), 0, 8).astype(jnp.int32),
        "capacitance": jnp.clip(jnp.exp(math.log(0.2) - 2.3025851 * jax.random.uniform(streams_of[4], (2, NX, NY), jnp.float32) ** shard_levels(streams_of[4], (2, NX, NY), ((1, 16), (2, 16)), -0.2, 0.2)), 0.02, 0.2),
        "prior_drop": jnp.clip(0.5 * jax.random.uniform(streams_of[5], (2, NX, NY), jnp.float32) ** shard_levels(streams_of[5], (2, NX, NY), ((1, 16), (2, 16)), -0.2, 0.2), 0.0, 0.5),
    }


def lateral_conductance():
    return jnp.array([1.0, 4.0], jnp.float32).reshape(2, 1, 1)


def chebyshev_taus():
    theta = 1.05
    delta = 0.95
    return [1.0 / (theta + delta * math.cos((2 * i - 1) * math.pi / 6.0)) for i in (1, 2, 3)]


def substep_weights():
    share = SUBSTEPS // STEPS
    rows = lax.broadcasted_iota(jnp.int32, (SUBSTEPS, SUBSTEPS * STEPS), 0)
    cols = lax.broadcasted_iota(jnp.int32, (SUBSTEPS, SUBSTEPS * STEPS), 1)
    moment = rows + cols // STEPS
    which = cols % STEPS
    valid = (moment < SUBSTEPS) & (moment // share == which)
    return jnp.where(valid, jnp.float32(1.0 / share), jnp.float32(0.0))


def apply_padded(padded, capacity):
    conduct = lateral_conductance()
    center = padded[:, 1:-1, 1:-1]
    beside = padded[:, :-2, 1:-1] + padded[:, 2:, 1:-1] + padded[:, 1:-1, :-2] + padded[:, 1:-1, 2:]
    return (capacity + 4.0 * conduct + 2.0) * center - conduct * beside - 2.0 * center[::-1]


def operate(field, capacity):
    return apply_padded(jnp.pad(field, ((0, 0), (1, 1), (1, 1))), capacity)


def precondition(resid, capacity, diagonal):
    taus = chebyshev_taus()
    first = taus[0] * resid / diagonal
    second = first + taus[1] * (resid - operate(first, capacity)) / diagonal
    return second + taus[2] * (resid - operate(second, capacity)) / diagonal


def solve(rhs, guess, capacity):
    diagonal = capacity + 4.0 * lateral_conductance() + 2.0
    drop = guess
    resid = rhs - operate(drop, capacity)
    conditioned = precondition(resid, capacity, diagonal)
    aligned = jnp.sum(resid * conditioned)
    direction = conditioned
    for turn in range(ITERS):
        image = operate(direction, capacity)
        step_size = aligned / jnp.sum(direction * image)
        drop = drop + step_size * direction
        resid = resid - step_size * image
        if turn + 1 < ITERS:
            conditioned = precondition(resid, capacity, diagonal)
            aligned_next = jnp.sum(resid * conditioned)
            direction = conditioned + (aligned_next / aligned) * direction
            aligned = aligned_next
    return drop


def reference(tables, table_index, toggle, tap_code, capacitance, prior_drop):
    capacity = capacitance
    expanded = jnp.dot(tables, substep_weights(), precision=lax.Precision.HIGHEST)
    flat = expanded.reshape(-1)
    base = table_index * (SUBSTEPS * STEPS) + toggle * STEPS
    charges = [jnp.take(flat, base + k) for k in range(STEPS)]
    stacked = jnp.stack(charges + [tap_code.astype(jnp.float32)])
    padded = jnp.pad(stacked, ((0, 0), (1, 1), (1, 1)))
    rows, cols = table_index.shape
    current = jnp.zeros((STEPS, rows, cols), jnp.float32)
    for shift_row in (-1, 0, 1):
        for shift_col in (-1, 0, 1):
            code = 3 * (shift_row + 1) + (shift_col + 1)
            source = padded[:, 1 - shift_row:1 - shift_row + rows, 1 - shift_col:1 - shift_col + cols]
            current = current + source[:STEPS] * (source[STEPS] == jnp.float32(code)).astype(jnp.float32)
    previous = prior_drop
    results = []
    empty = jnp.zeros((rows, cols), jnp.float32)
    for step in range(STEPS):
        rhs = capacity * previous + jnp.stack([current[step], empty])
        previous = solve(rhs, previous, capacity)
        results.append(previous)
    return results[0], results[1]
```

```python
import functools
import math

import jax
import jax.numpy as jnp
from jax import lax
from jax.experimental import pallas as pl
from jax.experimental.pallas import tpu as pltpu
from jax.sharding import PartitionSpec as P

SUBSTEPS = 32
STEPS = 2
BOTH = ("gx", "gy")
LANES = 128
HALO = 20
GROUP = 8
LO = 4
CONDUCT = (1.0, 4.0)


def chebyshev_taus():
    theta = 1.05
    delta = 0.95
    return [1.0 / (theta + delta * math.cos((2 * i - 1) * math.pi / 6.0)) for i in (1, 2, 3)]


TAU = chebyshev_taus()
ALPHA = TAU[1] + (1.0 - TAU[1]) * TAU[0]
BETA = TAU[0] * TAU[1]
KEEP = (1.0 - TAU[2]) * BETA / TAU[2]
SHIFT = 0.75
RADIUS = 0.7
BACK = SHIFT / TAU[2]
FORMER = 0.5 * (RADIUS / TAU[2]) ** 2


def params(mib):
    return pltpu.CompilerParams(vmem_limit_bytes=mib * 2**20)


def vmem():
    return pl.BlockSpec(memory_space=pltpu.VMEM)


def address_kernel(table_ref, out_ref):
    table = table_ref[...]
    many = table.shape[0] // LO
    block = jnp.concatenate([table[a * many : (a + 1) * many] for a in range(LO)], axis=1)
    out_ref[...] = jnp.broadcast_to(block[None], out_ref.shape)


def address(table, count):
    many = table.shape[0] // LO
    return pl.pallas_call(
        address_kernel,
        out_shape=jax.ShapeDtypeStruct((count, many, LANES), jnp.float32),
        in_specs=[vmem()],
        out_specs=vmem(),
        compiler_params=params(8),
        name="address",
    )(table)


MANY = 8
CHUNK = 256
UNROLL = 8


def split_kernel(table_refs, pieces_ref):
    for b, ref in enumerate(table_refs):
        across = ref[...].T
        high = across.astype(jnp.bfloat16)
        low = (across - high.astype(jnp.float32)).astype(jnp.bfloat16)
        for p, piece in enumerate((high, low)):
            pieces_ref[pl.ds((2 * p + b) * LANES, LANES), :] = piece


def charges(many, index, toggle, pieces_ref):
    many, inner = many
    cols = index.shape[1]
    groups = pieces_ref.shape[1]
    quarter = many // LO
    held = index & (many - 1)
    device = index // many
    half = (device // inner) & 1
    place = device // (2 * inner) * inner + (device & (inner - 1))
    row = place * quarter + (held & (quarter - 1))
    which = held // quarter + LO * half
    hot = []
    for k in range(groups // CHUNK):
        local = (row - CHUNK * k).astype(jnp.float32).astype(jnp.bfloat16)
        count = lax.broadcasted_iota(jnp.int32, (CHUNK, cols), 0)
        count = count.astype(jnp.float32).astype(jnp.bfloat16)
        same = jnp.broadcast_to(local, (CHUNK, cols)) == count
        hot.append(jnp.where(same, jnp.bfloat16(1), jnp.bfloat16(0)))
    got = jnp.dot(pieces_ref[...], jnp.concatenate(hot, 0), preferred_element_type=jnp.float32)
    half = got.shape[0] // 2
    value = (got[:half] + got[half:]).reshape(MANY, SUBSTEPS, cols)
    chosen = value[0]
    for a in range(1, MANY):
        chosen = jnp.where(which == a, value[a], chosen)
    moment = lax.broadcasted_iota(jnp.int32, (SUBSTEPS, cols), 0) + toggle
    share = SUBSTEPS // STEPS
    means = []
    for k in range(STEPS):
        inside = (moment >= k * share) & (moment < (k + 1) * share)
        total = jnp.sum(jnp.where(inside, chosen, 0.0), axis=0, keepdims=True)
        means.append(total * (1.0 / share))
    return means


def lookup_rows(many, index_ref, toggle_ref, pieces_ref, out_ref):
    rows, cols = index_ref.shape

    def body(i, carry):
        for u in range(UNROLL):
            row = pl.ds(i * UNROLL + u, 1)
            means = charges(many, index_ref[row, :], toggle_ref[row, :], pieces_ref)
            for k, mean in enumerate(means):
                for b in range(cols // LANES):
                    out_ref[k, b, row, :] = mean[:, b * LANES : (b + 1) * LANES]
        return carry

    lax.fori_loop(0, rows // UNROLL, body, 0)


def first_lookup_kernel(many, index_ref, toggle_ref, own_ref, other_ref, out_ref, pieces_ref):
    split_kernel((own_ref, other_ref), pieces_ref)
    lookup_rows(many, index_ref, toggle_ref, pieces_ref, out_ref)


def lookup_cost(cells, pieces):
    flops = 2 * cells * pieces.shape[0] * pieces.shape[1]
    return pl.CostEstimate(flops=flops, bytes_accessed=0, transcendentals=0)


def lookup(index, toggle, table, many):
    rows, cols = index.shape
    charge = jax.ShapeDtypeStruct((STEPS, cols // LANES, rows, LANES), jnp.float32)
    fresh = len(table) == 2
    pieces = table[0]
    if fresh:
        pieces = jax.ShapeDtypeStruct((2 * MANY * SUBSTEPS, pieces.shape[0]), jnp.bfloat16)
    return pl.pallas_call(
        functools.partial(first_lookup_kernel if fresh else lookup_rows, many),
        out_shape=[charge, pieces] if fresh else charge,
        in_specs=[vmem()] * (2 + len(table)),
        out_specs=[vmem()] * 2 if fresh else vmem(),
        compiler_params=params(20),
        cost_estimate=lookup_cost(rows * cols, pieces),
        name="lookup",
    )(index, toggle, *table)


def edge_lookup_kernel(many, left_ref, right_ref, pieces_ref, out_ref, cells_ref, got_ref):
    rows = left_ref.shape[1]
    lane = lax.broadcasted_iota(jnp.int32, (rows, LANES), 1)

    def merge(right, left):
        return jnp.where(lane < HALO, right, jnp.where(lane >= LANES - HALO, left, 0.0))

    for f in range(5):
        out_ref[f] = merge(right_ref[f], left_ref[f])
    pair = lax.broadcasted_iota(jnp.int32, (HALO, LANES), 1)
    for n in range(2):
        near = pltpu.roll(merge(right_ref[5 + n], left_ref[5 + n]), HALO, axis=1)
        turned = jnp.concatenate([near, jnp.zeros_like(near)], axis=0).T
        high = pltpu.roll(turned[HALO : 2 * HALO], LANES - rows, axis=1)
        cells_ref[n] = jnp.where(pair < rows, turned[:HALO], high).astype(jnp.int32)
    got_ref[...] = jnp.zeros_like(got_ref)
    step = 4
    for u in range(HALO // step):
        index, toggle = [
            jnp.concatenate([cells_ref[n, pl.ds(step * u + r, 1), :] for r in range(step)], axis=1)
            for n in range(2)
        ]
        for k, mean in enumerate(charges(many, index, toggle, pieces_ref)):
            for r in range(step):
                got_ref[k, pl.ds(step * u + r, 1), :] = mean[:, r * LANES : (r + 1) * LANES]
    inside = out_ref[0] > 0.0
    for k in range(STEPS):
        back = got_ref[k].T
        left = pltpu.roll(back[:rows], LANES - HALO, axis=1)
        out_ref[5 + k] = jnp.where(inside, merge(back[rows:], left), 0.0)


def edge_lookup(left, right, pieces, many):
    rows = left.shape[1]
    assert 2 * rows == LANES
    return pl.pallas_call(
        functools.partial(edge_lookup_kernel, many),
        out_shape=jax.ShapeDtypeStruct(left.shape, jnp.float32),
        in_specs=[vmem()] * 3,
        out_specs=vmem(),
        scratch_shapes=[
            pltpu.VMEM((2, HALO, LANES), jnp.int32),
            pltpu.VMEM((STEPS, LANES, LANES), jnp.float32),
        ],
        compiler_params=params(20),
        cost_estimate=lookup_cost(2 * HALO * rows, pieces),
        name="edge_lookup",
    )(left, right, pieces)


def sweep(deep, fetch, use):
    def load(i):
        if i < 0:
            return [pltpu.roll(fetch(l, deep - 1), 1, axis=0) for l in range(2)]
        if i >= deep:
            return [pltpu.roll(fetch(l, 0), GROUP - 1, axis=0) for l in range(2)]
        return [fetch(l, i) for l in range(2)]

    held = {}
    for i in range(deep):
        held = {k: v for k, v in held.items() if k in (i - 1, i, i + 1)}
        for k in (i - 1, i, i + 1):
            if k not in held:
                held[k] = load(k)
        for l in range(2):
            center = held[i][l]
            width = center.shape[-1]
            beside = pltpu.roll(center, 1, axis=1) + pltpu.roll(center, width - 1, axis=1)
            around = (held[i - 1][l] + held[i + 1][l]) + beside
            use(l, i, center, around, held[i][1 - l])


def weigh(cap_ref, deep, grid_ref, cross_ref):
    for l in range(2):
        for i in range(deep):
            cap = cap_ref[l, i]
            inverse = jnp.where(cap > 0.0, 1.0 / (cap + (4.0 * CONDUCT[l] + 2.0)), 0.0)
            grid_ref[l, i] = CONDUCT[l] * inverse
            cross_ref[l, i] = 2.0 * inverse


def residual(deep, drop_ref, current, cross_ref, width, start_ref, scaled_ref):
    def use(l, i, center, around, other):
        value = CONDUCT[l] * around + 2.0 * other - (4.0 * CONDUCT[l] + 2.0) * center
        if l == 0:
            value = value + current(i)
        start_ref[l, i] = value[:, :width]
        scaled_ref[l, i] = value * (cross_ref[l, i] * 0.5)

    sweep(deep, lambda l, i: drop_ref[l, i], use)


def krylov(deep, width, cap_ref, grid_ref, cross_ref, scaled_ref, second_ref, basis_ref, image_ref):
    def coupled(l, i, around, other):
        return grid_ref[l, i] * around + cross_ref[l, i] * other

    def use_second(l, i, center, around, other):
        second_ref[l, i] = (ALPHA / BETA) * center + coupled(l, i, around, other)

    for n in range(3):

        def use_basis(l, i, center, around, other, n=n):
            value = KEEP * center + (
                scaled_ref[l, i] + BETA * coupled(l, i, around, other)
            )
            if n == 1:
                value = value - BACK * basis_ref[0, l, i]
            if n == 2:
                value = value - BACK * basis_ref[1, l, i] - FORMER * basis_ref[0, l, i]
            basis_ref[n, l, i] = value

        def use_image(l, i, center, around, other, n=n):
            value = center - coupled(l, i, around, other)
            if n < 2:
                scaled_ref[l, i] = value
            diagonal = cap_ref[l, i][:, :width] + (4.0 * CONDUCT[l] + 2.0)
            image_ref[n, l, i] = value[:, :width] * diagonal

        sweep(deep, lambda l, i: scaled_ref[l, i], use_second)
        sweep(deep, lambda l, i: second_ref[l, i], use_basis)
        sweep(deep, lambda l, i, n=n: basis_ref[n, l, i], use_image)


PAIRS = ((0, 0), (1, 0), (2, 0), (1, 1), (2, 1), (2, 2))


def moments(deep, rows, width, start_ref, basis_ref, image_ref, sums_ref, out_ref):
    sub = lax.broadcasted_iota(jnp.int32, (GROUP, LANES), 0)

    def body(i, totals):
        inside = sub * deep + i < rows
        part = [None] * 9
        for l in range(2):
            for b in range(width // LANES):
                lanes = pl.ds(b * LANES, LANES)
                start = start_ref[l, i, :, lanes]
                basis = [basis_ref[n, l, i, :, lanes] for n in range(3)]
                image = [image_ref[n, l, i, :, lanes] for n in range(3)]
                terms = [start * v for v in basis] + [basis[p] * image[q] for p, q in PAIRS]
                part = [t if p is None else p + t for p, t in zip(part, terms)]
        return [t + jnp.where(inside, p, 0.0) for t, p in zip(totals, part)]

    totals = lax.fori_loop(0, deep, body, [jnp.zeros((GROUP, LANES), jnp.float32)] * 9)
    sums_ref[...] = jnp.zeros_like(sums_ref)
    for k, total in enumerate(totals):
        sums_ref[pl.ds(k, 1), :] = jnp.sum(total, axis=0, keepdims=True)
    row = lax.dot_general(
        jnp.ones((GROUP, LANES), jnp.float32),
        sums_ref[...],
        (((1,), (1,)), ((), ())),
        precision=lax.Precision.HIGHEST,
        preferred_element_type=jnp.float32,
    )
    out_ref[...] = jnp.broadcast_to(row[:1], out_ref.shape)


def weights_of(gathered_ref, spread_ref):
    total = jnp.sum(gathered_ref[...], axis=0, keepdims=True)
    row = lax.broadcasted_iota(jnp.int32, (LANES, LANES), 0)
    lane = lax.broadcasted_iota(jnp.int32, (LANES, LANES), 1)
    spread_ref[...] = lax.dot_general(
        jnp.where(row == lane, jnp.broadcast_to(total, (LANES, LANES)), 0.0),
        jnp.ones((LANES, LANES), jnp.float32),
        (((1,), (0,)), ((), ())),
        precision=lax.Precision.HIGHEST,
        preferred_element_type=jnp.float32,
    )
    b1, b2, b3, h11, h21, h31, h22, h32, h33 = [
        jnp.broadcast_to(spread_ref[pl.ds(k, 1), :], (GROUP, LANES)) for k in range(9)
    ]
    l21 = h21 / h11
    l31 = h31 / h11
    d2 = h22 - l21 * h21
    e32 = h32 - l31 * h21
    l32 = e32 / d2
    d3 = h33 - l31 * h31 - l32 * e32
    y2 = b2 - l21 * b1
    y3 = b3 - l31 * b1 - l32 * y2
    c3 = y3 / d3
    c2 = y2 / d2 - l32 * c3
    c1 = b1 / h11 - l21 * c2 - l31 * c3
    return c1, c2, c3


def widen(value, width):
    return jnp.concatenate([value] * (width // LANES), axis=1)


def spread(natural_ref, l, i, deep, value):
    for b in range(value.shape[1] // LANES):
        natural_ref[l, b, pl.ds(i, GROUP, stride=deep), :] = value[:, b * LANES : (b + 1) * LANES]


def settle(natural_ref, out_ref):
    for b in range(natural_ref.shape[1]):
        out_ref[:, :, pl.ds(b * LANES, LANES)] = natural_ref[:, b, : out_ref.shape[1], :]


def first_kernel(
    deep, rows, width, outer,
    field_ref, edge_ref, above_ref, below_ref, ends_ref, middle_ref,
    basis_ref, drop_ref, cap_ref, later_ref, out_ref,
    whole_ref, grid_ref, cross_ref, start_ref, scaled_ref, second_ref, image_ref, inject_ref, sums_ref,
):
    wide = width + LANES
    blocks = wide // LANES
    inner = pl.ds(0, rows)
    for f in range(7):
        whole_ref[f, blocks - 1, inner, :] = edge_ref[f]
        for b in range(blocks - 1):
            if f < 5:
                whole_ref[f, b, inner, :] = field_ref[f, b]
            else:
                end, middle = ends_ref.at[f - 5, b], middle_ref.at[f - 5, b]
                whole_ref[f, b, pl.ds(0, outer), :] = end[pl.ds(0, outer), :]
                whole_ref[f, b, pl.ds(outer, rows - 2 * outer), :] = middle[...]
                whole_ref[f, b, pl.ds(rows - outer, outer), :] = end[pl.ds(outer, outer), :]
        for ref, place in ((below_ref, pl.ds(rows, HALO)), (above_ref, pl.ds(rows + HALO, HALO))):
            for b in range(blocks - 1):
                whole_ref[f, b, place, :] = ref[f * (blocks - 1) + b]
            whole_ref[f, blocks - 1, place, :] = ref[7 * (blocks - 1) + f]

    def slab(f, i):
        pick = pl.ds(i, GROUP, stride=deep)
        return jnp.concatenate([whole_ref[f, b, pick, :] for b in range(blocks)], axis=1)

    for l in range(2):
        for i in range(deep):
            cap_ref[l, i] = slab(l, i)
            drop_ref[l, i] = slab(2 + l, i)
    weigh(cap_ref, deep, grid_ref, cross_ref)
    for i in range(deep):
        tap = slab(4, i)
        for k in range(STEPS):
            charge = slab(5 + k, i)
            for a in range(3):
                sent = [jnp.where(tap == float(3 * a + b), charge, 0.0) for b in range(3)]
                value = pltpu.roll(sent[0], wide - 1, axis=1) + sent[1] + pltpu.roll(sent[2], 1, axis=1)
                inject_ref[k, a, i] = value

    def current(k, i):
        if i == deep - 1:
            upward = pltpu.roll(inject_ref[k, 0, 0], GROUP - 1, axis=0)
        else:
            upward = inject_ref[k, 0, i + 1]
        if i == 0:
            downward = pltpu.roll(inject_ref[k, 2, deep - 1], 1, axis=0)
        else:
            downward = inject_ref[k, 2, i - 1]
        return upward + inject_ref[k, 1, i] + downward

    for i in range(deep):
        later_ref[i] = current(1, i)
    residual(deep, drop_ref, lambda i: current(0, i), cross_ref, width, start_ref, scaled_ref)
    krylov(deep, width, cap_ref, grid_ref, cross_ref, scaled_ref, second_ref, basis_ref, image_ref)
    moments(deep, rows, width, start_ref, basis_ref, image_ref, sums_ref, out_ref)


def first_step(field, edge, above, below, ends, middle, count):
    rows = field.shape[2]
    width = field.shape[1] * LANES
    wide = width + LANES
    deep = (rows + 2 * HALO) // GROUP
    full = (2, deep, GROUP, wide)
    shapes = [(3, *full), full, full, full[1:], (count, LANES)]
    return pl.pallas_call(
        functools.partial(first_kernel, deep, rows, width, ends.shape[2] // 2),
        out_shape=[jax.ShapeDtypeStruct(s, jnp.float32) for s in shapes],
        in_specs=[vmem()] * 6,
        out_specs=[vmem()] * len(shapes),
        scratch_shapes=[
            pltpu.VMEM((7, wide // LANES, deep * GROUP, LANES), jnp.float32),
            pltpu.VMEM(full, jnp.float32),
            pltpu.VMEM(full, jnp.float32),
            pltpu.VMEM((2, deep, GROUP, width), jnp.float32),
            pltpu.VMEM(full, jnp.float32),
            pltpu.VMEM(full, jnp.float32),
            pltpu.VMEM((3, 2, deep, GROUP, width), jnp.float32),
            pltpu.VMEM((STEPS, 3, *full[1:]), jnp.float32),
            pltpu.VMEM((LANES, LANES), jnp.float32),
        ],
        compiler_params=params(20),
        name="first_step",
    )(field, edge, above, below, ends, middle)


def second_kernel(
    deep, rows, width,
    gathered_ref, basis_ref, drop_ref, cap_ref, later_ref,
    first_ref, next_ref, held_ref, out_ref,
    now_ref, grid_ref, cross_ref, start_ref, scaled_ref, second_ref, image_ref, natural_ref, sums_ref,
):
    wide = width + LANES
    weigh(cap_ref, deep, grid_ref, cross_ref)
    weights = [widen(c, wide) for c in weights_of(gathered_ref, sums_ref)]
    for l in range(2):
        for i in range(deep):
            value = drop_ref[l, i]
            for n in range(3):
                value = value + weights[n] * basis_ref[n, l, i]
            now_ref[l, i] = value
            held_ref[l, i] = value[:, :width]
            spread(natural_ref, l, i, deep, value[:, :width])
    settle(natural_ref, first_ref)
    residual(deep, now_ref, lambda i: later_ref[i], cross_ref, width, start_ref, scaled_ref)
    krylov(deep, width, cap_ref, grid_ref, cross_ref, scaled_ref, second_ref, next_ref, image_ref)
    moments(deep, rows, width, start_ref, next_ref, image_ref, sums_ref, out_ref)


def second_step(gathered, basis, drop, cap, later, rows):
    deep = cap.shape[1]
    wide = cap.shape[-1]
    width = wide - LANES
    full = (2, deep, GROUP, wide)
    shapes = [(2, rows, width), (3, *full), (2, deep, GROUP, width), gathered.shape]
    return pl.pallas_call(
        functools.partial(second_kernel, deep, rows, width),
        out_shape=[jax.ShapeDtypeStruct(s, jnp.float32) for s in shapes],
        in_specs=[vmem()] * 5,
        out_specs=[vmem()] * len(shapes),
        scratch_shapes=[
            pltpu.VMEM(full, jnp.float32),
            pltpu.VMEM(full, jnp.float32),
            pltpu.VMEM(full, jnp.float32),
            pltpu.VMEM((2, deep, GROUP, width), jnp.float32),
            pltpu.VMEM(full, jnp.float32),
            pltpu.VMEM(full, jnp.float32),
            pltpu.VMEM((3, 2, deep, GROUP, width), jnp.float32),
            pltpu.VMEM((2, width // LANES, deep * GROUP, LANES), jnp.float32),
            pltpu.VMEM((LANES, LANES), jnp.float32),
        ],
        compiler_params=params(20),
        name="second_step",
    )(gathered, basis, drop, cap, later)


def last_kernel(deep, rows, width, gathered_ref, basis_ref, held_ref, out_ref, natural_ref, sums_ref):
    weights = [widen(c, width) for c in weights_of(gathered_ref, sums_ref)]
    for l in range(2):
        for i in range(deep):
            value = held_ref[l, i]
            for n in range(3):
                value = value + weights[n] * basis_ref[n, l, i, :, pl.ds(0, width)]
            spread(natural_ref, l, i, deep, value)
    settle(natural_ref, out_ref)


def last_step(gathered, basis, held, rows):
    deep = held.shape[1]
    width = held.shape[-1]
    return pl.pallas_call(
        functools.partial(last_kernel, deep, rows, width),
        out_shape=jax.ShapeDtypeStruct((2, rows, width), jnp.float32),
        in_specs=[vmem()] * 3,
        out_specs=vmem(),
        scratch_shapes=[
            pltpu.VMEM((2, width // LANES, deep * GROUP, LANES), jnp.float32),
            pltpu.VMEM((LANES, LANES), jnp.float32),
        ],
        compiler_params=params(12),
        name="last_step",
    )(gathered, basis, held)


def shift(block, axis, up):
    count = lax.axis_size(axis)
    pairs = [(i, i + 1) for i in range(count - 1)]
    return lax.ppermute(block, axis, pairs if up else [(b, a) for a, b in pairs])


def exchange(block):
    return lax.all_to_all(block, BOTH, 0, 0, tiled=True)


def gather_tables(tables):
    outer, inner = lax.axis_size("gx"), lax.axis_size("gy")
    groups = [
        [x * inner + y for x in range(parity, outer, 2) for y in range(inner)] for parity in range(2)
    ]
    block = address(tables, outer * inner // 2)
    own = lax.all_to_all(block, BOTH, 0, 0, tiled=True, axis_index_groups=groups)
    own = own.reshape(-1, LANES)
    return own, lax.ppermute(own, "gx", [(i, i ^ 1) for i in range(outer)])


def shards(tables, table_index, toggle, tap_code, capacitance, prior_drop):
    rows, cols = table_index.shape
    count = lax.axis_size("gx") * lax.axis_size("gy")
    inner = lax.axis_size("gy")
    many = tables.shape[0], inner
    outer = HALO
    table = gather_tables(tables)
    table_index = table_index ^ ((lax.axis_index("gx") & 1) * (inner * tables.shape[0]))
    codes = [a.astype(jnp.float32)[None] for a in (tap_code, table_index, toggle)]
    field = jnp.concatenate([capacitance, prior_drop, *codes])
    field = field.reshape(-1, rows, cols // LANES, LANES).transpose(0, 2, 1, 3)
    left = shift(field[:, -1], "gy", True)
    right = shift(field[:, 0], "gy", False)
    def ends_of(array):
        return jnp.concatenate([array[:outer], array[-outer:]])

    ends, pieces = lookup(ends_of(table_index), ends_of(toggle), table, many)
    edge = edge_lookup(left, right, pieces, many)

    def late(far):
        cut = slice(-HALO, None) if far else slice(0, HALO)
        charge, lower = [a[:, :, cut].reshape(-1, HALO, LANES) for a in (ends, field[:5])]
        return jnp.concatenate([lower, charge, edge[:, cut]])

    above = shift(late(True), "gx", True)
    below = shift(late(False), "gx", False)
    pieces, edge = lax.optimization_barrier((pieces, edge))
    middle = lookup(table_index[outer:-outer], toggle[outer:-outer], (pieces,), many)
    basis, drop, cap, later, part = first_step(field, edge, above, below, ends, middle, count)
    first, basis, held, part = second_step(exchange(part), basis, drop, cap, later, rows)
    return first, last_step(exchange(part), basis, held, rows)


def solution(mesh):
    in_specs = (
        P(BOTH, None),
        P("gx", "gy"),
        P("gx", "gy"),
        P("gx", "gy"),
        P(None, "gx", "gy"),
        P(None, "gx", "gy"),
    )
    out_specs = (P(None, "gx", "gy"), P(None, "gx", "gy"))
    return jax.shard_map(shards, mesh=mesh, in_specs=in_specs, out_specs=out_specs, check_vma=False)
```

```python
import functools
import math

import jax
import jax.numpy as jnp
from jax import lax
from jax.experimental import pallas as pl
from jax.experimental.pallas import tpu as pltpu
from jax.sharding import PartitionSpec as P

SUBSTEPS = 32
STEPS = 2
BOTH = ("gx", "gy")
LANES = 128
HALO = 20
GROUP = 8
LO = 4
CONDUCT = (1.0, 4.0)


def chebyshev_taus():
    theta = 1.05
    delta = 0.95
    return [1.0 / (theta + delta * math.cos((2 * i - 1) * math.pi / 6.0)) for i in (1, 2, 3)]


TAU = chebyshev_taus()
ALPHA = TAU[1] + (1.0 - TAU[1]) * TAU[0]
BETA = TAU[0] * TAU[1]
KEEP = (1.0 - TAU[2]) * BETA / TAU[2]
SHIFT = 0.75
RADIUS = 0.7
BACK = SHIFT / TAU[2]
FORMER = 0.5 * (RADIUS / TAU[2]) ** 2


def params(mib):
    return pltpu.CompilerParams(vmem_limit_bytes=mib * 2**20)


def vmem():
    return pl.BlockSpec(memory_space=pltpu.VMEM)


def address_kernel(table_ref, out_ref):
    table = table_ref[...]
    many = table.shape[0] // LO
    block = jnp.concatenate([table[a * many : (a + 1) * many] for a in range(LO)], axis=1)
    out_ref[...] = jnp.broadcast_to(block[None], out_ref.shape)


def address(table, count):
    many = table.shape[0] // LO
    return pl.pallas_call(
        address_kernel,
        out_shape=jax.ShapeDtypeStruct((count, many, LANES), jnp.float32),
        in_specs=[vmem()],
        out_specs=vmem(),
        compiler_params=params(8),
        name="address",
    )(table)


MANY = 8
CHUNK = 256
UNROLL = 8


def split_kernel(table_refs, pieces_ref):
    for b, ref in enumerate(table_refs):
        across = ref[...].T
        high = across.astype(jnp.bfloat16)
        low = (across - high.astype(jnp.float32)).astype(jnp.bfloat16)
        for p, piece in enumerate((high, low)):
            pieces_ref[pl.ds((2 * p + b) * LANES, LANES), :] = piece


def charges(many, index, toggle, pieces_ref):
    many, inner = many
    cols = index.shape[1]
    groups = pieces_ref.shape[1]
    quarter = many // LO
    held = index & (many - 1)
    device = index // many
    half = (device // inner) & 1
    place = device // (2 * inner) * inner + (device & (inner - 1))
    row = place * quarter + (held & (quarter - 1))
    which = held // quarter + LO * half
    hot = []
    for k in range(groups // CHUNK):
        local = (row - CHUNK * k).astype(jnp.float32).astype(jnp.bfloat16)
        count = lax.broadcasted_iota(jnp.int32, (CHUNK, cols), 0)
        count = count.astype(jnp.float32).astype(jnp.bfloat16)
        same = jnp.broadcast_to(local, (CHUNK, cols)) == count
        hot.append(jnp.where(same, jnp.bfloat16(1), jnp.bfloat16(0)))
    got = jnp.dot(pieces_ref[...], jnp.concatenate(hot, 0), preferred_element_type=jnp.float32)
    half = got.shape[0] // 2
    value = (got[:half] + got[half:]).reshape(MANY, SUBSTEPS, cols)
    chosen = value[0]
    for a in range(1, MANY):
        chosen = jnp.where(which == a, value[a], chosen)
    moment = lax.broadcasted_iota(jnp.int32, (SUBSTEPS, cols), 0) + toggle
    share = SUBSTEPS // STEPS
    means = []
    for k in range(STEPS):
        inside = (moment >= k * share) & (moment < (k + 1) * share)
        total = jnp.sum(jnp.where(inside, chosen, 0.0), axis=0, keepdims=True)
        means.append(total * (1.0 / share))
    return means


def lookup_rows(many, index_ref, toggle_ref, pieces_ref, out_ref):
    rows, cols = index_ref.shape

    def body(i, carry):
        for u in range(UNROLL):
            row = pl.ds(i * UNROLL + u, 1)
            means = charges(many, index_ref[row, :], toggle_ref[row, :], pieces_ref)
            for k, mean in enumerate(means):
                for b in range(cols // LANES):
                    out_ref[k, b, row, :] = mean[:, b * LANES : (b + 1) * LANES]
        return carry

    lax.fori_loop(0, rows // UNROLL, body, 0)


def first_lookup_kernel(many, index_ref, toggle_ref, own_ref, other_ref, out_ref, pieces_ref):
    split_kernel((own_ref, other_ref), pieces_ref)
    lookup_rows(many, index_ref, toggle_ref, pieces_ref, out_ref)


def lookup_cost(cells, pieces):
    flops = 2 * cells * pieces.shape[0] * pieces.shape[1]
    return pl.CostEstimate(flops=flops, bytes_accessed=0, transcendentals=0)


def lookup(index, toggle, table, many):
    rows, cols = index.shape
    charge = jax.ShapeDtypeStruct((STEPS, cols // LANES, rows, LANES), jnp.float32)
    fresh = len(table) == 2
    pieces = table[0]
    if fresh:
        pieces = jax.ShapeDtypeStruct((2 * MANY * SUBSTEPS, pieces.shape[0]), jnp.bfloat16)
    return pl.pallas_call(
        functools.partial(first_lookup_kernel if fresh else lookup_rows, many),
        out_shape=[charge, pieces] if fresh else charge,
        in_specs=[vmem()] * (2 + len(table)),
        out_specs=[vmem()] * 2 if fresh else vmem(),
        compiler_params=params(20),
        cost_estimate=lookup_cost(rows * cols, pieces),
        name="lookup",
    )(index, toggle, *table)


def edge_lookup_kernel(many, left_ref, right_ref, pieces_ref, out_ref, cells_ref, got_ref):
    rows = left_ref.shape[1]
    lane = lax.broadcasted_iota(jnp.int32, (rows, LANES), 1)

    def merge(right, left):
        return jnp.where(lane < HALO, right, jnp.where(lane >= LANES - HALO, left, 0.0))

    for f in range(5):
        out_ref[f] = merge(right_ref[f], left_ref[f])
    pair = lax.broadcasted_iota(jnp.int32, (HALO, LANES), 1)
    for n in range(2):
        near = pltpu.roll(merge(right_ref[5 + n], left_ref[5 + n]), HALO, axis=1)
        turned = jnp.concatenate([near, jnp.zeros_like(near)], axis=0).T
        high = pltpu.roll(turned[HALO : 2 * HALO], LANES - rows, axis=1)
        cells_ref[n] = jnp.where(pair < rows, turned[:HALO], high).astype(jnp.int32)
    got_ref[...] = jnp.zeros_like(got_ref)
    step = 4
    for u in range(HALO // step):
        index, toggle = [
            jnp.concatenate([cells_ref[n, pl.ds(step * u + r, 1), :] for r in range(step)], axis=1)
            for n in range(2)
        ]
        for k, mean in enumerate(charges(many, index, toggle, pieces_ref)):
            for r in range(step):
                got_ref[k, pl.ds(step * u + r, 1), :] = mean[:, r * LANES : (r + 1) * LANES]
    inside = out_ref[0] > 0.0
    for k in range(STEPS):
        back = got_ref[k].T
        left = pltpu.roll(back[:rows], LANES - HALO, axis=1)
        out_ref[5 + k] = jnp.where(inside, merge(back[rows:], left), 0.0)


def edge_lookup(left, right, pieces, many):
    rows = left.shape[1]
    assert 2 * rows == LANES
    return pl.pallas_call(
        functools.partial(edge_lookup_kernel, many),
        out_shape=jax.ShapeDtypeStruct(left.shape, jnp.float32),
        in_specs=[vmem()] * 3,
        out_specs=vmem(),
        scratch_shapes=[
            pltpu.VMEM((2, HALO, LANES), jnp.int32),
            pltpu.VMEM((STEPS, LANES, LANES), jnp.float32),
        ],
        compiler_params=params(20),
        cost_estimate=lookup_cost(2 * HALO * rows, pieces),
        name="edge_lookup",
    )(left, right, pieces)


def sweep(deep, fetch, use):
    def load(i):
        if i < 0:
            return [pltpu.roll(fetch(l, deep - 1), 1, axis=0) for l in range(2)]
        if i >= deep:
            return [pltpu.roll(fetch(l, 0), GROUP - 1, axis=0) for l in range(2)]
        return [fetch(l, i) for l in range(2)]

    held = {}
    for i in range(deep):
        held = {k: v for k, v in held.items() if k in (i - 1, i, i + 1)}
        for k in (i - 1, i, i + 1):
            if k not in held:
                held[k] = load(k)
        for l in range(2):
            center = held[i][l]
            width = center.shape[-1]
            beside = pltpu.roll(center, 1, axis=1) + pltpu.roll(center, width - 1, axis=1)
            around = (held[i - 1][l] + held[i + 1][l]) + beside
            use(l, i, center, around, held[i][1 - l])


def weigh(cap_ref, deep, grid_ref, cross_ref):
    for l in range(2):
        for i in range(deep):
            cap = cap_ref[l, i]
            inverse = jnp.where(cap > 0.0, 1.0 / (cap + (4.0 * CONDUCT[l] + 2.0)), 0.0)
            grid_ref[l, i] = CONDUCT[l] * inverse
            cross_ref[l, i] = 2.0 * inverse


def residual(deep, drop_ref, current, cross_ref, width, start_ref, scaled_ref):
    def use(l, i, center, around, other):
        value = CONDUCT[l] * around + 2.0 * other - (4.0 * CONDUCT[l] + 2.0) * center
        if l == 0:
            value = value + current(i)
        start_ref[l, i] = value[:, :width]
        scaled_ref[l, i] = value * (cross_ref[l, i] * 0.5)

    sweep(deep, lambda l, i: drop_ref[l, i], use)


def krylov(deep, width, cap_ref, grid_ref, cross_ref, scaled_ref, second_ref, basis_ref, image_ref):
    def coupled(l, i, around, other):
        return grid_ref[l, i] * around + cross_ref[l, i] * other

    def use_second(l, i, center, around, other):
        second_ref[l, i] = (ALPHA / BETA) * center + coupled(l, i, around, other)

    for n in range(3):

        def use_basis(l, i, center, around, other, n=n):
            value = KEEP * center + (
                scaled_ref[l, i] + BETA * coupled(l, i, around, other)
            )
            if n == 1:
                value = value - BACK * basis_ref[0, l, i]
            if n == 2:
                value = value - BACK * basis_ref[1, l, i] - FORMER * basis_ref[0, l, i]
            basis_ref[n, l, i] = value

        def use_image(l, i, center, around, other, n=n):
            value = center - coupled(l, i, around, other)
            if n < 2:
                scaled_ref[l, i] = value
            diagonal = cap_ref[l, i][:, :width] + (4.0 * CONDUCT[l] + 2.0)
            image_ref[n, l, i] = value[:, :width] * diagonal

        sweep(deep, lambda l, i: scaled_ref[l, i], use_second)
        sweep(deep, lambda l, i: second_ref[l, i], use_basis)
        sweep(deep, lambda l, i, n=n: basis_ref[n, l, i], use_image)


PAIRS = ((0, 0), (1, 0), (2, 0), (1, 1), (2, 1), (2, 2))


def moments(deep, rows, width, start_ref, basis_ref, image_ref, sums_ref, out_ref):
    sub = lax.broadcasted_iota(jnp.int32, (GROUP, LANES), 0)

    def body(i, totals):
        inside = sub * deep + i < rows
        part = [None] * 9
        for l in range(2):
            for b in range(width // LANES):
                lanes = pl.ds(b * LANES, LANES)
                start = start_ref[l, i, :, lanes]
                basis = [basis_ref[n, l, i, :, lanes] for n in range(3)]
                image = [image_ref[n, l, i, :, lanes] for n in range(3)]
                terms = [start * v for v in basis] + [basis[p] * image[q] for p, q in PAIRS]
                part = [t if p is None else p + t for p, t in zip(part, terms)]
        return [t + jnp.where(inside, p, 0.0) for t, p in zip(totals, part)]

    totals = lax.fori_loop(0, deep, body, [jnp.zeros((GROUP, LANES), jnp.float32)] * 9)
    sums_ref[...] = jnp.zeros_like(sums_ref)
    for k, total in enumerate(totals):
        sums_ref[pl.ds(k, 1), :] = jnp.sum(total, axis=0, keepdims=True)
    row = lax.dot_general(
        jnp.ones((GROUP, LANES), jnp.float32),
        sums_ref[...],
        (((1,), (1,)), ((), ())),
        precision=lax.Precision.HIGHEST,
        preferred_element_type=jnp.float32,
    )
    out_ref[...] = jnp.broadcast_to(row[:1], out_ref.shape)


def weights_of(own_ref, other_ref, spread_ref):
    total = jnp.sum(own_ref[...], axis=0, keepdims=True) + jnp.sum(other_ref[...], axis=0, keepdims=True)
    row = lax.broadcasted_iota(jnp.int32, (LANES, LANES), 0)
    lane = lax.broadcasted_iota(jnp.int32, (LANES, LANES), 1)
    spread_ref[...] = lax.dot_general(
        jnp.where(row == lane, jnp.broadcast_to(total, (LANES, LANES)), 0.0),
        jnp.ones((LANES, LANES), jnp.float32),
        (((1,), (0,)), ((), ())),
        precision=lax.Precision.HIGHEST,
        preferred_element_type=jnp.float32,
    )
    b1, b2, b3, h11, h21, h31, h22, h32, h33 = [
        jnp.broadcast_to(spread_ref[pl.ds(k, 1), :], (GROUP, LANES)) for k in range(9)
    ]
    l21 = h21 / h11
    l31 = h31 / h11
    d2 = h22 - l21 * h21
    e32 = h32 - l31 * h21
    l32 = e32 / d2
    d3 = h33 - l31 * h31 - l32 * e32
    y2 = b2 - l21 * b1
    y3 = b3 - l31 * b1 - l32 * y2
    c3 = y3 / d3
    c2 = y2 / d2 - l32 * c3
    c1 = b1 / h11 - l21 * c2 - l31 * c3
    return c1, c2, c3


def widen(value, width):
    return jnp.concatenate([value] * (width // LANES), axis=1)


def spread(natural_ref, l, i, deep, value):
    for b in range(value.shape[1] // LANES):
        natural_ref[l, b, pl.ds(i, GROUP, stride=deep), :] = value[:, b * LANES : (b + 1) * LANES]


def settle(natural_ref, out_ref):
    for b in range(natural_ref.shape[1]):
        out_ref[:, :, pl.ds(b * LANES, LANES)] = natural_ref[:, b, : out_ref.shape[1], :]


def first_kernel(
    deep, rows, width, outer,
    field_ref, edge_ref, above_ref, below_ref, ends_ref, middle_ref,
    basis_ref, drop_ref, cap_ref, later_ref, out_ref,
    whole_ref, grid_ref, cross_ref, start_ref, scaled_ref, second_ref, image_ref, inject_ref, sums_ref,
):
    wide = width + LANES
    blocks = wide // LANES
    inner = pl.ds(0, rows)
    for f in range(7):
        whole_ref[f, blocks - 1, inner, :] = edge_ref[f]
        for b in range(blocks - 1):
            if f < 5:
                whole_ref[f, b, inner, :] = field_ref[f, b]
            else:
                end, middle = ends_ref.at[f - 5, b], middle_ref.at[f - 5, b]
                whole_ref[f, b, pl.ds(0, outer), :] = end[pl.ds(0, outer), :]
                whole_ref[f, b, pl.ds(outer, rows - 2 * outer), :] = middle[...]
                whole_ref[f, b, pl.ds(rows - outer, outer), :] = end[pl.ds(outer, outer), :]
        for ref, place in ((below_ref, pl.ds(rows, HALO)), (above_ref, pl.ds(rows + HALO, HALO))):
            for b in range(blocks - 1):
                whole_ref[f, b, place, :] = ref[f * (blocks - 1) + b]
            whole_ref[f, blocks - 1, place, :] = ref[7 * (blocks - 1) + f]

    def slab(f, i):
        pick = pl.ds(i, GROUP, stride=deep)
        return jnp.concatenate([whole_ref[f, b, pick, :] for b in range(blocks)], axis=1)

    for l in range(2):
        for i in range(deep):
            cap_ref[l, i] = slab(l, i)
            drop_ref[l, i] = slab(2 + l, i)
    weigh(cap_ref, deep, grid_ref, cross_ref)
    for i in range(deep):
        tap = slab(4, i)
        for k in range(STEPS):
            charge = slab(5 + k, i)
            for a in range(3):
                sent = [jnp.where(tap == float(3 * a + b), charge, 0.0) for b in range(3)]
                value = pltpu.roll(sent[0], wide - 1, axis=1) + sent[1] + pltpu.roll(sent[2], 1, axis=1)
                inject_ref[k, a, i] = value

    def current(k, i):
        if i == deep - 1:
            upward = pltpu.roll(inject_ref[k, 0, 0], GROUP - 1, axis=0)
        else:
            upward = inject_ref[k, 0, i + 1]
        if i == 0:
            downward = pltpu.roll(inject_ref[k, 2, deep - 1], 1, axis=0)
        else:
            downward = inject_ref[k, 2, i - 1]
        return upward + inject_ref[k, 1, i] + downward

    for i in range(deep):
        later_ref[i] = current(1, i)
    residual(deep, drop_ref, lambda i: current(0, i), cross_ref, width, start_ref, scaled_ref)
    krylov(deep, width, cap_ref, grid_ref, cross_ref, scaled_ref, second_ref, basis_ref, image_ref)
    moments(deep, rows, width, start_ref, basis_ref, image_ref, sums_ref, out_ref)


def first_step(field, edge, above, below, ends, middle, count):
    rows = field.shape[2]
    width = field.shape[1] * LANES
    wide = width + LANES
    deep = (rows + 2 * HALO) // GROUP
    full = (2, deep, GROUP, wide)
    shapes = [(3, *full), full, full, full[1:], (count, LANES)]
    return pl.pallas_call(
        functools.partial(first_kernel, deep, rows, width, ends.shape[2] // 2),
        out_shape=[jax.ShapeDtypeStruct(s, jnp.float32) for s in shapes],
        in_specs=[vmem()] * 6,
        out_specs=[vmem()] * len(shapes),
        scratch_shapes=[
            pltpu.VMEM((7, wide // LANES, deep * GROUP, LANES), jnp.float32),
            pltpu.VMEM(full, jnp.float32),
            pltpu.VMEM(full, jnp.float32),
            pltpu.VMEM((2, deep, GROUP, width), jnp.float32),
            pltpu.VMEM(full, jnp.float32),
            pltpu.VMEM(full, jnp.float32),
            pltpu.VMEM((3, 2, deep, GROUP, width), jnp.float32),
            pltpu.VMEM((STEPS, 3, *full[1:]), jnp.float32),
            pltpu.VMEM((LANES, LANES), jnp.float32),
        ],
        compiler_params=params(20),
        name="first_step",
    )(field, edge, above, below, ends, middle)


def second_kernel(
    deep, rows, width,
    own_ref, other_ref, basis_ref, drop_ref, cap_ref, later_ref,
    first_ref, next_ref, held_ref, out_ref,
    now_ref, grid_ref, cross_ref, start_ref, scaled_ref, second_ref, image_ref, natural_ref, sums_ref,
):
    wide = width + LANES
    weigh(cap_ref, deep, grid_ref, cross_ref)
    weights = [widen(c, wide) for c in weights_of(own_ref, other_ref, sums_ref)]
    for l in range(2):
        for i in range(deep):
            value = drop_ref[l, i]
            for n in range(3):
                value = value + weights[n] * basis_ref[n, l, i]
            now_ref[l, i] = value
            held_ref[l, i] = value[:, :width]
            spread(natural_ref, l, i, deep, value[:, :width])
    settle(natural_ref, first_ref)
    residual(deep, now_ref, lambda i: later_ref[i], cross_ref, width, start_ref, scaled_ref)
    krylov(deep, width, cap_ref, grid_ref, cross_ref, scaled_ref, second_ref, next_ref, image_ref)
    moments(deep, rows, width, start_ref, next_ref, image_ref, sums_ref, out_ref)


def second_step(gathered, basis, drop, cap, later, rows):
    deep = cap.shape[1]
    wide = cap.shape[-1]
    width = wide - LANES
    full = (2, deep, GROUP, wide)
    shapes = [(2, rows, width), (3, *full), (2, deep, GROUP, width), gathered[0].shape]
    return pl.pallas_call(
        functools.partial(second_kernel, deep, rows, width),
        out_shape=[jax.ShapeDtypeStruct(s, jnp.float32) for s in shapes],
        in_specs=[vmem()] * 6,
        out_specs=[vmem()] * len(shapes),
        scratch_shapes=[
            pltpu.VMEM(full, jnp.float32),
            pltpu.VMEM(full, jnp.float32),
            pltpu.VMEM(full, jnp.float32),
            pltpu.VMEM((2, deep, GROUP, width), jnp.float32),
            pltpu.VMEM(full, jnp.float32),
            pltpu.VMEM(full, jnp.float32),
            pltpu.VMEM((3, 2, deep, GROUP, width), jnp.float32),
            pltpu.VMEM((2, width // LANES, deep * GROUP, LANES), jnp.float32),
            pltpu.VMEM((LANES, LANES), jnp.float32),
        ],
        compiler_params=params(20),
        name="second_step",
    )(*gathered, basis, drop, cap, later)


def last_kernel(deep, rows, width, own_ref, other_ref, basis_ref, held_ref, out_ref, natural_ref, sums_ref):
    weights = [widen(c, width) for c in weights_of(own_ref, other_ref, sums_ref)]
    for l in range(2):
        for i in range(deep):
            value = held_ref[l, i]
            for n in range(3):
                value = value + weights[n] * basis_ref[n, l, i, :, pl.ds(0, width)]
            spread(natural_ref, l, i, deep, value)
    settle(natural_ref, out_ref)


def last_step(gathered, basis, held, rows):
    deep = held.shape[1]
    width = held.shape[-1]
    return pl.pallas_call(
        functools.partial(last_kernel, deep, rows, width),
        out_shape=jax.ShapeDtypeStruct((2, rows, width), jnp.float32),
        in_specs=[vmem()] * 4,
        out_specs=vmem(),
        scratch_shapes=[
            pltpu.VMEM((2, width // LANES, deep * GROUP, LANES), jnp.float32),
            pltpu.VMEM((LANES, LANES), jnp.float32),
        ],
        compiler_params=params(12),
        name="last_step",
    )(*gathered, basis, held)


def shift(block, axis, up):
    count = lax.axis_size(axis)
    pairs = [(i, i + 1) for i in range(count - 1)]
    return lax.ppermute(block, axis, pairs if up else [(b, a) for a, b in pairs])


def from_all(block):
    outer, inner = lax.axis_size("gx"), lax.axis_size("gy")
    groups = [
        [x * inner + y for x in range(parity, outer, 2) for y in range(inner)] for parity in range(2)
    ]
    own = lax.all_to_all(block, BOTH, 0, 0, tiled=True, axis_index_groups=groups)
    own = own.reshape(-1, LANES)
    return own, lax.ppermute(own, "gx", [(i, i ^ 1) for i in range(outer)])


def shards(tables, table_index, toggle, tap_code, capacitance, prior_drop):
    rows, cols = table_index.shape
    inner = lax.axis_size("gy")
    count = lax.axis_size("gx") * inner // 2
    many = tables.shape[0], inner
    outer = HALO
    table = from_all(address(tables, count))
    table_index = table_index ^ ((lax.axis_index("gx") & 1) * (inner * tables.shape[0]))

    def columns(cut):
        codes = jnp.stack([a[:, cut] for a in (tap_code, table_index, toggle)]).astype(jnp.float32)
        return jnp.concatenate([capacitance[:, :, cut], prior_drop[:, :, cut], codes])

    left = shift(columns(slice(-LANES, None)), "gy", True)
    right = shift(columns(slice(0, LANES)), "gy", False)
    field = jnp.concatenate([capacitance, prior_drop, tap_code.astype(jnp.float32)[None]])
    field = field.reshape(-1, rows, cols // LANES, LANES).transpose(0, 2, 1, 3)

    def ends_of(array):
        return jnp.concatenate([array[:outer], array[-outer:]])

    ends, pieces = lookup(ends_of(table_index), ends_of(toggle), table, many)
    edge = edge_lookup(left, right, pieces, many)

    def late(far):
        cut = slice(-HALO, None) if far else slice(0, HALO)
        charge, lower = [a[:, :, cut].reshape(-1, HALO, LANES) for a in (ends, field)]
        return jnp.concatenate([lower, charge, edge[:, cut]])

    above = shift(late(True), "gx", True)
    below = shift(late(False), "gx", False)
    pieces, edge = lax.optimization_barrier((pieces, edge))
    middle = lookup(table_index[outer:-outer], toggle[outer:-outer], (pieces,), many)
    basis, drop, cap, later, part = first_step(field, edge, above, below, ends, middle, count)
    first, basis, held, part = second_step(from_all(part), basis, drop, cap, later, rows)
    return first, last_step(from_all(part), basis, held, rows)


def solution(mesh):
    in_specs = (
        P(BOTH, None),
        P("gx", "gy"),
        P("gx", "gy"),
        P("gx", "gy"),
        P(None, "gx", "gy"),
        P(None, "gx", "gy"),
    )
    out_specs = (P(None, "gx", "gy"), P(None, "gx", "gy"))
    return jax.shard_map(shards, mesh=mesh, in_specs=in_specs, out_specs=out_specs, check_vma=False)
```

```python
import functools
import math

import jax
import jax.numpy as jnp
from jax import lax
from jax.experimental import pallas as pl
from jax.experimental.pallas import tpu as pltpu
from jax.sharding import PartitionSpec as P

SUBSTEPS = 32
STEPS = 2
BOTH = ("gx", "gy")
LANES = 128
HALO = 20
GROUP = 8
LO = 4
CONDUCT = (1.0, 4.0)


def chebyshev_taus():
    theta = 1.05
    delta = 0.95
    return [1.0 / (theta + delta * math.cos((2 * i - 1) * math.pi / 6.0)) for i in (1, 2, 3)]


TAU = chebyshev_taus()
ALPHA = TAU[1] + (1.0 - TAU[1]) * TAU[0]
BETA = TAU[0] * TAU[1]
KEEP = (1.0 - TAU[2]) * BETA / TAU[2]
SHIFT = 0.75
RADIUS = 0.7
BACK = SHIFT / TAU[2]
FORMER = 0.5 * (RADIUS / TAU[2]) ** 2


def params(mib):
    return pltpu.CompilerParams(vmem_limit_bytes=mib * 2**20)


def vmem():
    return pl.BlockSpec(memory_space=pltpu.VMEM)


def address_kernel(table_ref, out_ref):
    table = table_ref[...]
    many = table.shape[0] // LO
    block = jnp.concatenate([table[a * many : (a + 1) * many] for a in range(LO)], axis=1)
    out_ref[...] = jnp.broadcast_to(block[None], out_ref.shape)


def address(table, count):
    many = table.shape[0] // LO
    return pl.pallas_call(
        address_kernel,
        out_shape=jax.ShapeDtypeStruct((count, many, LANES), jnp.float32),
        in_specs=[vmem()],
        out_specs=vmem(),
        compiler_params=params(8),
        name="address",
    )(table)


def arrange_kernel(
    flip, outer,
    cap_ref, drop_ref, tap_ref, index_ref, toggle_ref,
    left_ref, right_ref, field_ref, ends_ref, middle_ref,
):
    rows, cols = tap_ref.shape
    blocks = cols // LANES
    turn = (lax.axis_index("gx") & 1) * flip
    index = index_ref[...] ^ turn
    toggle = toggle_ref[...]
    for n, cells in enumerate((index, toggle)):
        ends_ref[n, pl.ds(0, outer), :] = cells[:outer]
        ends_ref[n, pl.ds(outer, outer), :] = cells[rows - outer :]
        middle_ref[n] = cells[outer : rows - outer]
    tap = tap_ref[...].astype(jnp.float32)
    fields = [cap_ref[0], cap_ref[1], drop_ref[0], drop_ref[1], tap]
    for f, field in enumerate(fields):
        for b in range(blocks):
            field_ref[f, b] = field[:, b * LANES : (b + 1) * LANES]
    fields += [index.astype(jnp.float32), toggle.astype(jnp.float32)]
    for f, field in enumerate(fields):
        left_ref[f] = field[:, cols - LANES :]
        right_ref[f] = field[:, :LANES]


def arrange(cap, drop, tap, index, toggle, flip, outer):
    rows, cols = tap.shape
    edge = jax.ShapeDtypeStruct((7, rows, LANES), jnp.float32)
    return pl.pallas_call(
        functools.partial(arrange_kernel, flip, outer),
        out_shape=[
            edge,
            edge,
            jax.ShapeDtypeStruct((5, cols // LANES, rows, LANES), jnp.float32),
            jax.ShapeDtypeStruct((2, 2 * outer, cols), jnp.int32),
            jax.ShapeDtypeStruct((2, rows - 2 * outer, cols), jnp.int32),
        ],
        in_specs=[vmem()] * 5,
        out_specs=[vmem()] * 5,
        compiler_params=params(12),
        name="arrange",
    )(cap, drop, tap, index, toggle)


MANY = 8
CHUNK = 256


def split_kernel(table_refs, pieces_ref):
    for b, ref in enumerate(table_refs):
        across = ref[...].T
        high = across.astype(jnp.bfloat16)
        low = (across - high.astype(jnp.float32)).astype(jnp.bfloat16)
        for p, piece in enumerate((high, low)):
            pieces_ref[pl.ds((2 * p + b) * LANES, LANES), :] = piece


def charges(many, index, toggle, pieces_ref):
    many, inner = many
    cols = index.shape[1]
    groups = pieces_ref.shape[1]
    quarter = many // LO
    held = index & (many - 1)
    device = index // many
    half = (device // inner) & 1
    place = device // (2 * inner) * inner + (device & (inner - 1))
    row = place * quarter + (held & (quarter - 1))
    which = held // quarter + LO * half
    hot = []
    for k in range(groups // CHUNK):
        local = (row - CHUNK * k).astype(jnp.float32).astype(jnp.bfloat16)
        count = lax.broadcasted_iota(jnp.int32, (CHUNK, cols), 0)
        count = count.astype(jnp.float32).astype(jnp.bfloat16)
        same = jnp.broadcast_to(local, (CHUNK, cols)) == count
        hot.append(jnp.where(same, jnp.bfloat16(1), jnp.bfloat16(0)))
    got = jnp.dot(pieces_ref[...], jnp.concatenate(hot, 0), preferred_element_type=jnp.float32)
    half = got.shape[0] // 2
    value = (got[:half] + got[half:]).reshape(MANY, SUBSTEPS, cols)
    chosen = value[0]
    for a in range(1, MANY):
        chosen = jnp.where(which == a, value[a], chosen)
    moment = lax.broadcasted_iota(jnp.int32, (SUBSTEPS, cols), 0) + toggle
    share = SUBSTEPS // STEPS
    means = []
    for k in range(STEPS):
        inside = (moment >= k * share) & (moment < (k + 1) * share)
        total = jnp.sum(jnp.where(inside, chosen, 0.0), axis=0, keepdims=True)
        means.append(total * (1.0 / share))
    return means


def lookup_rows(many, cells_ref, pieces_ref, out_ref):
    _, rows, cols = cells_ref.shape
    unroll = rows if rows <= 24 else math.gcd(rows, 20)

    def body(i, carry):
        for u in range(unroll):
            row = pl.ds(i * unroll + u, 1)
            means = charges(many, cells_ref[0, row, :], cells_ref[1, row, :], pieces_ref)
            for k, mean in enumerate(means):
                for b in range(cols // LANES):
                    out_ref[k, b, row, :] = mean[:, b * LANES : (b + 1) * LANES]
        return carry

    lax.fori_loop(0, rows // unroll, body, 0)


def first_lookup_kernel(many, cells_ref, own_ref, other_ref, out_ref, pieces_ref):
    split_kernel((own_ref, other_ref), pieces_ref)
    lookup_rows(many, cells_ref, pieces_ref, out_ref)


def lookup_cost(cells, pieces):
    flops = 2 * cells * pieces.shape[0] * pieces.shape[1]
    return pl.CostEstimate(flops=flops, bytes_accessed=0, transcendentals=0)


def lookup(cells, table, many):
    _, rows, cols = cells.shape
    charge = jax.ShapeDtypeStruct((STEPS, cols // LANES, rows, LANES), jnp.float32)
    fresh = len(table) == 2
    pieces = table[0]
    if fresh:
        pieces = jax.ShapeDtypeStruct((2 * MANY * SUBSTEPS, pieces.shape[0]), jnp.bfloat16)
    return pl.pallas_call(
        functools.partial(first_lookup_kernel if fresh else lookup_rows, many),
        out_shape=[charge, pieces] if fresh else charge,
        in_specs=[vmem()] * (1 + len(table)),
        out_specs=[vmem()] * 2 if fresh else vmem(),
        compiler_params=params(20),
        cost_estimate=lookup_cost(rows * cols, pieces),
        name="lookup",
    )(cells, *table)


def edge_lookup_kernel(many, left_ref, right_ref, pieces_ref, out_ref, cells_ref, got_ref):
    rows = left_ref.shape[1]
    lane = lax.broadcasted_iota(jnp.int32, (rows, LANES), 1)

    def merge(right, left):
        return jnp.where(lane < HALO, right, jnp.where(lane >= LANES - HALO, left, 0.0))

    for f in range(5):
        out_ref[f] = merge(right_ref[f], left_ref[f])
    pair = lax.broadcasted_iota(jnp.int32, (HALO, LANES), 1)
    for n in range(2):
        near = pltpu.roll(merge(right_ref[5 + n], left_ref[5 + n]), HALO, axis=1)
        turned = jnp.concatenate([near, jnp.zeros_like(near)], axis=0).T
        high = pltpu.roll(turned[HALO : 2 * HALO], LANES - rows, axis=1)
        cells_ref[n] = jnp.where(pair < rows, turned[:HALO], high).astype(jnp.int32)
    got_ref[...] = jnp.zeros_like(got_ref)
    step = 4
    for u in range(HALO // step):
        index, toggle = [
            jnp.concatenate([cells_ref[n, pl.ds(step * u + r, 1), :] for r in range(step)], axis=1)
            for n in range(2)
        ]
        for k, mean in enumerate(charges(many, index, toggle, pieces_ref)):
            for r in range(step):
                got_ref[k, pl.ds(step * u + r, 1), :] = mean[:, r * LANES : (r + 1) * LANES]
    inside = out_ref[0] > 0.0
    for k in range(STEPS):
        back = got_ref[k].T
        left = pltpu.roll(back[:rows], LANES - HALO, axis=1)
        out_ref[5 + k] = jnp.where(inside, merge(back[rows:], left), 0.0)


def edge_lookup(left, right, pieces, many):
    rows = left.shape[1]
    assert 2 * rows == LANES
    return pl.pallas_call(
        functools.partial(edge_lookup_kernel, many),
        out_shape=jax.ShapeDtypeStruct(left.shape, jnp.float32),
        in_specs=[vmem()] * 3,
        out_specs=vmem(),
        scratch_shapes=[
            pltpu.VMEM((2, HALO, LANES), jnp.int32),
            pltpu.VMEM((STEPS, LANES, LANES), jnp.float32),
        ],
        compiler_params=params(20),
        cost_estimate=lookup_cost(2 * HALO * rows, pieces),
        name="edge_lookup",
    )(left, right, pieces)


def sweep(deep, fetch, use):
    def load(i):
        if i < 0:
            return [pltpu.roll(fetch(l, deep - 1), 1, axis=0) for l in range(2)]
        if i >= deep:
            return [pltpu.roll(fetch(l, 0), GROUP - 1, axis=0) for l in range(2)]
        return [fetch(l, i) for l in range(2)]

    held = {}
    for i in range(deep):
        held = {k: v for k, v in held.items() if k in (i - 1, i, i + 1)}
        for k in (i - 1, i, i + 1):
            if k not in held:
                held[k] = load(k)
        for l in range(2):
            center = held[i][l]
            width = center.shape[-1]
            beside = pltpu.roll(center, 1, axis=1) + pltpu.roll(center, width - 1, axis=1)
            around = (held[i - 1][l] + held[i + 1][l]) + beside
            use(l, i, center, around, held[i][1 - l])


def weigh(cap_ref, deep, grid_ref, cross_ref):
    for l in range(2):
        for i in range(deep):
            cap = cap_ref[l, i]
            inverse = jnp.where(cap > 0.0, 1.0 / (cap + (4.0 * CONDUCT[l] + 2.0)), 0.0)
            grid_ref[l, i] = CONDUCT[l] * inverse
            cross_ref[l, i] = 2.0 * inverse


def residual(deep, drop_ref, current, cross_ref, width, start_ref, scaled_ref):
    def use(l, i, center, around, other):
        value = CONDUCT[l] * around + 2.0 * other - (4.0 * CONDUCT[l] + 2.0) * center
        if l == 0:
            value = value + current(i)
        start_ref[l, i] = value[:, :width]
        scaled_ref[l, i] = value * (cross_ref[l, i] * 0.5)

    sweep(deep, lambda l, i: drop_ref[l, i], use)


def krylov(deep, width, cap_ref, grid_ref, cross_ref, scaled_ref, second_ref, basis_ref, image_ref):
    def coupled(l, i, around, other):
        return grid_ref[l, i] * around + cross_ref[l, i] * other

    def use_second(l, i, center, around, other):
        second_ref[l, i] = (ALPHA / BETA) * center + coupled(l, i, around, other)

    for n in range(3):

        def use_basis(l, i, center, around, other, n=n):
            value = KEEP * center + (
                scaled_ref[l, i] + BETA * coupled(l, i, around, other)
            )
            if n == 1:
                value = value - BACK * basis_ref[0, l, i]
            if n == 2:
                value = value - BACK * basis_ref[1, l, i] - FORMER * basis_ref[0, l, i]
            basis_ref[n, l, i] = value

        def use_image(l, i, center, around, other, n=n):
            value = center - coupled(l, i, around, other)
            if n < 2:
                scaled_ref[l, i] = value
            diagonal = cap_ref[l, i][:, :width] + (4.0 * CONDUCT[l] + 2.0)
            image_ref[n, l, i] = value[:, :width] * diagonal

        sweep(deep, lambda l, i: scaled_ref[l, i], use_second)
        sweep(deep, lambda l, i: second_ref[l, i], use_basis)
        sweep(deep, lambda l, i, n=n: basis_ref[n, l, i], use_image)


PAIRS = ((0, 0), (1, 0), (2, 0), (1, 1), (2, 1), (2, 2))


def moments(deep, rows, width, start_ref, basis_ref, image_ref, sums_ref, out_ref):
    sub = lax.broadcasted_iota(jnp.int32, (GROUP, LANES), 0)

    def body(i, totals):
        inside = sub * deep + i < rows
        part = [None] * 9
        for l in range(2):
            for b in range(width // LANES):
                lanes = pl.ds(b * LANES, LANES)
                start = start_ref[l, i, :, lanes]
                basis = [basis_ref[n, l, i, :, lanes] for n in range(3)]
                image = [image_ref[n, l, i, :, lanes] for n in range(3)]
                terms = [start * v for v in basis] + [basis[p] * image[q] for p, q in PAIRS]
                part = [t if p is None else p + t for p, t in zip(part, terms)]
        return [t + jnp.where(inside, p, 0.0) for t, p in zip(totals, part)]

    totals = lax.fori_loop(0, deep, body, [jnp.zeros((GROUP, LANES), jnp.float32)] * 9)
    sums_ref[...] = jnp.zeros_like(sums_ref)
    for k, total in enumerate(totals):
        sums_ref[pl.ds(k, 1), :] = jnp.sum(total, axis=0, keepdims=True)
    row = lax.dot_general(
        jnp.ones((GROUP, LANES), jnp.float32),
        sums_ref[...],
        (((1,), (1,)), ((), ())),
        precision=lax.Precision.HIGHEST,
        preferred_element_type=jnp.float32,
    )
    out_ref[...] = jnp.broadcast_to(row[:1], out_ref.shape)


def weights_of(gathered_ref, spread_ref):
    total = jnp.sum(gathered_ref[...], axis=0, keepdims=True)
    row = lax.broadcasted_iota(jnp.int32, (LANES, LANES), 0)
    lane = lax.broadcasted_iota(jnp.int32, (LANES, LANES), 1)
    spread_ref[...] = lax.dot_general(
        jnp.where(row == lane, jnp.broadcast_to(total, (LANES, LANES)), 0.0),
        jnp.ones((LANES, LANES), jnp.float32),
        (((1,), (0,)), ((), ())),
        precision=lax.Precision.HIGHEST,
        preferred_element_type=jnp.float32,
    )
    b1, b2, b3, h11, h21, h31, h22, h32, h33 = [
        jnp.broadcast_to(spread_ref[pl.ds(k, 1), :], (GROUP, LANES)) for k in range(9)
    ]
    l21 = h21 / h11
    l31 = h31 / h11
    d2 = h22 - l21 * h21
    e32 = h32 - l31 * h21
    l32 = e32 / d2
    d3 = h33 - l31 * h31 - l32 * e32
    y2 = b2 - l21 * b1
    y3 = b3 - l31 * b1 - l32 * y2
    c3 = y3 / d3
    c2 = y2 / d2 - l32 * c3
    c1 = b1 / h11 - l21 * c2 - l31 * c3
    return c1, c2, c3


def widen(value, width):
    return jnp.concatenate([value] * (width // LANES), axis=1)


def spread(natural_ref, l, i, deep, value):
    for b in range(value.shape[1] // LANES):
        natural_ref[l, b, pl.ds(i, GROUP, stride=deep), :] = value[:, b * LANES : (b + 1) * LANES]


def settle(natural_ref, out_ref):
    for b in range(natural_ref.shape[1]):
        out_ref[:, :, pl.ds(b * LANES, LANES)] = natural_ref[:, b, : out_ref.shape[1], :]


def first_kernel(
    deep, rows, width, outer,
    field_ref, edge_ref, above_ref, below_ref, ends_ref, middle_ref,
    basis_ref, drop_ref, cap_ref, later_ref, out_ref,
    whole_ref, grid_ref, cross_ref, start_ref, scaled_ref, second_ref, image_ref, inject_ref, sums_ref,
):
    wide = width + LANES
    blocks = wide // LANES
    inner = pl.ds(0, rows)
    for f in range(7):
        whole_ref[f, blocks - 1, inner, :] = edge_ref[f]
        for b in range(blocks - 1):
            if f < 5:
                whole_ref[f, b, inner, :] = field_ref[f, b]
            else:
                end, middle = ends_ref.at[f - 5, b], middle_ref.at[f - 5, b]
                whole_ref[f, b, pl.ds(0, outer), :] = end[pl.ds(0, outer), :]
                whole_ref[f, b, pl.ds(outer, rows - 2 * outer), :] = middle[...]
                whole_ref[f, b, pl.ds(rows - outer, outer), :] = end[pl.ds(outer, outer), :]
        for ref, place in ((below_ref, pl.ds(rows, HALO)), (above_ref, pl.ds(rows + HALO, HALO))):
            for b in range(blocks - 1):
                whole_ref[f, b, place, :] = ref[f * (blocks - 1) + b]
            whole_ref[f, blocks - 1, place, :] = ref[7 * (blocks - 1) + f]

    def slab(f, i):
        pick = pl.ds(i, GROUP, stride=deep)
        return jnp.concatenate([whole_ref[f, b, pick, :] for b in range(blocks)], axis=1)

    for l in range(2):
        for i in range(deep):
            cap_ref[l, i] = slab(l, i)
            drop_ref[l, i] = slab(2 + l, i)
    weigh(cap_ref, deep, grid_ref, cross_ref)
    for i in range(deep):
        tap = slab(4, i)
        for k in range(STEPS):
            charge = slab(5 + k, i)
            for a in range(3):
                sent = [jnp.where(tap == float(3 * a + b), charge, 0.0) for b in range(3)]
                value = pltpu.roll(sent[0], wide - 1, axis=1) + sent[1] + pltpu.roll(sent[2], 1, axis=1)
                inject_ref[k, a, i] = value

    def current(k, i):
        if i == deep - 1:
            upward = pltpu.roll(inject_ref[k, 0, 0], GROUP - 1, axis=0)
        else:
            upward = inject_ref[k, 0, i + 1]
        if i == 0:
            downward = pltpu.roll(inject_ref[k, 2, deep - 1], 1, axis=0)
        else:
            downward = inject_ref[k, 2, i - 1]
        return upward + inject_ref[k, 1, i] + downward

    for i in range(deep):
        later_ref[i] = current(1, i)
    residual(deep, drop_ref, lambda i: current(0, i), cross_ref, width, start_ref, scaled_ref)
    krylov(deep, width, cap_ref, grid_ref, cross_ref, scaled_ref, second_ref, basis_ref, image_ref)
    moments(deep, rows, width, start_ref, basis_ref, image_ref, sums_ref, out_ref)


def first_step(field, edge, above, below, ends, middle, count):
    rows = field.shape[2]
    width = field.shape[1] * LANES
    wide = width + LANES
    deep = (rows + 2 * HALO) // GROUP
    full = (2, deep, GROUP, wide)
    shapes = [(3, *full), full, full, full[1:], (count, LANES)]
    return pl.pallas_call(
        functools.partial(first_kernel, deep, rows, width, ends.shape[2] // 2),
        out_shape=[jax.ShapeDtypeStruct(s, jnp.float32) for s in shapes],
        in_specs=[vmem()] * 6,
        out_specs=[vmem()] * len(shapes),
        scratch_shapes=[
            pltpu.VMEM((7, wide // LANES, deep * GROUP, LANES), jnp.float32),
            pltpu.VMEM(full, jnp.float32),
            pltpu.VMEM(full, jnp.float32),
            pltpu.VMEM((2, deep, GROUP, width), jnp.float32),
            pltpu.VMEM(full, jnp.float32),
            pltpu.VMEM(full, jnp.float32),
            pltpu.VMEM((3, 2, deep, GROUP, width), jnp.float32),
            pltpu.VMEM((STEPS, 3, *full[1:]), jnp.float32),
            pltpu.VMEM((LANES, LANES), jnp.float32),
        ],
        compiler_params=params(20),
        name="first_step",
    )(field, edge, above, below, ends, middle)


def second_kernel(
    deep, rows, width,
    gathered_ref, basis_ref, drop_ref, cap_ref, later_ref,
    first_ref, next_ref, held_ref, out_ref,
    now_ref, grid_ref, cross_ref, start_ref, scaled_ref, second_ref, image_ref, natural_ref, sums_ref,
):
    wide = width + LANES
    weigh(cap_ref, deep, grid_ref, cross_ref)
    weights = [widen(c, wide) for c in weights_of(gathered_ref, sums_ref)]
    for l in range(2):
        for i in range(deep):
            value = drop_ref[l, i]
            for n in range(3):
                value = value + weights[n] * basis_ref[n, l, i]
            now_ref[l, i] = value
            held_ref[l, i] = value[:, :width]
            spread(natural_ref, l, i, deep, value[:, :width])
    settle(natural_ref, first_ref)
    residual(deep, now_ref, lambda i: later_ref[i], cross_ref, width, start_ref, scaled_ref)
    krylov(deep, width, cap_ref, grid_ref, cross_ref, scaled_ref, second_ref, next_ref, image_ref)
    moments(deep, rows, width, start_ref, next_ref, image_ref, sums_ref, out_ref)


def second_step(gathered, basis, drop, cap, later, rows):
    deep = cap.shape[1]
    wide = cap.shape[-1]
    width = wide - LANES
    full = (2, deep, GROUP, wide)
    shapes = [(2, rows, width), (3, *full), (2, deep, GROUP, width), gathered.shape]
    return pl.pallas_call(
        functools.partial(second_kernel, deep, rows, width),
        out_shape=[jax.ShapeDtypeStruct(s, jnp.float32) for s in shapes],
        in_specs=[vmem()] * 5,
        out_specs=[vmem()] * len(shapes),
        scratch_shapes=[
            pltpu.VMEM(full, jnp.float32),
            pltpu.VMEM(full, jnp.float32),
            pltpu.VMEM(full, jnp.float32),
            pltpu.VMEM((2, deep, GROUP, width), jnp.float32),
            pltpu.VMEM(full, jnp.float32),
            pltpu.VMEM(full, jnp.float32),
            pltpu.VMEM((3, 2, deep, GROUP, width), jnp.float32),
            pltpu.VMEM((2, width // LANES, deep * GROUP, LANES), jnp.float32),
            pltpu.VMEM((LANES, LANES), jnp.float32),
        ],
        compiler_params=params(20),
        name="second_step",
    )(gathered, basis, drop, cap, later)


def last_kernel(deep, rows, width, gathered_ref, basis_ref, held_ref, out_ref, natural_ref, sums_ref):
    weights = [widen(c, width) for c in weights_of(gathered_ref, sums_ref)]
    for l in range(2):
        for i in range(deep):
            value = held_ref[l, i]
            for n in range(3):
                value = value + weights[n] * basis_ref[n, l, i, :, pl.ds(0, width)]
            spread(natural_ref, l, i, deep, value)
    settle(natural_ref, out_ref)


def last_step(gathered, basis, held, rows):
    deep = held.shape[1]
    width = held.shape[-1]
    return pl.pallas_call(
        functools.partial(last_kernel, deep, rows, width),
        out_shape=jax.ShapeDtypeStruct((2, rows, width), jnp.float32),
        in_specs=[vmem()] * 3,
        out_specs=vmem(),
        scratch_shapes=[
            pltpu.VMEM((2, width // LANES, deep * GROUP, LANES), jnp.float32),
            pltpu.VMEM((LANES, LANES), jnp.float32),
        ],
        compiler_params=params(12),
        name="last_step",
    )(gathered, basis, held)


def shift(block, axis, up):
    count = lax.axis_size(axis)
    pairs = [(i, i + 1) for i in range(count - 1)]
    return lax.ppermute(block, axis, pairs if up else [(b, a) for a, b in pairs])


def exchange(block):
    return lax.all_to_all(block, BOTH, 0, 0, tiled=True)


def by_parity(block):
    outer, inner = lax.axis_size("gx"), lax.axis_size("gy")
    groups = [
        [x * inner + y for x in range(parity, outer, 2) for y in range(inner)] for parity in range(2)
    ]
    own = lax.all_to_all(block, BOTH, 0, 0, tiled=True, axis_index_groups=groups)
    own = own.reshape(-1, LANES)
    return own, lax.ppermute(own, "gx", [(i, i ^ 1) for i in range(outer)])


def shards(tables, table_index, toggle, tap_code, capacitance, prior_drop):
    rows = table_index.shape[0]
    inner = lax.axis_size("gy")
    count = lax.axis_size("gx") * inner
    many = tables.shape[0], inner
    outer = HALO
    table = by_parity(address(tables, count // 2))
    flip = inner * tables.shape[0]
    left, right, field, outside, inside = arrange(
        capacitance, prior_drop, tap_code, table_index, toggle, flip, outer
    )
    left = shift(left, "gy", True)
    right = shift(right, "gy", False)
    ends, pieces = lookup(outside, table, many)
    edge = edge_lookup(left, right, pieces, many)

    def late(far):
        cut = slice(-HALO, None) if far else slice(0, HALO)
        charge, lower = [a[:, :, cut].reshape(-1, HALO, LANES) for a in (ends, field)]
        return jnp.concatenate([lower, charge, edge[:, cut]])

    above = shift(late(True), "gx", True)
    below = shift(late(False), "gx", False)
    pieces, edge = lax.optimization_barrier((pieces, edge))
    middle = lookup(inside, (pieces,), many)
    basis, drop, cap, later, part = first_step(field, edge, above, below, ends, middle, count)
    first, basis, held, part = second_step(exchange(part), basis, drop, cap, later, rows)
    return first, last_step(exchange(part), basis, held, rows)


def solution(mesh):
    in_specs = (
        P(BOTH, None),
        P("gx", "gy"),
        P("gx", "gy"),
        P("gx", "gy"),
        P(None, "gx", "gy"),
        P(None, "gx", "gy"),
    )
    out_specs = (P(None, "gx", "gy"), P(None, "gx", "gy"))
    return jax.shard_map(shards, mesh=mesh, in_specs=in_specs, out_specs=out_specs, check_vma=False)
```

```python
import functools
import math

import jax
import jax.numpy as jnp
from jax import lax
from jax.experimental import pallas as pl
from jax.experimental.pallas import tpu as pltpu
from jax.sharding import PartitionSpec as P

SUBSTEPS = 32
STEPS = 2
BOTH = ("gx", "gy")
LANES = 128
HALO = 20
GROUP = 8
LO = 4
CONDUCT = (1.0, 4.0)


def chebyshev_taus():
    theta = 1.05
    delta = 0.95
    return [1.0 / (theta + delta * math.cos((2 * i - 1) * math.pi / 6.0)) for i in (1, 2, 3)]


TAU = chebyshev_taus()
ALPHA = TAU[1] + (1.0 - TAU[1]) * TAU[0]
BETA = TAU[0] * TAU[1]
KEEP = (1.0 - TAU[2]) * BETA / TAU[2]
SHIFT = 0.75
RADIUS = 0.7
BACK = SHIFT / TAU[2]
FORMER = 0.5 * (RADIUS / TAU[2]) ** 2


def params(mib):
    return pltpu.CompilerParams(vmem_limit_bytes=mib * 2**20)


def vmem():
    return pl.BlockSpec(memory_space=pltpu.VMEM)


def address_kernel(
    table_in, tap_in, index_in, toggle_in, out_ref, codes_ref, table_ref, cells_ref, arrived
):
    copies = [pltpu.make_async_copy(table_in, table_ref, arrived.at[3])]
    for n, source in enumerate((tap_in, index_in, toggle_in)):
        copies.append(pltpu.make_async_copy(source, cells_ref.at[n], arrived.at[n]))
    for copy in copies:
        copy.start()
    copies[0].wait()
    table = table_ref[...]
    many = table.shape[0] // LO
    block = jnp.concatenate([table[a * many : (a + 1) * many] for a in range(LO)], axis=1)
    out_ref[...] = jnp.broadcast_to(block[None], out_ref.shape)
    for n in range(3):
        copies[1 + n].wait()
        codes_ref[n] = cells_ref[n].astype(jnp.float32)


def address(table, tap, index, toggle, count):
    many = table.shape[0] // LO
    return pl.pallas_call(
        address_kernel,
        out_shape=[
            jax.ShapeDtypeStruct((count, many, LANES), jnp.float32),
            jax.ShapeDtypeStruct((3, *tap.shape), jnp.float32),
        ],
        in_specs=[pl.BlockSpec(memory_space=pl.ANY)] * 4,
        out_specs=[vmem()] * 2,
        scratch_shapes=[
            pltpu.VMEM(table.shape, jnp.float32),
            pltpu.VMEM((3, *tap.shape), jnp.int32),
            pltpu.SemaphoreType.DMA((4,)),
        ],
        compiler_params=params(62),
        name="address",
    )(table, tap, index, toggle)


MANY = 8
CHUNK = 256


def split_kernel(table_refs, pieces_ref):
    for b, ref in enumerate(table_refs):
        across = ref[...].T
        high = across.astype(jnp.bfloat16)
        low = (across - high.astype(jnp.float32)).astype(jnp.bfloat16)
        for p, piece in enumerate((high, low)):
            pieces_ref[pl.ds((2 * p + b) * LANES, LANES), :] = piece


def charges(many, index, toggle, pieces_ref):
    many, inner = many
    cols = index.shape[1]
    groups = pieces_ref.shape[1]
    quarter = many // LO
    held = index & (many - 1)
    device = index // many
    half = (device // inner + lax.axis_index("gx")) & 1
    place = device // (2 * inner) * inner + (device & (inner - 1))
    row = place * quarter + (held & (quarter - 1))
    which = held // quarter + LO * half
    hot = []
    for k in range(groups // CHUNK):
        local = (row - CHUNK * k).astype(jnp.float32).astype(jnp.bfloat16)
        count = lax.broadcasted_iota(jnp.int32, (CHUNK, cols), 0)
        count = count.astype(jnp.float32).astype(jnp.bfloat16)
        same = jnp.broadcast_to(local, (CHUNK, cols)) == count
        hot.append(jnp.where(same, jnp.bfloat16(1), jnp.bfloat16(0)))
    got = jnp.dot(pieces_ref[...], jnp.concatenate(hot, 0), preferred_element_type=jnp.float32)
    half = got.shape[0] // 2
    value = (got[:half] + got[half:]).reshape(MANY, SUBSTEPS, cols)
    chosen = value[0]
    for a in range(1, MANY):
        chosen = jnp.where(which == a, value[a], chosen)
    moment = lax.broadcasted_iota(jnp.int32, (SUBSTEPS, cols), 0) + toggle
    share = SUBSTEPS // STEPS
    means = []
    for k in range(STEPS):
        inside = (moment >= k * share) & (moment < (k + 1) * share)
        total = jnp.sum(jnp.where(inside, chosen, 0.0), axis=0, keepdims=True)
        means.append(total * (1.0 / share))
    return means


def lookup_rows(many, index_ref, toggle_ref, pieces_ref, out_ref):
    rows, cols = index_ref.shape
    unroll = rows if rows <= 24 else math.gcd(rows, 20)

    def body(i, carry):
        for u in range(unroll):
            row = pl.ds(i * unroll + u, 1)
            means = charges(many, index_ref[row, :], toggle_ref[row, :], pieces_ref)
            for k, mean in enumerate(means):
                for b in range(cols // LANES):
                    out_ref[k, b, row, :] = mean[:, b * LANES : (b + 1) * LANES]
        return carry

    lax.fori_loop(0, rows // unroll, body, 0)


def first_lookup_kernel(many, index_ref, toggle_ref, own_ref, other_ref, out_ref, pieces_ref):
    split_kernel((own_ref, other_ref), pieces_ref)
    lookup_rows(many, index_ref, toggle_ref, pieces_ref, out_ref)


def lookup_cost(cells, pieces):
    flops = 2 * cells * pieces.shape[0] * pieces.shape[1]
    return pl.CostEstimate(flops=flops, bytes_accessed=0, transcendentals=0)


def lookup(index, toggle, table, many):
    rows, cols = index.shape
    charge = jax.ShapeDtypeStruct((STEPS, cols // LANES, rows, LANES), jnp.float32)
    fresh = len(table) == 2
    pieces = table[0]
    if fresh:
        pieces = jax.ShapeDtypeStruct((2 * MANY * SUBSTEPS, pieces.shape[0]), jnp.bfloat16)
    return pl.pallas_call(
        functools.partial(first_lookup_kernel if fresh else lookup_rows, many),
        out_shape=[charge, pieces] if fresh else charge,
        in_specs=[vmem()] * (2 + len(table)),
        out_specs=[vmem()] * 2 if fresh else vmem(),
        compiler_params=params(20),
        cost_estimate=lookup_cost(rows * cols, pieces),
        name="lookup",
    )(index, toggle, *table)


def edge_lookup_kernel(many, left_ref, right_ref, pieces_ref, out_ref, cells_ref, got_ref):
    rows = left_ref.shape[1]
    lane = lax.broadcasted_iota(jnp.int32, (rows, LANES), 1)

    def merge(right, left):
        return jnp.where(lane < HALO, right, jnp.where(lane >= LANES - HALO, left, 0.0))

    for f in range(5):
        out_ref[f] = merge(right_ref[f], left_ref[f])
    pair = lax.broadcasted_iota(jnp.int32, (HALO, LANES), 1)
    for n in range(2):
        near = pltpu.roll(merge(right_ref[5 + n], left_ref[5 + n]), HALO, axis=1)
        turned = jnp.concatenate([near, jnp.zeros_like(near)], axis=0).T
        high = pltpu.roll(turned[HALO : 2 * HALO], LANES - rows, axis=1)
        cells_ref[n] = jnp.where(pair < rows, turned[:HALO], high).astype(jnp.int32)
    got_ref[...] = jnp.zeros_like(got_ref)
    step = 4
    for u in range(HALO // step):
        index, toggle = [
            jnp.concatenate([cells_ref[n, pl.ds(step * u + r, 1), :] for r in range(step)], axis=1)
            for n in range(2)
        ]
        for k, mean in enumerate(charges(many, index, toggle, pieces_ref)):
            for r in range(step):
                got_ref[k, pl.ds(step * u + r, 1), :] = mean[:, r * LANES : (r + 1) * LANES]
    inside = out_ref[0] > 0.0
    for k in range(STEPS):
        back = got_ref[k].T
        left = pltpu.roll(back[:rows], LANES - HALO, axis=1)
        out_ref[5 + k] = jnp.where(inside, merge(back[rows:], left), 0.0)


def edge_lookup(left, right, pieces, many):
    rows = left.shape[1]
    assert 2 * rows == LANES
    return pl.pallas_call(
        functools.partial(edge_lookup_kernel, many),
        out_shape=jax.ShapeDtypeStruct(left.shape, jnp.float32),
        in_specs=[vmem()] * 3,
        out_specs=vmem(),
        scratch_shapes=[
            pltpu.VMEM((2, HALO, LANES), jnp.int32),
            pltpu.VMEM((STEPS, LANES, LANES), jnp.float32),
        ],
        compiler_params=params(20),
        cost_estimate=lookup_cost(2 * HALO * rows, pieces),
        name="edge_lookup",
    )(left, right, pieces)


def sweep(deep, fetch, use):
    def load(i):
        if i < 0:
            return [pltpu.roll(fetch(l, deep - 1), 1, axis=0) for l in range(2)]
        if i >= deep:
            return [pltpu.roll(fetch(l, 0), GROUP - 1, axis=0) for l in range(2)]
        return [fetch(l, i) for l in range(2)]

    held = {}
    for i in range(deep):
        held = {k: v for k, v in held.items() if k in (i - 1, i, i + 1)}
        for k in (i - 1, i, i + 1):
            if k not in held:
                held[k] = load(k)
        for l in range(2):
            center = held[i][l]
            width = center.shape[-1]
            beside = pltpu.roll(center, 1, axis=1) + pltpu.roll(center, width - 1, axis=1)
            around = (held[i - 1][l] + held[i + 1][l]) + beside
            use(l, i, center, around, held[i][1 - l])


def weigh(cap_ref, deep, grid_ref, cross_ref):
    for l in range(2):
        for i in range(deep):
            cap = cap_ref[l, i]
            inverse = jnp.where(cap > 0.0, 1.0 / (cap + (4.0 * CONDUCT[l] + 2.0)), 0.0)
            grid_ref[l, i] = CONDUCT[l] * inverse
            cross_ref[l, i] = 2.0 * inverse


def residual(deep, drop_ref, current, cross_ref, width, start_ref, scaled_ref):
    def use(l, i, center, around, other):
        value = CONDUCT[l] * around + 2.0 * other - (4.0 * CONDUCT[l] + 2.0) * center
        if l == 0:
            value = value + current(i)
        start_ref[l, i] = value[:, :width]
        scaled_ref[l, i] = value * (cross_ref[l, i] * 0.5)

    sweep(deep, lambda l, i: drop_ref[l, i], use)


def krylov(deep, width, cap_ref, grid_ref, cross_ref, scaled_ref, second_ref, basis_ref, image_ref):
    def coupled(l, i, around, other):
        return grid_ref[l, i] * around + cross_ref[l, i] * other

    def use_second(l, i, center, around, other):
        second_ref[l, i] = (ALPHA / BETA) * center + coupled(l, i, around, other)

    for n in range(3):

        def use_basis(l, i, center, around, other, n=n):
            value = KEEP * center + (
                scaled_ref[l, i] + BETA * coupled(l, i, around, other)
            )
            if n == 1:
                value = value - BACK * basis_ref[0, l, i]
            if n == 2:
                value = value - BACK * basis_ref[1, l, i] - FORMER * basis_ref[0, l, i]
            basis_ref[n, l, i] = value

        def use_image(l, i, center, around, other, n=n):
            value = center - coupled(l, i, around, other)
            if n < 2:
                scaled_ref[l, i] = value
            diagonal = cap_ref[l, i][:, :width] + (4.0 * CONDUCT[l] + 2.0)
            image_ref[n, l, i] = value[:, :width] * diagonal

        sweep(deep, lambda l, i: scaled_ref[l, i], use_second)
        sweep(deep, lambda l, i: second_ref[l, i], use_basis)
        sweep(deep, lambda l, i, n=n: basis_ref[n, l, i], use_image)


PAIRS = ((0, 0), (1, 0), (2, 0), (1, 1), (2, 1), (2, 2))


def moments(deep, rows, width, start_ref, basis_ref, image_ref, sums_ref, out_ref):
    sub = lax.broadcasted_iota(jnp.int32, (GROUP, LANES), 0)

    def body(i, totals):
        inside = sub * deep + i < rows
        part = [None] * 9
        for l in range(2):
            for b in range(width // LANES):
                lanes = pl.ds(b * LANES, LANES)
                start = start_ref[l, i, :, lanes]
                basis = [basis_ref[n, l, i, :, lanes] for n in range(3)]
                image = [image_ref[n, l, i, :, lanes] for n in range(3)]
                terms = [start * v for v in basis] + [basis[p] * image[q] for p, q in PAIRS]
                part = [t if p is None else p + t for p, t in zip(part, terms)]
        return [t + jnp.where(inside, p, 0.0) for t, p in zip(totals, part)]

    totals = lax.fori_loop(0, deep, body, [jnp.zeros((GROUP, LANES), jnp.float32)] * 9)
    sums_ref[...] = jnp.zeros_like(sums_ref)
    for k, total in enumerate(totals):
        sums_ref[pl.ds(k, 1), :] = jnp.sum(total, axis=0, keepdims=True)
    across = jnp.sum(sums_ref[...], axis=1, keepdims=True)
    row = lax.broadcasted_iota(jnp.int32, sums_ref.shape, 0)
    lane = lax.broadcasted_iota(jnp.int32, sums_ref.shape, 1)
    row = jnp.sum(jnp.where(row == lane, across, 0.0), axis=0, keepdims=True)
    out_ref[...] = jnp.broadcast_to(row, out_ref.shape)


def weights_of(gathered_ref):
    total = jnp.sum(gathered_ref[...], axis=0, keepdims=True)
    b1, b2, b3, h11, h21, h31, h22, h32, h33 = [
        jnp.broadcast_to(total[:, k : k + 1], (GROUP, LANES)) for k in range(9)
    ]
    l21 = h21 / h11
    l31 = h31 / h11
    d2 = h22 - l21 * h21
    e32 = h32 - l31 * h21
    l32 = e32 / d2
    d3 = h33 - l31 * h31 - l32 * e32
    y2 = b2 - l21 * b1
    y3 = b3 - l31 * b1 - l32 * y2
    c3 = y3 / d3
    c2 = y2 / d2 - l32 * c3
    c1 = b1 / h11 - l21 * c2 - l31 * c3
    return c1, c2, c3


def widen(value, width):
    return jnp.concatenate([value] * (width // LANES), axis=1)


def spread(natural_ref, l, i, deep, value):
    for b in range(value.shape[1] // LANES):
        natural_ref[l, b, pl.ds(i, GROUP, stride=deep), :] = value[:, b * LANES : (b + 1) * LANES]


def settle(natural_ref, out_ref):
    for b in range(natural_ref.shape[1]):
        out_ref[:, :, pl.ds(b * LANES, LANES)] = natural_ref[:, b, : out_ref.shape[1], :]


def first_kernel(
    deep, rows, width, outer,
    field_ref, edge_ref, above_ref, below_ref, ends_ref, middle_ref,
    basis_ref, drop_ref, cap_ref, later_ref, out_ref,
    whole_ref, grid_ref, cross_ref, start_ref, scaled_ref, second_ref, image_ref, inject_ref, sums_ref,
):
    wide = width + LANES
    blocks = wide // LANES
    inner = pl.ds(0, rows)
    for f in range(7):
        whole_ref[f, blocks - 1, inner, :] = edge_ref[f]
        for b in range(blocks - 1):
            if f < 5:
                whole_ref[f, b, inner, :] = field_ref[f, b]
            else:
                end, middle = ends_ref.at[f - 5, b], middle_ref.at[f - 5, b]
                whole_ref[f, b, pl.ds(0, outer), :] = end[pl.ds(0, outer), :]
                whole_ref[f, b, pl.ds(outer, rows - 2 * outer), :] = middle[...]
                whole_ref[f, b, pl.ds(rows - outer, outer), :] = end[pl.ds(outer, outer), :]
        for ref, place in ((below_ref, pl.ds(rows, HALO)), (above_ref, pl.ds(rows + HALO, HALO))):
            for b in range(blocks - 1):
                whole_ref[f, b, place, :] = ref[f * (blocks - 1) + b]
            whole_ref[f, blocks - 1, place, :] = ref[7 * (blocks - 1) + f]

    def slab(f, i):
        pick = pl.ds(i, GROUP, stride=deep)
        return jnp.concatenate([whole_ref[f, b, pick, :] for b in range(blocks)], axis=1)

    for l in range(2):
        for i in range(deep):
            cap_ref[l, i] = slab(l, i)
            drop_ref[l, i] = slab(2 + l, i)
    weigh(cap_ref, deep, grid_ref, cross_ref)
    for i in range(deep):
        tap = slab(4, i)
        for k in range(STEPS):
            charge = slab(5 + k, i)
            for a in range(3):
                sent = [jnp.where(tap == float(3 * a + b), charge, 0.0) for b in range(3)]
                value = pltpu.roll(sent[0], wide - 1, axis=1) + sent[1] + pltpu.roll(sent[2], 1, axis=1)
                inject_ref[k, a, i] = value

    def current(k, i):
        if i == deep - 1:
            upward = pltpu.roll(inject_ref[k, 0, 0], GROUP - 1, axis=0)
        else:
            upward = inject_ref[k, 0, i + 1]
        if i == 0:
            downward = pltpu.roll(inject_ref[k, 2, deep - 1], 1, axis=0)
        else:
            downward = inject_ref[k, 2, i - 1]
        return upward + inject_ref[k, 1, i] + downward

    for i in range(deep):
        later_ref[i] = current(1, i)
    residual(deep, drop_ref, lambda i: current(0, i), cross_ref, width, start_ref, scaled_ref)
    krylov(deep, width, cap_ref, grid_ref, cross_ref, scaled_ref, second_ref, basis_ref, image_ref)
    moments(deep, rows, width, start_ref, basis_ref, image_ref, sums_ref, out_ref)


def first_step(field, edge, above, below, ends, middle, count):
    rows = field.shape[2]
    width = field.shape[1] * LANES
    wide = width + LANES
    deep = (rows + 2 * HALO) // GROUP
    full = (2, deep, GROUP, wide)
    shapes = [(3, *full), full, full, full[1:], (count, LANES)]
    return pl.pallas_call(
        functools.partial(first_kernel, deep, rows, width, ends.shape[2] // 2),
        out_shape=[jax.ShapeDtypeStruct(s, jnp.float32) for s in shapes],
        in_specs=[vmem()] * 6,
        out_specs=[vmem()] * len(shapes),
        scratch_shapes=[
            pltpu.VMEM((7, wide // LANES, deep * GROUP, LANES), jnp.float32),
            pltpu.VMEM(full, jnp.float32),
            pltpu.VMEM(full, jnp.float32),
            pltpu.VMEM((2, deep, GROUP, width), jnp.float32),
            pltpu.VMEM(full, jnp.float32),
            pltpu.VMEM(full, jnp.float32),
            pltpu.VMEM((3, 2, deep, GROUP, width), jnp.float32),
            pltpu.VMEM((STEPS, 3, *full[1:]), jnp.float32),
            pltpu.VMEM((2 * GROUP, LANES), jnp.float32),
        ],
        compiler_params=params(20),
        name="first_step",
    )(field, edge, above, below, ends, middle)


def second_kernel(
    deep, rows, width,
    gathered_ref, basis_ref, drop_ref, cap_ref, later_ref,
    first_ref, next_ref, held_ref, out_ref,
    now_ref, grid_ref, cross_ref, start_ref, scaled_ref, second_ref, image_ref, natural_ref, sums_ref,
):
    wide = width + LANES
    weigh(cap_ref, deep, grid_ref, cross_ref)
    weights = [widen(c, wide) for c in weights_of(gathered_ref)]
    for l in range(2):
        for i in range(deep):
            value = drop_ref[l, i]
            for n in range(3):
                value = value + weights[n] * basis_ref[n, l, i]
            now_ref[l, i] = value
            held_ref[l, i] = value[:, :width]
            spread(natural_ref, l, i, deep, value[:, :width])
    settle(natural_ref, first_ref)
    residual(deep, now_ref, lambda i: later_ref[i], cross_ref, width, start_ref, scaled_ref)
    krylov(deep, width, cap_ref, grid_ref, cross_ref, scaled_ref, second_ref, next_ref, image_ref)
    moments(deep, rows, width, start_ref, next_ref, image_ref, sums_ref, out_ref)


def second_step(gathered, basis, drop, cap, later, rows):
    deep = cap.shape[1]
    wide = cap.shape[-1]
    width = wide - LANES
    full = (2, deep, GROUP, wide)
    shapes = [(2, rows, width), (3, *full), (2, deep, GROUP, width), gathered.shape]
    return pl.pallas_call(
        functools.partial(second_kernel, deep, rows, width),
        out_shape=[jax.ShapeDtypeStruct(s, jnp.float32) for s in shapes],
        in_specs=[vmem()] * 5,
        out_specs=[vmem()] * len(shapes),
        scratch_shapes=[
            pltpu.VMEM(full, jnp.float32),
            pltpu.VMEM(full, jnp.float32),
            pltpu.VMEM(full, jnp.float32),
            pltpu.VMEM((2, deep, GROUP, width), jnp.float32),
            pltpu.VMEM(full, jnp.float32),
            pltpu.VMEM(full, jnp.float32),
            pltpu.VMEM((3, 2, deep, GROUP, width), jnp.float32),
            pltpu.VMEM((2, width // LANES, deep * GROUP, LANES), jnp.float32),
            pltpu.VMEM((2 * GROUP, LANES), jnp.float32),
        ],
        compiler_params=params(20),
        name="second_step",
    )(gathered, basis, drop, cap, later)


def last_kernel(deep, rows, width, gathered_ref, basis_ref, held_ref, out_ref, natural_ref):
    weights = [widen(c, width) for c in weights_of(gathered_ref)]
    for l in range(2):
        for i in range(deep):
            value = held_ref[l, i]
            for n in range(3):
                value = value + weights[n] * basis_ref[n, l, i, :, pl.ds(0, width)]
            spread(natural_ref, l, i, deep, value)
    settle(natural_ref, out_ref)


def last_step(gathered, basis, held, rows):
    deep = held.shape[1]
    width = held.shape[-1]
    return pl.pallas_call(
        functools.partial(last_kernel, deep, rows, width),
        out_shape=jax.ShapeDtypeStruct((2, rows, width), jnp.float32),
        in_specs=[vmem()] * 3,
        out_specs=vmem(),
        scratch_shapes=[
            pltpu.VMEM((2, width // LANES, deep * GROUP, LANES), jnp.float32),
        ],
        compiler_params=params(12),
        name="last_step",
    )(gathered, basis, held)


def shift(block, axis, up):
    count = lax.axis_size(axis)
    pairs = [(i, i + 1) for i in range(count - 1)]
    return lax.ppermute(block, axis, pairs if up else [(b, a) for a, b in pairs])


def exchange(block):
    return lax.all_to_all(block, BOTH, 0, 0, tiled=True)


def gather_tables(block):
    outer, inner = lax.axis_size("gx"), lax.axis_size("gy")
    groups = [
        [x * inner + y for x in range(parity, outer, 2) for y in range(inner)] for parity in range(2)
    ]
    own = lax.all_to_all(block, BOTH, 0, 0, tiled=True, axis_index_groups=groups)
    own = own.reshape(-1, LANES)
    return own, lax.ppermute(own, "gx", [(i, i ^ 1) for i in range(outer)])


def shards(tables, table_index, toggle, tap_code, capacitance, prior_drop):
    rows, cols = table_index.shape
    count = lax.axis_size("gx") * lax.axis_size("gy")
    inner = lax.axis_size("gy")
    many = tables.shape[0], inner
    outer = HALO
    block, codes = address(tables, tap_code, table_index, toggle, count // 2)
    table = gather_tables(block)
    field = jnp.concatenate([capacitance, prior_drop, codes])
    field = field.reshape(-1, rows, cols // LANES, LANES).transpose(0, 2, 1, 3)
    left = shift(field[:, -1], "gy", True)
    right = shift(field[:, 0], "gy", False)
    def ends_of(array):
        return jnp.concatenate([array[:outer], array[-outer:]])

    ends, pieces = lookup(ends_of(table_index), ends_of(toggle), table, many)
    edge = edge_lookup(left, right, pieces, many)

    def late(far):
        cut = slice(-HALO, None) if far else slice(0, HALO)
        charge, lower = [a[:, :, cut].reshape(-1, HALO, LANES) for a in (ends, field[:5])]
        return jnp.concatenate([lower, charge, edge[:, cut]])

    above = shift(late(True), "gx", True)
    below = shift(late(False), "gx", False)
    pieces, edge = lax.optimization_barrier((pieces, edge))
    middle = lookup(table_index[outer:-outer], toggle[outer:-outer], (pieces,), many)
    basis, drop, cap, later, part = first_step(field, edge, above, below, ends, middle, count)
    first, basis, held, part = second_step(exchange(part), basis, drop, cap, later, rows)
    return first, last_step(exchange(part), basis, held, rows)


def solution(mesh):
    in_specs = (
        P(BOTH, None),
        P("gx", "gy"),
        P("gx", "gy"),
        P("gx", "gy"),
        P(None, "gx", "gy"),
        P(None, "gx", "gy"),
    )
    out_specs = (P(None, "gx", "gy"), P(None, "gx", "gy"))
    return jax.shard_map(shards, mesh=mesh, in_specs=in_specs, out_specs=out_specs, check_vma=False)
```

```python
import functools
import math

import jax
import jax.numpy as jnp
from jax import lax
from jax.experimental import pallas as pl
from jax.experimental.pallas import tpu as pltpu
from jax.sharding import PartitionSpec as P

SUBSTEPS = 32
STEPS = 2
BOTH = ("gx", "gy")
LANES = 128
HALO = 20
GROUP = 8
LO = 4
CONDUCT = (1.0, 4.0)


def chebyshev_taus():
    theta = 1.05
    delta = 0.95
    return [1.0 / (theta + delta * math.cos((2 * i - 1) * math.pi / 6.0)) for i in (1, 2, 3)]


TAU = chebyshev_taus()
ALPHA = TAU[1] + (1.0 - TAU[1]) * TAU[0]
BETA = TAU[0] * TAU[1]
KEEP = (1.0 - TAU[2]) * BETA / TAU[2]
SHIFT = 0.75
RADIUS = 0.7
BACK = SHIFT / TAU[2]
FORMER = 0.5 * (RADIUS / TAU[2]) ** 2


def params(mib):
    return pltpu.CompilerParams(vmem_limit_bytes=mib * 2**20)


def vmem():
    return pl.BlockSpec(memory_space=pltpu.VMEM)


def address_kernel(
    table_in, tap_in, index_in, toggle_in, out_ref, codes_ref, table_ref, cells_ref, arrived
):
    copies = [pltpu.make_async_copy(table_in, table_ref, arrived.at[3])]
    for n, source in enumerate((tap_in, index_in, toggle_in)):
        copies.append(pltpu.make_async_copy(source, cells_ref.at[n], arrived.at[n]))
    for copy in copies:
        copy.start()
    copies[0].wait()
    table = table_ref[...]
    many = table.shape[0] // LO
    block = jnp.concatenate([table[a * many : (a + 1) * many] for a in range(LO)], axis=1)
    out_ref[...] = jnp.broadcast_to(block[None], out_ref.shape)
    for n in range(3):
        copies[1 + n].wait()
        codes_ref[n] = cells_ref[n].astype(jnp.float32)


def address(table, tap, index, toggle, count):
    many = table.shape[0] // LO
    return pl.pallas_call(
        address_kernel,
        out_shape=[
            jax.ShapeDtypeStruct((count, many, LANES), jnp.float32),
            jax.ShapeDtypeStruct((3, *tap.shape), jnp.float32),
        ],
        in_specs=[pl.BlockSpec(memory_space=pl.ANY)] * 4,
        out_specs=[vmem()] * 2,
        scratch_shapes=[
            pltpu.VMEM(table.shape, jnp.float32),
            pltpu.VMEM((3, *tap.shape), jnp.int32),
            pltpu.SemaphoreType.DMA((4,)),
        ],
        compiler_params=params(62),
        name="address",
    )(table, tap, index, toggle)


MANY = 8
CHUNK = 256


def split_kernel(table_refs, pieces_ref):
    for b, ref in enumerate(table_refs):
        across = ref[...].T
        high = across.astype(jnp.bfloat16)
        low = (across - high.astype(jnp.float32)).astype(jnp.bfloat16)
        for p, piece in enumerate((high, low)):
            pieces_ref[pl.ds((2 * p + b) * LANES, LANES), :] = piece


def charges(many, index, toggle, pieces_ref):
    many, inner = many
    cols = index.shape[1]
    groups = pieces_ref.shape[1]
    quarter = many // LO
    held = index & (many - 1)
    device = index // many
    half = (device // inner + lax.axis_index("gx")) & 1
    place = device // (2 * inner) * inner + (device & (inner - 1))
    row = place * quarter + (held & (quarter - 1))
    which = held // quarter + LO * half
    hot = []
    for k in range(groups // CHUNK):
        local = (row - CHUNK * k).astype(jnp.float32).astype(jnp.bfloat16)
        count = lax.broadcasted_iota(jnp.int32, (CHUNK, cols), 0)
        count = count.astype(jnp.float32).astype(jnp.bfloat16)
        same = jnp.broadcast_to(local, (CHUNK, cols)) == count
        hot.append(jnp.where(same, jnp.bfloat16(1), jnp.bfloat16(0)))
    got = jnp.dot(pieces_ref[...], jnp.concatenate(hot, 0), preferred_element_type=jnp.float32)
    half = got.shape[0] // 2
    value = (got[:half] + got[half:]).reshape(MANY, SUBSTEPS, cols)
    values = [value[a] for a in range(MANY)]
    for bit in range(MANY.bit_length() - 1):
        upper = (which >> bit) & 1 == 1
        values = [jnp.where(upper, v, u) for u, v in zip(values[::2], values[1::2])]
    chosen = values[0]
    moment = lax.broadcasted_iota(jnp.int32, (SUBSTEPS, cols), 0) + toggle
    share = SUBSTEPS // STEPS
    window = moment >> (share.bit_length() - 1)
    means = []
    for k in range(STEPS):
        total = jnp.sum(jnp.where(window == k, chosen, 0.0), axis=0, keepdims=True)
        means.append(total * (1.0 / share))
    return means


def lookup_rows(many, index_ref, toggle_ref, pieces_ref, out_ref):
    rows, cols = index_ref.shape
    unroll = rows if rows <= 24 else math.gcd(rows, 20)

    def body(i, carry):
        for u in range(unroll):
            row = pl.ds(i * unroll + u, 1)
            means = charges(many, index_ref[row, :], toggle_ref[row, :], pieces_ref)
            for k, mean in enumerate(means):
                for b in range(cols // LANES):
                    out_ref[k, b, row, :] = mean[:, b * LANES : (b + 1) * LANES]
        return carry

    lax.fori_loop(0, rows // unroll, body, 0)


def first_lookup_kernel(many, index_ref, toggle_ref, own_ref, other_ref, out_ref, pieces_ref):
    split_kernel((own_ref, other_ref), pieces_ref)
    lookup_rows(many, index_ref, toggle_ref, pieces_ref, out_ref)


def lookup_cost(cells, pieces):
    flops = 2 * cells * pieces.shape[0] * pieces.shape[1]
    return pl.CostEstimate(flops=flops, bytes_accessed=0, transcendentals=0)


def lookup(index, toggle, table, many):
    rows, cols = index.shape
    charge = jax.ShapeDtypeStruct((STEPS, cols // LANES, rows, LANES), jnp.float32)
    fresh = len(table) == 2
    pieces = table[0]
    if fresh:
        pieces = jax.ShapeDtypeStruct((2 * MANY * SUBSTEPS, pieces.shape[0]), jnp.bfloat16)
    return pl.pallas_call(
        functools.partial(first_lookup_kernel if fresh else lookup_rows, many),
        out_shape=[charge, pieces] if fresh else charge,
        in_specs=[vmem()] * (2 + len(table)),
        out_specs=[vmem()] * 2 if fresh else vmem(),
        compiler_params=params(20),
        cost_estimate=lookup_cost(rows * cols, pieces),
        name="lookup",
    )(index, toggle, *table)


def edge_lookup_kernel(many, left_ref, right_ref, pieces_ref, out_ref, cells_ref, got_ref):
    rows = left_ref.shape[1]
    lane = lax.broadcasted_iota(jnp.int32, (rows, LANES), 1)

    def merge(right, left):
        return jnp.where(lane < HALO, right, jnp.where(lane >= LANES - HALO, left, 0.0))

    for f in range(5):
        out_ref[f] = merge(right_ref[f], left_ref[f])
    pair = lax.broadcasted_iota(jnp.int32, (HALO, LANES), 1)
    for n in range(2):
        near = pltpu.roll(merge(right_ref[5 + n], left_ref[5 + n]), HALO, axis=1)
        turned = jnp.concatenate([near, jnp.zeros_like(near)], axis=0).T
        high = pltpu.roll(turned[HALO : 2 * HALO], LANES - rows, axis=1)
        cells_ref[n] = jnp.where(pair < rows, turned[:HALO], high).astype(jnp.int32)
    got_ref[...] = jnp.zeros_like(got_ref)
    step = 4
    for u in range(HALO // step):
        index, toggle = [
            jnp.concatenate([cells_ref[n, pl.ds(step * u + r, 1), :] for r in range(step)], axis=1)
            for n in range(2)
        ]
        for k, mean in enumerate(charges(many, index, toggle, pieces_ref)):
            for r in range(step):
                got_ref[k, pl.ds(step * u + r, 1), :] = mean[:, r * LANES : (r + 1) * LANES]
    inside = out_ref[0] > 0.0
    for k in range(STEPS):
        back = got_ref[k].T
        left = pltpu.roll(back[:rows], LANES - HALO, axis=1)
        out_ref[5 + k] = jnp.where(inside, merge(back[rows:], left), 0.0)


def edge_lookup(left, right, pieces, many):
    rows = left.shape[1]
    assert 2 * rows == LANES
    return pl.pallas_call(
        functools.partial(edge_lookup_kernel, many),
        out_shape=jax.ShapeDtypeStruct(left.shape, jnp.float32),
        in_specs=[vmem()] * 3,
        out_specs=vmem(),
        scratch_shapes=[
            pltpu.VMEM((2, HALO, LANES), jnp.int32),
            pltpu.VMEM((STEPS, LANES, LANES), jnp.float32),
        ],
        compiler_params=params(20),
        cost_estimate=lookup_cost(2 * HALO * rows, pieces),
        name="edge_lookup",
    )(left, right, pieces)


def sweep(deep, fetch, use):
    def load(i):
        if i < 0:
            return [pltpu.roll(fetch(l, deep - 1), 1, axis=0) for l in range(2)]
        if i >= deep:
            return [pltpu.roll(fetch(l, 0), GROUP - 1, axis=0) for l in range(2)]
        return [fetch(l, i) for l in range(2)]

    held = {}
    for i in range(deep):
        held = {k: v for k, v in held.items() if k in (i - 1, i, i + 1)}
        for k in (i - 1, i, i + 1):
            if k not in held:
                held[k] = load(k)
        for l in range(2):
            center = held[i][l]
            width = center.shape[-1]
            beside = pltpu.roll(center, 1, axis=1) + pltpu.roll(center, width - 1, axis=1)
            around = (held[i - 1][l] + held[i + 1][l]) + beside
            use(l, i, center, around, held[i][1 - l])


def weigh(cap_ref, deep, grid_ref, cross_ref):
    for l in range(2):
        for i in range(deep):
            cap = cap_ref[l, i]
            inverse = jnp.where(cap > 0.0, 1.0 / (cap + (4.0 * CONDUCT[l] + 2.0)), 0.0)
            grid_ref[l, i] = CONDUCT[l] * inverse
            cross_ref[l, i] = 2.0 * inverse


def residual(deep, drop_ref, current, cross_ref, width, start_ref, scaled_ref):
    def use(l, i, center, around, other):
        value = CONDUCT[l] * around + 2.0 * other - (4.0 * CONDUCT[l] + 2.0) * center
        if l == 0:
            value = value + current(i)
        start_ref[l, i] = value[:, :width]
        scaled_ref[l, i] = value * (cross_ref[l, i] * 0.5)

    sweep(deep, lambda l, i: drop_ref[l, i], use)


def krylov(deep, width, cap_ref, grid_ref, cross_ref, scaled_ref, second_ref, basis_ref, image_ref):
    def coupled(l, i, around, other):
        return grid_ref[l, i] * around + cross_ref[l, i] * other

    def use_second(l, i, center, around, other):
        second_ref[l, i] = (ALPHA / BETA) * center + coupled(l, i, around, other)

    for n in range(3):

        def use_basis(l, i, center, around, other, n=n):
            value = KEEP * center + (
                scaled_ref[l, i] + BETA * coupled(l, i, around, other)
            )
            if n == 1:
                value = value - BACK * basis_ref[0, l, i]
            if n == 2:
                value = value - BACK * basis_ref[1, l, i] - FORMER * basis_ref[0, l, i]
            basis_ref[n, l, i] = value

        def use_image(l, i, center, around, other, n=n):
            value = center - coupled(l, i, around, other)
            if n < 2:
                scaled_ref[l, i] = value
            diagonal = cap_ref[l, i][:, :width] + (4.0 * CONDUCT[l] + 2.0)
            image_ref[n, l, i] = value[:, :width] * diagonal

        sweep(deep, lambda l, i: scaled_ref[l, i], use_second)
        sweep(deep, lambda l, i: second_ref[l, i], use_basis)
        sweep(deep, lambda l, i, n=n: basis_ref[n, l, i], use_image)


PAIRS = ((0, 0), (1, 0), (2, 0), (1, 1), (2, 1), (2, 2))


def moments(deep, rows, width, start_ref, basis_ref, image_ref, sums_ref, out_ref):
    sub = lax.broadcasted_iota(jnp.int32, (GROUP, LANES), 0)

    def body(i, totals):
        inside = sub * deep + i < rows
        part = [None] * 9
        for l in range(2):
            for b in range(width // LANES):
                lanes = pl.ds(b * LANES, LANES)
                start = start_ref[l, i, :, lanes]
                basis = [basis_ref[n, l, i, :, lanes] for n in range(3)]
                image = [image_ref[n, l, i, :, lanes] for n in range(3)]
                terms = [start * v for v in basis] + [basis[p] * image[q] for p, q in PAIRS]
                part = [t if p is None else p + t for p, t in zip(part, terms)]
        return [t + jnp.where(inside, p, 0.0) for t, p in zip(totals, part)]

    totals = lax.fori_loop(0, deep, body, [jnp.zeros((GROUP, LANES), jnp.float32)] * 9)
    sums_ref[...] = jnp.zeros_like(sums_ref)
    for k, total in enumerate(totals):
        sums_ref[pl.ds(k, 1), :] = jnp.sum(total, axis=0, keepdims=True)
    across = jnp.sum(sums_ref[...], axis=1, keepdims=True)
    row = lax.broadcasted_iota(jnp.int32, sums_ref.shape, 0)
    lane = lax.broadcasted_iota(jnp.int32, sums_ref.shape, 1)
    row = jnp.sum(jnp.where(row == lane, across, 0.0), axis=0, keepdims=True)
    out_ref[...] = jnp.broadcast_to(row, out_ref.shape)


def weights_of(gathered_ref):
    total = jnp.sum(gathered_ref[...], axis=0, keepdims=True)
    b1, b2, b3, h11, h21, h31, h22, h32, h33 = [
        jnp.broadcast_to(total[:, k : k + 1], (GROUP, LANES)) for k in range(9)
    ]
    l21 = h21 / h11
    l31 = h31 / h11
    d2 = h22 - l21 * h21
    e32 = h32 - l31 * h21
    l32 = e32 / d2
    d3 = h33 - l31 * h31 - l32 * e32
    y2 = b2 - l21 * b1
    y3 = b3 - l31 * b1 - l32 * y2
    c3 = y3 / d3
    c2 = y2 / d2 - l32 * c3
    c1 = b1 / h11 - l21 * c2 - l31 * c3
    return c1, c2, c3


def widen(value, width):
    return jnp.concatenate([value] * (width // LANES), axis=1)


def spread(natural_ref, l, i, deep, value):
    for b in range(value.shape[1] // LANES):
        natural_ref[l, b, pl.ds(i, GROUP, stride=deep), :] = value[:, b * LANES : (b + 1) * LANES]


def settle(natural_ref, out_ref):
    for b in range(natural_ref.shape[1]):
        out_ref[:, :, pl.ds(b * LANES, LANES)] = natural_ref[:, b, : out_ref.shape[1], :]


def first_kernel(
    deep, rows, width, outer,
    field_ref, edge_ref, above_ref, below_ref, ends_ref, middle_ref,
    basis_ref, drop_ref, cap_ref, later_ref, out_ref,
    whole_ref, grid_ref, cross_ref, start_ref, scaled_ref, second_ref, image_ref, inject_ref, sums_ref,
):
    wide = width + LANES
    blocks = wide // LANES
    inner = pl.ds(0, rows)
    for f in range(7):
        whole_ref[f, blocks - 1, inner, :] = edge_ref[f]
        for b in range(blocks - 1):
            if f < 5:
                whole_ref[f, b, inner, :] = field_ref[f, b]
            else:
                end, middle = ends_ref.at[f - 5, b], middle_ref.at[f - 5, b]
                whole_ref[f, b, pl.ds(0, outer), :] = end[pl.ds(0, outer), :]
                whole_ref[f, b, pl.ds(outer, rows - 2 * outer), :] = middle[...]
                whole_ref[f, b, pl.ds(rows - outer, outer), :] = end[pl.ds(outer, outer), :]
        for ref, place in ((below_ref, pl.ds(rows, HALO)), (above_ref, pl.ds(rows + HALO, HALO))):
            for b in range(blocks - 1):
                whole_ref[f, b, place, :] = ref[f * (blocks - 1) + b]
            whole_ref[f, blocks - 1, place, :] = ref[7 * (blocks - 1) + f]

    def slab(f, i):
        pick = pl.ds(i, GROUP, stride=deep)
        return jnp.concatenate([whole_ref[f, b, pick, :] for b in range(blocks)], axis=1)

    for l in range(2):
        for i in range(deep):
            cap_ref[l, i] = slab(l, i)
            drop_ref[l, i] = slab(2 + l, i)
    weigh(cap_ref, deep, grid_ref, cross_ref)
    for i in range(deep):
        tap = slab(4, i)
        for k in range(STEPS):
            charge = slab(5 + k, i)
            for a in range(3):
                sent = [jnp.where(tap == float(3 * a + b), charge, 0.0) for b in range(3)]
                value = pltpu.roll(sent[0], wide - 1, axis=1) + sent[1] + pltpu.roll(sent[2], 1, axis=1)
                inject_ref[k, a, i] = value

    def current(k, i):
        if i == deep - 1:
            upward = pltpu.roll(inject_ref[k, 0, 0], GROUP - 1, axis=0)
        else:
            upward = inject_ref[k, 0, i + 1]
        if i == 0:
            downward = pltpu.roll(inject_ref[k, 2, deep - 1], 1, axis=0)
        else:
            downward = inject_ref[k, 2, i - 1]
        return upward + inject_ref[k, 1, i] + downward

    for i in range(deep):
        later_ref[i] = current(1, i)
    residual(deep, drop_ref, lambda i: current(0, i), cross_ref, width, start_ref, scaled_ref)
    krylov(deep, width, cap_ref, grid_ref, cross_ref, scaled_ref, second_ref, basis_ref, image_ref)
    moments(deep, rows, width, start_ref, basis_ref, image_ref, sums_ref, out_ref)


def first_step(field, edge, above, below, ends, middle, count):
    rows = field.shape[2]
    width = field.shape[1] * LANES
    wide = width + LANES
    deep = (rows + 2 * HALO) // GROUP
    full = (2, deep, GROUP, wide)
    shapes = [(3, *full), full, full, full[1:], (count, LANES)]
    return pl.pallas_call(
        functools.partial(first_kernel, deep, rows, width, ends.shape[2] // 2),
        out_shape=[jax.ShapeDtypeStruct(s, jnp.float32) for s in shapes],
        in_specs=[vmem()] * 6,
        out_specs=[vmem()] * len(shapes),
        scratch_shapes=[
            pltpu.VMEM((7, wide // LANES, deep * GROUP, LANES), jnp.float32),
            pltpu.VMEM(full, jnp.float32),
            pltpu.VMEM(full, jnp.float32),
            pltpu.VMEM((2, deep, GROUP, width), jnp.float32),
            pltpu.VMEM(full, jnp.float32),
            pltpu.VMEM(full, jnp.float32),
            pltpu.VMEM((3, 2, deep, GROUP, width), jnp.float32),
            pltpu.VMEM((STEPS, 3, *full[1:]), jnp.float32),
            pltpu.VMEM((2 * GROUP, LANES), jnp.float32),
        ],
        compiler_params=params(20),
        name="first_step",
    )(field, edge, above, below, ends, middle)


def second_kernel(
    deep, rows, width,
    gathered_ref, basis_ref, drop_ref, cap_ref, later_ref,
    first_ref, next_ref, held_ref, out_ref,
    now_ref, grid_ref, cross_ref, start_ref, scaled_ref, second_ref, image_ref, natural_ref, sums_ref,
):
    wide = width + LANES
    weigh(cap_ref, deep, grid_ref, cross_ref)
    weights = [widen(c, wide) for c in weights_of(gathered_ref)]
    for l in range(2):
        for i in range(deep):
            value = drop_ref[l, i]
            for n in range(3):
                value = value + weights[n] * basis_ref[n, l, i]
            now_ref[l, i] = value
            held_ref[l, i] = value[:, :width]
            spread(natural_ref, l, i, deep, value[:, :width])
    settle(natural_ref, first_ref)
    residual(deep, now_ref, lambda i: later_ref[i], cross_ref, width, start_ref, scaled_ref)
    krylov(deep, width, cap_ref, grid_ref, cross_ref, scaled_ref, second_ref, next_ref, image_ref)
    moments(deep, rows, width, start_ref, next_ref, image_ref, sums_ref, out_ref)


def second_step(gathered, basis, drop, cap, later, rows):
    deep = cap.shape[1]
    wide = cap.shape[-1]
    width = wide - LANES
    full = (2, deep, GROUP, wide)
    shapes = [(2, rows, width), (3, *full), (2, deep, GROUP, width), gathered.shape]
    return pl.pallas_call(
        functools.partial(second_kernel, deep, rows, width),
        out_shape=[jax.ShapeDtypeStruct(s, jnp.float32) for s in shapes],
        in_specs=[vmem()] * 5,
        out_specs=[vmem()] * len(shapes),
        scratch_shapes=[
            pltpu.VMEM(full, jnp.float32),
            pltpu.VMEM(full, jnp.float32),
            pltpu.VMEM(full, jnp.float32),
            pltpu.VMEM((2, deep, GROUP, width), jnp.float32),
            pltpu.VMEM(full, jnp.float32),
            pltpu.VMEM(full, jnp.float32),
            pltpu.VMEM((3, 2, deep, GROUP, width), jnp.float32),
            pltpu.VMEM((2, width // LANES, deep * GROUP, LANES), jnp.float32),
            pltpu.VMEM((2 * GROUP, LANES), jnp.float32),
        ],
        compiler_params=params(20),
        name="second_step",
    )(gathered, basis, drop, cap, later)


def last_kernel(deep, rows, width, gathered_ref, basis_ref, held_ref, out_ref, natural_ref):
    weights = [widen(c, width) for c in weights_of(gathered_ref)]
    for l in range(2):
        for i in range(deep):
            value = held_ref[l, i]
            for n in range(3):
                value = value + weights[n] * basis_ref[n, l, i, :, pl.ds(0, width)]
            spread(natural_ref, l, i, deep, value)
    settle(natural_ref, out_ref)


def last_step(gathered, basis, held, rows):
    deep = held.shape[1]
    width = held.shape[-1]
    return pl.pallas_call(
        functools.partial(last_kernel, deep, rows, width),
        out_shape=jax.ShapeDtypeStruct((2, rows, width), jnp.float32),
        in_specs=[vmem()] * 3,
        out_specs=vmem(),
        scratch_shapes=[
            pltpu.VMEM((2, width // LANES, deep * GROUP, LANES), jnp.float32),
        ],
        compiler_params=params(12),
        name="last_step",
    )(gathered, basis, held)


def shift(block, axis, up):
    count = lax.axis_size(axis)
    pairs = [(i, i + 1) for i in range(count - 1)]
    return lax.ppermute(block, axis, pairs if up else [(b, a) for a, b in pairs])


def exchange(block):
    return lax.all_to_all(block, BOTH, 0, 0, tiled=True)


def gather_tables(block):
    outer, inner = lax.axis_size("gx"), lax.axis_size("gy")
    groups = [
        [x * inner + y for x in range(parity, outer, 2) for y in range(inner)] for parity in range(2)
    ]
    own = lax.all_to_all(block, BOTH, 0, 0, tiled=True, axis_index_groups=groups)
    own = own.reshape(-1, LANES)
    return own, lax.ppermute(own, "gx", [(i, i ^ 1) for i in range(outer)])


def shards(tables, table_index, toggle, tap_code, capacitance, prior_drop):
    rows, cols = table_index.shape
    count = lax.axis_size("gx") * lax.axis_size("gy")
    inner = lax.axis_size("gy")
    many = tables.shape[0], inner
    outer = HALO
    block, codes = address(tables, tap_code, table_index, toggle, count // 2)
    table = gather_tables(block)
    field = jnp.concatenate([capacitance, prior_drop, codes])
    field = field.reshape(-1, rows, cols // LANES, LANES).transpose(0, 2, 1, 3)
    left = shift(field[:, -1], "gy", True)
    right = shift(field[:, 0], "gy", False)
    def ends_of(array):
        return jnp.concatenate([array[:outer], array[-outer:]])

    ends, pieces = lookup(ends_of(table_index), ends_of(toggle), table, many)
    edge = edge_lookup(left, right, pieces, many)

    def late(far):
        cut = slice(-HALO, None) if far else slice(0, HALO)
        charge, lower = [a[:, :, cut].reshape(-1, HALO, LANES) for a in (ends, field[:5])]
        return jnp.concatenate([lower, charge, edge[:, cut]])

    above = shift(late(True), "gx", True)
    below = shift(late(False), "gx", False)
    pieces, edge = lax.optimization_barrier((pieces, edge))
    middle = lookup(table_index[outer:-outer], toggle[outer:-outer], (pieces,), many)
    basis, drop, cap, later, part = first_step(field, edge, above, below, ends, middle, count)
    first, basis, held, part = second_step(exchange(part), basis, drop, cap, later, rows)
    return first, last_step(exchange(part), basis, held, rows)


def solution(mesh):
    in_specs = (
        P(BOTH, None),
        P("gx", "gy"),
        P("gx", "gy"),
        P("gx", "gy"),
        P(None, "gx", "gy"),
        P(None, "gx", "gy"),
    )
    out_specs = (P(None, "gx", "gy"), P(None, "gx", "gy"))
    return jax.shard_map(shards, mesh=mesh, in_specs=in_specs, out_specs=out_specs, check_vma=False)
```

```python
import functools
import math

import jax
import jax.numpy as jnp
from jax import lax
from jax.experimental import pallas as pl
from jax.experimental.pallas import tpu as pltpu
from jax.sharding import PartitionSpec as P

SUBSTEPS = 32
STEPS = 2
BOTH = ("gx", "gy")
LANES = 128
HALO = 20
GROUP = 8
LO = 4
CONDUCT = (1.0, 4.0)


def chebyshev_taus():
    theta = 1.05
    delta = 0.95
    return [1.0 / (theta + delta * math.cos((2 * i - 1) * math.pi / 6.0)) for i in (1, 2, 3)]


TAU = chebyshev_taus()
ALPHA = TAU[1] + (1.0 - TAU[1]) * TAU[0]
BETA = TAU[0] * TAU[1]
KEEP = (1.0 - TAU[2]) * BETA / TAU[2]
SHIFT = 0.75
RADIUS = 0.7
BACK = SHIFT / TAU[2]
FORMER = 0.5 * (RADIUS / TAU[2]) ** 2


def params(mib):
    return pltpu.CompilerParams(vmem_limit_bytes=mib * 2**20)


def vmem():
    return pl.BlockSpec(memory_space=pltpu.VMEM)


def address_kernel(
    table_in, tap_in, index_in, toggle_in, out_ref, codes_ref, table_ref, cells_ref, arrived
):
    copies = [pltpu.make_async_copy(table_in, table_ref, arrived.at[3])]
    for n, source in enumerate((tap_in, index_in, toggle_in)):
        copies.append(pltpu.make_async_copy(source, cells_ref.at[n], arrived.at[n]))
    for copy in copies:
        copy.start()
    copies[0].wait()
    table = table_ref[...]
    many = table.shape[0] // LO
    block = jnp.concatenate([table[a * many : (a + 1) * many] for a in range(LO)], axis=1)
    out_ref[...] = jnp.broadcast_to(block[None], out_ref.shape)
    for n in range(3):
        copies[1 + n].wait()
        codes_ref[n] = cells_ref[n].astype(jnp.float32)


def address(table, tap, index, toggle, count):
    many = table.shape[0] // LO
    return pl.pallas_call(
        address_kernel,
        out_shape=[
            jax.ShapeDtypeStruct((count, many, LANES), jnp.float32),
            jax.ShapeDtypeStruct((3, *tap.shape), jnp.float32),
        ],
        in_specs=[pl.BlockSpec(memory_space=pl.ANY)] * 4,
        out_specs=[vmem()] * 2,
        scratch_shapes=[
            pltpu.VMEM(table.shape, jnp.float32),
            pltpu.VMEM((3, *tap.shape), jnp.int32),
            pltpu.SemaphoreType.DMA((4,)),
        ],
        compiler_params=params(62),
        name="address",
    )(table, tap, index, toggle)


MANY = 8
CHUNK = 256


def split_kernel(table_refs, pieces_ref):
    for b, ref in enumerate(table_refs):
        across = ref[...].T
        high = across.astype(jnp.bfloat16)
        low = (across - high.astype(jnp.float32)).astype(jnp.bfloat16)
        for p, piece in enumerate((high, low)):
            pieces_ref[pl.ds((2 * p + b) * LANES, LANES), :] = piece


def charges(many, index, toggle, pieces_ref):
    many, inner = many
    cols = index.shape[1]
    groups = pieces_ref.shape[1]
    quarter = many // LO
    held = index & (many - 1)
    device = index // many
    half = (device // inner + lax.axis_index("gx")) & 1
    place = device // (2 * inner) * inner + (device & (inner - 1))
    row = place * quarter + (held & (quarter - 1))
    which = held // quarter + LO * half
    hot = []
    for k in range(groups // CHUNK):
        local = (row - CHUNK * k).astype(jnp.float32).astype(jnp.bfloat16)
        count = lax.broadcasted_iota(jnp.int32, (CHUNK, cols), 0)
        count = count.astype(jnp.float32).astype(jnp.bfloat16)
        same = jnp.broadcast_to(local, (CHUNK, cols)) == count
        hot.append(jnp.where(same, jnp.bfloat16(1), jnp.bfloat16(0)))
    got = jnp.dot(pieces_ref[...], jnp.concatenate(hot, 0), preferred_element_type=jnp.float32)
    half = got.shape[0] // 2
    value = (got[:half] + got[half:]).reshape(MANY, SUBSTEPS, cols)
    chosen = value[0]
    for a in range(1, MANY):
        chosen = jnp.where(which == a, value[a], chosen)
    moment = lax.broadcasted_iota(jnp.int32, (SUBSTEPS, cols), 0) + toggle
    share = SUBSTEPS // STEPS
    means = []
    for k in range(STEPS):
        inside = (moment >= k * share) & (moment < (k + 1) * share)
        total = jnp.sum(jnp.where(inside, chosen, 0.0), axis=0, keepdims=True)
        means.append(total * (1.0 / share))
    return means


def lookup_rows(many, index_ref, toggle_ref, pieces_ref, out_ref):
    rows, cols = index_ref.shape
    for r in range(rows):
        row = pl.ds(r, 1)
        means = charges(many, index_ref[row, :], toggle_ref[row, :], pieces_ref)
        for k, mean in enumerate(means):
            for b in range(cols // LANES):
                out_ref[k, b, row, :] = mean[:, b * LANES : (b + 1) * LANES]


def first_lookup_kernel(many, index_ref, toggle_ref, own_ref, other_ref, out_ref, pieces_ref):
    split_kernel((own_ref, other_ref), pieces_ref)
    lookup_rows(many, index_ref, toggle_ref, pieces_ref, out_ref)


def lookup_cost(cells, pieces):
    flops = 2 * cells * pieces.shape[0] * pieces.shape[1]
    return pl.CostEstimate(flops=flops, bytes_accessed=0, transcendentals=0)


def lookup(index, toggle, table, many):
    rows, cols = index.shape
    charge = jax.ShapeDtypeStruct((STEPS, cols // LANES, rows, LANES), jnp.float32)
    fresh = len(table) == 2
    pieces = table[0]
    if fresh:
        pieces = jax.ShapeDtypeStruct((2 * MANY * SUBSTEPS, pieces.shape[0]), jnp.bfloat16)
    return pl.pallas_call(
        functools.partial(first_lookup_kernel if fresh else lookup_rows, many),
        out_shape=[charge, pieces] if fresh else charge,
        in_specs=[vmem()] * (2 + len(table)),
        out_specs=[vmem()] * 2 if fresh else vmem(),
        compiler_params=params(20),
        cost_estimate=lookup_cost(rows * cols, pieces),
        name="lookup",
    )(index, toggle, *table)


def edge_lookup_kernel(many, left_ref, right_ref, pieces_ref, out_ref, cells_ref, got_ref):
    rows = left_ref.shape[1]
    lane = lax.broadcasted_iota(jnp.int32, (rows, LANES), 1)

    def merge(right, left):
        return jnp.where(lane < HALO, right, jnp.where(lane >= LANES - HALO, left, 0.0))

    for f in range(5):
        out_ref[f] = merge(right_ref[f], left_ref[f])
    pair = lax.broadcasted_iota(jnp.int32, (HALO, LANES), 1)
    for n in range(2):
        near = pltpu.roll(merge(right_ref[5 + n], left_ref[5 + n]), HALO, axis=1)
        turned = jnp.concatenate([near, jnp.zeros_like(near)], axis=0).T
        high = pltpu.roll(turned[HALO : 2 * HALO], LANES - rows, axis=1)
        cells_ref[n] = jnp.where(pair < rows, turned[:HALO], high).astype(jnp.int32)
    got_ref[...] = jnp.zeros_like(got_ref)
    step = 4
    for u in range(HALO // step):
        index, toggle = [
            jnp.concatenate([cells_ref[n, pl.ds(step * u + r, 1), :] for r in range(step)], axis=1)
            for n in range(2)
        ]
        for k, mean in enumerate(charges(many, index, toggle, pieces_ref)):
            for r in range(step):
                got_ref[k, pl.ds(step * u + r, 1), :] = mean[:, r * LANES : (r + 1) * LANES]
    inside = out_ref[0] > 0.0
    for k in range(STEPS):
        back = got_ref[k].T
        left = pltpu.roll(back[:rows], LANES - HALO, axis=1)
        out_ref[5 + k] = jnp.where(inside, merge(back[rows:], left), 0.0)


def edge_lookup(left, right, pieces, many):
    rows = left.shape[1]
    assert 2 * rows == LANES
    return pl.pallas_call(
        functools.partial(edge_lookup_kernel, many),
        out_shape=jax.ShapeDtypeStruct(left.shape, jnp.float32),
        in_specs=[vmem()] * 3,
        out_specs=vmem(),
        scratch_shapes=[
            pltpu.VMEM((2, HALO, LANES), jnp.int32),
            pltpu.VMEM((STEPS, LANES, LANES), jnp.float32),
        ],
        compiler_params=params(20),
        cost_estimate=lookup_cost(2 * HALO * rows, pieces),
        name="edge_lookup",
    )(left, right, pieces)


def sweep(deep, fetch, use):
    def load(i):
        if i < 0:
            return [pltpu.roll(fetch(l, deep - 1), 1, axis=0) for l in range(2)]
        if i >= deep:
            return [pltpu.roll(fetch(l, 0), GROUP - 1, axis=0) for l in range(2)]
        return [fetch(l, i) for l in range(2)]

    held = {}
    for i in range(deep):
        held = {k: v for k, v in held.items() if k in (i - 1, i, i + 1)}
        for k in (i - 1, i, i + 1):
            if k not in held:
                held[k] = load(k)
        for l in range(2):
            center = held[i][l]
            width = center.shape[-1]
            beside = pltpu.roll(center, 1, axis=1) + pltpu.roll(center, width - 1, axis=1)
            around = (held[i - 1][l] + held[i + 1][l]) + beside
            use(l, i, center, around, held[i][1 - l])


def weigh(cap_ref, deep, grid_ref, cross_ref):
    for l in range(2):
        for i in range(deep):
            cap = cap_ref[l, i]
            inverse = jnp.where(cap > 0.0, 1.0 / (cap + (4.0 * CONDUCT[l] + 2.0)), 0.0)
            grid_ref[l, i] = CONDUCT[l] * inverse
            cross_ref[l, i] = 2.0 * inverse


def residual(deep, drop_ref, current, cross_ref, width, start_ref, scaled_ref):
    def use(l, i, center, around, other):
        value = CONDUCT[l] * around + 2.0 * other - (4.0 * CONDUCT[l] + 2.0) * center
        if l == 0:
            value = value + current(i)
        start_ref[l, i] = value[:, :width]
        scaled_ref[l, i] = value * (cross_ref[l, i] * 0.5)

    sweep(deep, lambda l, i: drop_ref[l, i], use)


def krylov(deep, width, cap_ref, grid_ref, cross_ref, scaled_ref, second_ref, basis_ref, image_ref):
    def coupled(l, i, around, other):
        return grid_ref[l, i] * around + cross_ref[l, i] * other

    def use_second(l, i, center, around, other):
        second_ref[l, i] = (ALPHA / BETA) * center + coupled(l, i, around, other)

    for n in range(3):

        def use_basis(l, i, center, around, other, n=n):
            value = KEEP * center + (
                scaled_ref[l, i] + BETA * coupled(l, i, around, other)
            )
            if n == 1:
                value = value - BACK * basis_ref[0, l, i]
            if n == 2:
                value = value - BACK * basis_ref[1, l, i] - FORMER * basis_ref[0, l, i]
            basis_ref[n, l, i] = value

        def use_image(l, i, center, around, other, n=n):
            value = center - coupled(l, i, around, other)
            if n < 2:
                scaled_ref[l, i] = value
            diagonal = cap_ref[l, i][:, :width] + (4.0 * CONDUCT[l] + 2.0)
            image_ref[n, l, i] = value[:, :width] * diagonal

        sweep(deep, lambda l, i: scaled_ref[l, i], use_second)
        sweep(deep, lambda l, i: second_ref[l, i], use_basis)
        sweep(deep, lambda l, i, n=n: basis_ref[n, l, i], use_image)


PAIRS = ((0, 0), (1, 0), (2, 0), (1, 1), (2, 1), (2, 2))


def moments(deep, rows, width, start_ref, basis_ref, image_ref, sums_ref, out_ref):
    sub = lax.broadcasted_iota(jnp.int32, (GROUP, LANES), 0)

    def body(i, totals):
        inside = sub * deep + i < rows
        part = [None] * 9
        for l in range(2):
            for b in range(width // LANES):
                lanes = pl.ds(b * LANES, LANES)
                start = start_ref[l, i, :, lanes]
                basis = [basis_ref[n, l, i, :, lanes] for n in range(3)]
                image = [image_ref[n, l, i, :, lanes] for n in range(3)]
                terms = [start * v for v in basis] + [basis[p] * image[q] for p, q in PAIRS]
                part = [t if p is None else p + t for p, t in zip(part, terms)]
        return [t + jnp.where(inside, p, 0.0) for t, p in zip(totals, part)]

    totals = lax.fori_loop(0, deep, body, [jnp.zeros((GROUP, LANES), jnp.float32)] * 9)
    sums_ref[...] = jnp.zeros_like(sums_ref)
    for k, total in enumerate(totals):
        sums_ref[pl.ds(k, 1), :] = jnp.sum(total, axis=0, keepdims=True)
    across = jnp.sum(sums_ref[...], axis=1, keepdims=True)
    row = lax.broadcasted_iota(jnp.int32, sums_ref.shape, 0)
    lane = lax.broadcasted_iota(jnp.int32, sums_ref.shape, 1)
    row = jnp.sum(jnp.where(row == lane, across, 0.0), axis=0, keepdims=True)
    out_ref[...] = jnp.broadcast_to(row, out_ref.shape)


def weights_of(gathered_ref):
    total = jnp.sum(gathered_ref[...], axis=0, keepdims=True)
    b1, b2, b3, h11, h21, h31, h22, h32, h33 = [
        jnp.broadcast_to(total[:, k : k + 1], (GROUP, LANES)) for k in range(9)
    ]
    l21 = h21 / h11
    l31 = h31 / h11
    d2 = h22 - l21 * h21
    e32 = h32 - l31 * h21
    l32 = e32 / d2
    d3 = h33 - l31 * h31 - l32 * e32
    y2 = b2 - l21 * b1
    y3 = b3 - l31 * b1 - l32 * y2
    c3 = y3 / d3
    c2 = y2 / d2 - l32 * c3
    c1 = b1 / h11 - l21 * c2 - l31 * c3
    return c1, c2, c3


def widen(value, width):
    return jnp.concatenate([value] * (width // LANES), axis=1)


def spread(natural_ref, l, i, deep, value):
    for b in range(value.shape[1] // LANES):
        natural_ref[l, b, pl.ds(i, GROUP, stride=deep), :] = value[:, b * LANES : (b + 1) * LANES]


def settle(natural_ref, out_ref):
    for b in range(natural_ref.shape[1]):
        out_ref[:, :, pl.ds(b * LANES, LANES)] = natural_ref[:, b, : out_ref.shape[1], :]


def first_kernel(
    deep, rows, width, outer,
    field_ref, edge_ref, above_ref, below_ref, ends_ref, middle_ref,
    basis_ref, drop_ref, cap_ref, later_ref, out_ref,
    whole_ref, grid_ref, cross_ref, start_ref, scaled_ref, second_ref, image_ref, inject_ref, sums_ref,
):
    wide = width + LANES
    blocks = wide // LANES
    inner = pl.ds(0, rows)
    for f in range(7):
        whole_ref[f, blocks - 1, inner, :] = edge_ref[f]
        for b in range(blocks - 1):
            if f < 5:
                whole_ref[f, b, inner, :] = field_ref[f, b]
            else:
                end, middle = ends_ref.at[f - 5, b], middle_ref.at[f - 5, b]
                whole_ref[f, b, pl.ds(0, outer), :] = end[pl.ds(0, outer), :]
                whole_ref[f, b, pl.ds(outer, rows - 2 * outer), :] = middle[...]
                whole_ref[f, b, pl.ds(rows - outer, outer), :] = end[pl.ds(outer, outer), :]
        for ref, place in ((below_ref, pl.ds(rows, HALO)), (above_ref, pl.ds(rows + HALO, HALO))):
            for b in range(blocks - 1):
                whole_ref[f, b, place, :] = ref[f * (blocks - 1) + b]
            whole_ref[f, blocks - 1, place, :] = ref[7 * (blocks - 1) + f]

    def slab(f, i):
        pick = pl.ds(i, GROUP, stride=deep)
        return jnp.concatenate([whole_ref[f, b, pick, :] for b in range(blocks)], axis=1)

    for l in range(2):
        for i in range(deep):
            cap_ref[l, i] = slab(l, i)
            drop_ref[l, i] = slab(2 + l, i)
    weigh(cap_ref, deep, grid_ref, cross_ref)
    for i in range(deep):
        tap = slab(4, i)
        for k in range(STEPS):
            charge = slab(5 + k, i)
            for a in range(3):
                sent = [jnp.where(tap == float(3 * a + b), charge, 0.0) for b in range(3)]
                value = pltpu.roll(sent[0], wide - 1, axis=1) + sent[1] + pltpu.roll(sent[2], 1, axis=1)
                inject_ref[k, a, i] = value

    def current(k, i):
        if i == deep - 1:
            upward = pltpu.roll(inject_ref[k, 0, 0], GROUP - 1, axis=0)
        else:
            upward = inject_ref[k, 0, i + 1]
        if i == 0:
            downward = pltpu.roll(inject_ref[k, 2, deep - 1], 1, axis=0)
        else:
            downward = inject_ref[k, 2, i - 1]
        return upward + inject_ref[k, 1, i] + downward

    for i in range(deep):
        later_ref[i] = current(1, i)
    residual(deep, drop_ref, lambda i: current(0, i), cross_ref, width, start_ref, scaled_ref)
    krylov(deep, width, cap_ref, grid_ref, cross_ref, scaled_ref, second_ref, basis_ref, image_ref)
    moments(deep, rows, width, start_ref, basis_ref, image_ref, sums_ref, out_ref)


def first_step(field, edge, above, below, ends, middle, count):
    rows = field.shape[2]
    width = field.shape[1] * LANES
    wide = width + LANES
    deep = (rows + 2 * HALO) // GROUP
    full = (2, deep, GROUP, wide)
    shapes = [(3, *full), full, full, full[1:], (count, LANES)]
    return pl.pallas_call(
        functools.partial(first_kernel, deep, rows, width, ends.shape[2] // 2),
        out_shape=[jax.ShapeDtypeStruct(s, jnp.float32) for s in shapes],
        in_specs=[vmem()] * 6,
        out_specs=[vmem()] * len(shapes),
        scratch_shapes=[
            pltpu.VMEM((7, wide // LANES, deep * GROUP, LANES), jnp.float32),
            pltpu.VMEM(full, jnp.float32),
            pltpu.VMEM(full, jnp.float32),
            pltpu.VMEM((2, deep, GROUP, width), jnp.float32),
            pltpu.VMEM(full, jnp.float32),
            pltpu.VMEM(full, jnp.float32),
            pltpu.VMEM((3, 2, deep, GROUP, width), jnp.float32),
            pltpu.VMEM((STEPS, 3, *full[1:]), jnp.float32),
            pltpu.VMEM((2 * GROUP, LANES), jnp.float32),
        ],
        compiler_params=params(20),
        name="first_step",
    )(field, edge, above, below, ends, middle)


def second_kernel(
    deep, rows, width,
    gathered_ref, basis_ref, drop_ref, cap_ref, later_ref,
    first_ref, next_ref, held_ref, out_ref,
    now_ref, grid_ref, cross_ref, start_ref, scaled_ref, second_ref, image_ref, natural_ref, sums_ref,
):
    wide = width + LANES
    weigh(cap_ref, deep, grid_ref, cross_ref)
    weights = [widen(c, wide) for c in weights_of(gathered_ref)]
    for l in range(2):
        for i in range(deep):
            value = drop_ref[l, i]
            for n in range(3):
                value = value + weights[n] * basis_ref[n, l, i]
            now_ref[l, i] = value
            held_ref[l, i] = value[:, :width]
            spread(natural_ref, l, i, deep, value[:, :width])
    settle(natural_ref, first_ref)
    residual(deep, now_ref, lambda i: later_ref[i], cross_ref, width, start_ref, scaled_ref)
    krylov(deep, width, cap_ref, grid_ref, cross_ref, scaled_ref, second_ref, next_ref, image_ref)
    moments(deep, rows, width, start_ref, next_ref, image_ref, sums_ref, out_ref)


def second_step(gathered, basis, drop, cap, later, rows):
    deep = cap.shape[1]
    wide = cap.shape[-1]
    width = wide - LANES
    full = (2, deep, GROUP, wide)
    shapes = [(2, rows, width), (3, *full), (2, deep, GROUP, width), gathered.shape]
    return pl.pallas_call(
        functools.partial(second_kernel, deep, rows, width),
        out_shape=[jax.ShapeDtypeStruct(s, jnp.float32) for s in shapes],
        in_specs=[vmem()] * 5,
        out_specs=[vmem()] * len(shapes),
        scratch_shapes=[
            pltpu.VMEM(full, jnp.float32),
            pltpu.VMEM(full, jnp.float32),
            pltpu.VMEM(full, jnp.float32),
            pltpu.VMEM((2, deep, GROUP, width), jnp.float32),
            pltpu.VMEM(full, jnp.float32),
            pltpu.VMEM(full, jnp.float32),
            pltpu.VMEM((3, 2, deep, GROUP, width), jnp.float32),
            pltpu.VMEM((2, width // LANES, deep * GROUP, LANES), jnp.float32),
            pltpu.VMEM((2 * GROUP, LANES), jnp.float32),
        ],
        compiler_params=params(20),
        name="second_step",
    )(gathered, basis, drop, cap, later)


def last_kernel(deep, rows, width, gathered_ref, basis_ref, held_ref, out_ref, natural_ref):
    weights = [widen(c, width) for c in weights_of(gathered_ref)]
    for l in range(2):
        for i in range(deep):
            value = held_ref[l, i]
            for n in range(3):
                value = value + weights[n] * basis_ref[n, l, i, :, pl.ds(0, width)]
            spread(natural_ref, l, i, deep, value)
    settle(natural_ref, out_ref)


def last_step(gathered, basis, held, rows):
    deep = held.shape[1]
    width = held.shape[-1]
    return pl.pallas_call(
        functools.partial(last_kernel, deep, rows, width),
        out_shape=jax.ShapeDtypeStruct((2, rows, width), jnp.float32),
        in_specs=[vmem()] * 3,
        out_specs=vmem(),
        scratch_shapes=[
            pltpu.VMEM((2, width // LANES, deep * GROUP, LANES), jnp.float32),
        ],
        compiler_params=params(12),
        name="last_step",
    )(gathered, basis, held)


def shift(block, axis, up):
    count = lax.axis_size(axis)
    pairs = [(i, i + 1) for i in range(count - 1)]
    return lax.ppermute(block, axis, pairs if up else [(b, a) for a, b in pairs])


def exchange(block):
    return lax.all_to_all(block, BOTH, 0, 0, tiled=True)


def gather_tables(block):
    outer, inner = lax.axis_size("gx"), lax.axis_size("gy")
    groups = [
        [x * inner + y for x in range(parity, outer, 2) for y in range(inner)] for parity in range(2)
    ]
    own = lax.all_to_all(block, BOTH, 0, 0, tiled=True, axis_index_groups=groups)
    own = own.reshape(-1, LANES)
    return own, lax.ppermute(own, "gx", [(i, i ^ 1) for i in range(outer)])


def shards(tables, table_index, toggle, tap_code, capacitance, prior_drop):
    rows, cols = table_index.shape
    count = lax.axis_size("gx") * lax.axis_size("gy")
    inner = lax.axis_size("gy")
    many = tables.shape[0], inner
    outer = HALO
    block, codes = address(tables, tap_code, table_index, toggle, count // 2)
    table = gather_tables(block)
    field = jnp.concatenate([capacitance, prior_drop, codes])
    field = field.reshape(-1, rows, cols // LANES, LANES).transpose(0, 2, 1, 3)
    left = shift(field[:, -1], "gy", True)
    right = shift(field[:, 0], "gy", False)
    def ends_of(array):
        return jnp.concatenate([array[:outer], array[-outer:]])

    ends, pieces = lookup(ends_of(table_index), ends_of(toggle), table, many)
    edge = edge_lookup(left, right, pieces, many)

    def late(far):
        cut = slice(-HALO, None) if far else slice(0, HALO)
        charge, lower = [a[:, :, cut].reshape(-1, HALO, LANES) for a in (ends, field[:5])]
        return jnp.concatenate([lower, charge, edge[:, cut]])

    above = shift(late(True), "gx", True)
    below = shift(late(False), "gx", False)
    pieces, edge = lax.optimization_barrier((pieces, edge))
    middle = lookup(table_index[outer:-outer], toggle[outer:-outer], (pieces,), many)
    basis, drop, cap, later, part = first_step(field, edge, above, below, ends, middle, count)
    first, basis, held, part = second_step(exchange(part), basis, drop, cap, later, rows)
    return first, last_step(exchange(part), basis, held, rows)


def solution(mesh):
    in_specs = (
        P(BOTH, None),
        P("gx", "gy"),
        P("gx", "gy"),
        P("gx", "gy"),
        P(None, "gx", "gy"),
        P(None, "gx", "gy"),
    )
    out_specs = (P(None, "gx", "gy"), P(None, "gx", "gy"))
    return jax.shard_map(shards, mesh=mesh, in_specs=in_specs, out_specs=out_specs, check_vma=False)
```

```python
import functools
import math

import jax
import jax.numpy as jnp
from jax import lax
from jax.experimental import pallas as pl
from jax.experimental.pallas import tpu as pltpu
from jax.sharding import PartitionSpec as P

SUBSTEPS = 32
STEPS = 2
BOTH = ("gx", "gy")
LANES = 128
HALO = 20
GROUP = 8
LO = 4
CONDUCT = (1.0, 4.0)


def chebyshev_taus():
    theta = 1.05
    delta = 0.95
    return [1.0 / (theta + delta * math.cos((2 * i - 1) * math.pi / 6.0)) for i in (1, 2, 3)]


TAU = chebyshev_taus()
ALPHA = TAU[1] + (1.0 - TAU[1]) * TAU[0]
BETA = TAU[0] * TAU[1]
KEEP = (1.0 - TAU[2]) * BETA / TAU[2]
SHIFT = 0.75
RADIUS = 0.7
BACK = SHIFT / TAU[2]
FORMER = 0.5 * (RADIUS / TAU[2]) ** 2


def params(mib):
    return pltpu.CompilerParams(vmem_limit_bytes=mib * 2**20)


def vmem():
    return pl.BlockSpec(memory_space=pltpu.VMEM)


def address_kernel(
    table_in, tap_in, index_in, toggle_in, out_ref, codes_ref, table_ref, cells_ref, arrived
):
    copies = [pltpu.make_async_copy(table_in, table_ref, arrived.at[3])]
    for n, source in enumerate((tap_in, index_in, toggle_in)):
        copies.append(pltpu.make_async_copy(source, cells_ref.at[n], arrived.at[n]))
    for copy in copies:
        copy.start()
    copies[0].wait()
    table = table_ref[...]
    many = table.shape[0] // LO
    block = jnp.concatenate([table[a * many : (a + 1) * many] for a in range(LO)], axis=1)
    out_ref[...] = jnp.broadcast_to(block[None], out_ref.shape)
    for n in range(3):
        copies[1 + n].wait()
        codes_ref[n] = cells_ref[n].astype(jnp.float32)


def address(table, tap, index, toggle, count):
    many = table.shape[0] // LO
    return pl.pallas_call(
        address_kernel,
        out_shape=[
            jax.ShapeDtypeStruct((count, many, LANES), jnp.float32),
            jax.ShapeDtypeStruct((3, *tap.shape), jnp.float32),
        ],
        in_specs=[pl.BlockSpec(memory_space=pl.ANY)] * 4,
        out_specs=[vmem()] * 2,
        scratch_shapes=[
            pltpu.VMEM(table.shape, jnp.float32),
            pltpu.VMEM((3, *tap.shape), jnp.int32),
            pltpu.SemaphoreType.DMA((4,)),
        ],
        compiler_params=params(62),
        name="address",
    )(table, tap, index, toggle)


MANY = 8
CHUNK = 256


def split_kernel(table_refs, pieces_ref):
    for b, ref in enumerate(table_refs):
        across = ref[...].T
        high = across.astype(jnp.bfloat16)
        low = (across - high.astype(jnp.float32)).astype(jnp.bfloat16)
        for p, piece in enumerate((high, low)):
            pieces_ref[pl.ds((2 * p + b) * LANES, LANES), :] = piece


def charges(many, index, toggle, pieces_ref):
    many, inner = many
    cols = index.shape[1]
    groups = pieces_ref.shape[1]
    quarter = many // LO
    held = index & (many - 1)
    device = index // many
    half = (device // inner + lax.axis_index("gx")) & 1
    place = device // (2 * inner) * inner + (device & (inner - 1))
    row = place * quarter + (held & (quarter - 1))
    which = held // quarter + LO * half
    hot = []
    for k in range(groups // CHUNK):
        local = (row - CHUNK * k).astype(jnp.float32).astype(jnp.bfloat16)
        count = lax.broadcasted_iota(jnp.int32, (CHUNK, cols), 0)
        count = count.astype(jnp.float32).astype(jnp.bfloat16)
        same = jnp.broadcast_to(local, (CHUNK, cols)) == count
        hot.append(jnp.where(same, jnp.bfloat16(1), jnp.bfloat16(0)))
    got = jnp.dot(pieces_ref[...], jnp.concatenate(hot, 0), preferred_element_type=jnp.float32)
    half = got.shape[0] // 2
    value = (got[:half] + got[half:]).reshape(MANY, SUBSTEPS, cols)
    chosen = value[0]
    for a in range(1, MANY):
        chosen = jnp.where(which == a, value[a], chosen)
    moment = lax.broadcasted_iota(jnp.int32, (SUBSTEPS, cols), 0) + toggle
    share = SUBSTEPS // STEPS
    means = []
    for k in range(STEPS):
        inside = (moment >= k * share) & (moment < (k + 1) * share)
        total = jnp.sum(jnp.where(inside, chosen, 0.0), axis=0, keepdims=True)
        means.append(total * (1.0 / share))
    return means


def lookup_rows(many, index_ref, toggle_ref, pieces_ref, out_ref):
    rows, cols = index_ref.shape
    for r in range(rows):
        row = pl.ds(r, 1)
        means = charges(many, index_ref[row, :], toggle_ref[row, :], pieces_ref)
        for k, mean in enumerate(means):
            for b in range(cols // LANES):
                out_ref[k, b, row, :] = mean[:, b * LANES : (b + 1) * LANES]


def first_lookup_kernel(many, index_ref, toggle_ref, own_ref, other_ref, out_ref, pieces_ref):
    split_kernel((own_ref, other_ref), pieces_ref)
    lookup_rows(many, index_ref, toggle_ref, pieces_ref, out_ref)


def lookup_cost(cells, pieces):
    flops = 2 * cells * pieces.shape[0] * pieces.shape[1]
    return pl.CostEstimate(flops=flops, bytes_accessed=0, transcendentals=0)


def lookup(index, toggle, table, many):
    rows, cols = index.shape
    charge = jax.ShapeDtypeStruct((STEPS, cols // LANES, rows, LANES), jnp.float32)
    fresh = len(table) == 2
    pieces = table[0]
    if fresh:
        pieces = jax.ShapeDtypeStruct((2 * MANY * SUBSTEPS, pieces.shape[0]), jnp.bfloat16)
    return pl.pallas_call(
        functools.partial(first_lookup_kernel if fresh else lookup_rows, many),
        out_shape=[charge, pieces] if fresh else charge,
        in_specs=[vmem()] * (2 + len(table)),
        out_specs=[vmem()] * 2 if fresh else vmem(),
        compiler_params=params(20),
        cost_estimate=lookup_cost(rows * cols, pieces),
        name="lookup",
    )(index, toggle, *table)


def edge_lookup_kernel(many, left_ref, right_ref, pieces_ref, out_ref, cells_ref, got_ref):
    rows = left_ref.shape[1]
    lane = lax.broadcasted_iota(jnp.int32, (rows, LANES), 1)

    def merge(right, left):
        return jnp.where(lane < HALO, right, jnp.where(lane >= LANES - HALO, left, 0.0))

    for f in range(5):
        out_ref[f] = merge(right_ref[f], left_ref[f])
    pair = lax.broadcasted_iota(jnp.int32, (HALO, LANES), 1)
    for n in range(2):
        near = pltpu.roll(merge(right_ref[5 + n], left_ref[5 + n]), HALO, axis=1)
        turned = jnp.concatenate([near, jnp.zeros_like(near)], axis=0).T
        high = pltpu.roll(turned[HALO : 2 * HALO], LANES - rows, axis=1)
        cells_ref[n] = jnp.where(pair < rows, turned[:HALO], high).astype(jnp.int32)
    got_ref[...] = jnp.zeros_like(got_ref)
    step = 4
    for u in range(HALO // step):
        index, toggle = [
            jnp.concatenate([cells_ref[n, pl.ds(step * u + r, 1), :] for r in range(step)], axis=1)
            for n in range(2)
        ]
        for k, mean in enumerate(charges(many, index, toggle, pieces_ref)):
            for r in range(step):
                got_ref[k, pl.ds(step * u + r, 1), :] = mean[:, r * LANES : (r + 1) * LANES]
    inside = out_ref[0] > 0.0
    for k in range(STEPS):
        back = got_ref[k].T
        left = pltpu.roll(back[:rows], LANES - HALO, axis=1)
        out_ref[5 + k] = jnp.where(inside, merge(back[rows:], left), 0.0)


def edge_lookup(left, right, pieces, many):
    rows = left.shape[1]
    assert 2 * rows == LANES
    return pl.pallas_call(
        functools.partial(edge_lookup_kernel, many),
        out_shape=jax.ShapeDtypeStruct(left.shape, jnp.float32),
        in_specs=[vmem()] * 3,
        out_specs=vmem(),
        scratch_shapes=[
            pltpu.VMEM((2, HALO, LANES), jnp.int32),
            pltpu.VMEM((STEPS, LANES, LANES), jnp.float32),
        ],
        compiler_params=params(20),
        cost_estimate=lookup_cost(2 * HALO * rows, pieces),
        name="edge_lookup",
    )(left, right, pieces)


def sweep(deep, fetch, use):
    def load(i):
        if i < 0:
            return [pltpu.roll(fetch(l, deep - 1), 1, axis=0) for l in range(2)]
        if i >= deep:
            return [pltpu.roll(fetch(l, 0), GROUP - 1, axis=0) for l in range(2)]
        return [fetch(l, i) for l in range(2)]

    held = {}
    for i in range(deep):
        held = {k: v for k, v in held.items() if k in (i - 1, i, i + 1)}
        for k in (i - 1, i, i + 1):
            if k not in held:
                held[k] = load(k)
        for l in range(2):
            center = held[i][l]
            width = center.shape[-1]
            beside = pltpu.roll(center, 1, axis=1) + pltpu.roll(center, width - 1, axis=1)
            around = (held[i - 1][l] + held[i + 1][l]) + beside
            use(l, i, center, around, held[i][1 - l])


def weigh(cap_ref, deep, grid_ref, cross_ref):
    for l in range(2):
        for i in range(deep):
            cap = cap_ref[l, i]
            inverse = jnp.where(cap > 0.0, 1.0 / (cap + (4.0 * CONDUCT[l] + 2.0)), 0.0)
            grid_ref[l, i] = CONDUCT[l] * inverse
            cross_ref[l, i] = 2.0 * inverse


def residual(deep, drop_ref, current, cross_ref, width, start_ref, scaled_ref):
    def use(l, i, center, around, other):
        value = CONDUCT[l] * around + 2.0 * other - (4.0 * CONDUCT[l] + 2.0) * center
        if l == 0:
            value = value + current(i)
        start_ref[l, i] = value[:, :width]
        scaled_ref[l, i] = value * (cross_ref[l, i] * 0.5)

    sweep(deep, lambda l, i: drop_ref[l, i], use)


def krylov(deep, width, cap_ref, grid_ref, cross_ref, scaled_ref, second_ref, basis_ref, image_ref):
    def coupled(l, i, around, other):
        return grid_ref[l, i] * around + cross_ref[l, i] * other

    def use_second(l, i, center, around, other):
        second_ref[l, i] = (ALPHA / BETA) * center + coupled(l, i, around, other)

    for n in range(3):

        def use_basis(l, i, center, around, other, n=n):
            value = KEEP * center + (
                scaled_ref[l, i] + BETA * coupled(l, i, around, other)
            )
            if n == 1:
                value = value - BACK * basis_ref[0, l, i]
            if n == 2:
                value = value - BACK * basis_ref[1, l, i] - FORMER * basis_ref[0, l, i]
            basis_ref[n, l, i] = value

        def use_image(l, i, center, around, other, n=n):
            value = center - coupled(l, i, around, other)
            if n < 2:
                scaled_ref[l, i] = value
            diagonal = cap_ref[l, i][:, :width] + (4.0 * CONDUCT[l] + 2.0)
            image_ref[n, l, i] = value[:, :width] * diagonal

        sweep(deep, lambda l, i: scaled_ref[l, i], use_second)
        sweep(deep, lambda l, i: second_ref[l, i], use_basis)
        sweep(deep, lambda l, i, n=n: basis_ref[n, l, i], use_image)


PAIRS = ((0, 0), (1, 0), (2, 0), (1, 1), (2, 1), (2, 2))


def moments(deep, rows, width, start_ref, basis_ref, image_ref, sums_ref, out_ref):
    sub = lax.broadcasted_iota(jnp.int32, (GROUP, LANES), 0)

    def body(i, totals):
        inside = sub * deep + i < rows
        part = [None] * 9
        for l in range(2):
            for b in range(width // LANES):
                lanes = pl.ds(b * LANES, LANES)
                start = start_ref[l, i, :, lanes]
                basis = [basis_ref[n, l, i, :, lanes] for n in range(3)]
                image = [image_ref[n, l, i, :, lanes] for n in range(3)]
                terms = [start * v for v in basis] + [basis[p] * image[q] for p, q in PAIRS]
                part = [t if p is None else p + t for p, t in zip(part, terms)]
        return [t + jnp.where(inside, p, 0.0) for t, p in zip(totals, part)]

    totals = [jnp.zeros((GROUP, LANES), jnp.float32)] * 9
    for i in range(deep):
        totals = body(i, totals)
    sums_ref[...] = jnp.zeros_like(sums_ref)
    for k, total in enumerate(totals):
        sums_ref[pl.ds(k, 1), :] = jnp.sum(total, axis=0, keepdims=True)
    across = jnp.sum(sums_ref[...], axis=1, keepdims=True)
    row = lax.broadcasted_iota(jnp.int32, sums_ref.shape, 0)
    lane = lax.broadcasted_iota(jnp.int32, sums_ref.shape, 1)
    row = jnp.sum(jnp.where(row == lane, across, 0.0), axis=0, keepdims=True)
    out_ref[...] = jnp.broadcast_to(row, out_ref.shape)


def weights_of(gathered_ref):
    total = jnp.sum(gathered_ref[...], axis=0, keepdims=True)
    b1, b2, b3, h11, h21, h31, h22, h32, h33 = [
        jnp.broadcast_to(total[:, k : k + 1], (GROUP, LANES)) for k in range(9)
    ]
    l21 = h21 / h11
    l31 = h31 / h11
    d2 = h22 - l21 * h21
    e32 = h32 - l31 * h21
    l32 = e32 / d2
    d3 = h33 - l31 * h31 - l32 * e32
    y2 = b2 - l21 * b1
    y3 = b3 - l31 * b1 - l32 * y2
    c3 = y3 / d3
    c2 = y2 / d2 - l32 * c3
    c1 = b1 / h11 - l21 * c2 - l31 * c3
    return c1, c2, c3


def widen(value, width):
    return jnp.concatenate([value] * (width // LANES), axis=1)


def spread(natural_ref, l, i, deep, value):
    for b in range(value.shape[1] // LANES):
        natural_ref[l, b, pl.ds(i, GROUP, stride=deep), :] = value[:, b * LANES : (b + 1) * LANES]


def settle(natural_ref, out_ref):
    for b in range(natural_ref.shape[1]):
        out_ref[:, :, pl.ds(b * LANES, LANES)] = natural_ref[:, b, : out_ref.shape[1], :]


def first_kernel(
    deep, rows, width, outer,
    field_ref, edge_ref, above_ref, below_ref, ends_ref, middle_ref,
    basis_ref, drop_ref, cap_ref, grid_ref, cross_ref, later_ref, out_ref,
    whole_ref, start_ref, scaled_ref, second_ref, image_ref, inject_ref, sums_ref,
):
    wide = width + LANES
    blocks = wide // LANES
    inner = pl.ds(0, rows)
    for f in range(7):
        whole_ref[f, blocks - 1, inner, :] = edge_ref[f]
        for b in range(blocks - 1):
            if f < 5:
                whole_ref[f, b, inner, :] = field_ref[f, b]
            else:
                end, middle = ends_ref.at[f - 5, b], middle_ref.at[f - 5, b]
                whole_ref[f, b, pl.ds(0, outer), :] = end[pl.ds(0, outer), :]
                whole_ref[f, b, pl.ds(outer, rows - 2 * outer), :] = middle[...]
                whole_ref[f, b, pl.ds(rows - outer, outer), :] = end[pl.ds(outer, outer), :]
        for ref, place in ((below_ref, pl.ds(rows, HALO)), (above_ref, pl.ds(rows + HALO, HALO))):
            for b in range(blocks - 1):
                whole_ref[f, b, place, :] = ref[f * (blocks - 1) + b]
            whole_ref[f, blocks - 1, place, :] = ref[7 * (blocks - 1) + f]

    def slab(f, i):
        pick = pl.ds(i, GROUP, stride=deep)
        return jnp.concatenate([whole_ref[f, b, pick, :] for b in range(blocks)], axis=1)

    for l in range(2):
        for i in range(deep):
            cap_ref[l, i] = slab(l, i)
            drop_ref[l, i] = slab(2 + l, i)
    weigh(cap_ref, deep, grid_ref, cross_ref)
    for i in range(deep):
        tap = slab(4, i)
        for k in range(STEPS):
            charge = slab(5 + k, i)
            for a in range(3):
                sent = [jnp.where(tap == float(3 * a + b), charge, 0.0) for b in range(3)]
                value = pltpu.roll(sent[0], wide - 1, axis=1) + sent[1] + pltpu.roll(sent[2], 1, axis=1)
                inject_ref[k, a, i] = value

    def current(k, i):
        if i == deep - 1:
            upward = pltpu.roll(inject_ref[k, 0, 0], GROUP - 1, axis=0)
        else:
            upward = inject_ref[k, 0, i + 1]
        if i == 0:
            downward = pltpu.roll(inject_ref[k, 2, deep - 1], 1, axis=0)
        else:
            downward = inject_ref[k, 2, i - 1]
        return upward + inject_ref[k, 1, i] + downward

    for i in range(deep):
        later_ref[i] = current(1, i)
    residual(deep, drop_ref, lambda i: current(0, i), cross_ref, width, start_ref, scaled_ref)
    krylov(deep, width, cap_ref, grid_ref, cross_ref, scaled_ref, second_ref, basis_ref, image_ref)
    moments(deep, rows, width, start_ref, basis_ref, image_ref, sums_ref, out_ref)


def first_step(field, edge, above, below, ends, middle, count):
    rows = field.shape[2]
    width = field.shape[1] * LANES
    wide = width + LANES
    deep = (rows + 2 * HALO) // GROUP
    full = (2, deep, GROUP, wide)
    shapes = [(3, *full), full, full, full, full, full[1:], (count, LANES)]
    return pl.pallas_call(
        functools.partial(first_kernel, deep, rows, width, ends.shape[2] // 2),
        out_shape=[jax.ShapeDtypeStruct(s, jnp.float32) for s in shapes],
        in_specs=[vmem()] * 6,
        out_specs=[vmem()] * len(shapes),
        scratch_shapes=[
            pltpu.VMEM((7, wide // LANES, deep * GROUP, LANES), jnp.float32),
            pltpu.VMEM((2, deep, GROUP, width), jnp.float32),
            pltpu.VMEM(full, jnp.float32),
            pltpu.VMEM(full, jnp.float32),
            pltpu.VMEM((3, 2, deep, GROUP, width), jnp.float32),
            pltpu.VMEM((STEPS, 3, *full[1:]), jnp.float32),
            pltpu.VMEM((2 * GROUP, LANES), jnp.float32),
        ],
        compiler_params=params(20),
        name="first_step",
    )(field, edge, above, below, ends, middle)


def second_kernel(
    deep, rows, width,
    gathered_ref, basis_ref, drop_ref, cap_ref, grid_ref, cross_ref, later_ref,
    first_ref, next_ref, held_ref, out_ref,
    now_ref, start_ref, scaled_ref, second_ref, image_ref, natural_ref, sums_ref,
):
    wide = width + LANES
    weights = [widen(c, wide) for c in weights_of(gathered_ref)]
    for l in range(2):
        for i in range(deep):
            value = drop_ref[l, i]
            for n in range(3):
                value = value + weights[n] * basis_ref[n, l, i]
            now_ref[l, i] = value
            held_ref[l, i] = value[:, :width]
            spread(natural_ref, l, i, deep, value[:, :width])
    settle(natural_ref, first_ref)
    residual(deep, now_ref, lambda i: later_ref[i], cross_ref, width, start_ref, scaled_ref)
    krylov(deep, width, cap_ref, grid_ref, cross_ref, scaled_ref, second_ref, next_ref, image_ref)
    moments(deep, rows, width, start_ref, next_ref, image_ref, sums_ref, out_ref)


def second_step(gathered, basis, drop, cap, grid, cross, later, rows):
    deep = cap.shape[1]
    wide = cap.shape[-1]
    width = wide - LANES
    full = (2, deep, GROUP, wide)
    shapes = [(2, rows, width), (3, *full), (2, deep, GROUP, width), gathered.shape]
    return pl.pallas_call(
        functools.partial(second_kernel, deep, rows, width),
        out_shape=[jax.ShapeDtypeStruct(s, jnp.float32) for s in shapes],
        in_specs=[vmem()] * 7,
        out_specs=[vmem()] * len(shapes),
        scratch_shapes=[
            pltpu.VMEM(full, jnp.float32),
            pltpu.VMEM((2, deep, GROUP, width), jnp.float32),
            pltpu.VMEM(full, jnp.float32),
            pltpu.VMEM(full, jnp.float32),
            pltpu.VMEM((3, 2, deep, GROUP, width), jnp.float32),
            pltpu.VMEM((2, width // LANES, deep * GROUP, LANES), jnp.float32),
            pltpu.VMEM((2 * GROUP, LANES), jnp.float32),
        ],
        compiler_params=params(20),
        name="second_step",
    )(gathered, basis, drop, cap, grid, cross, later)


def last_kernel(deep, rows, width, gathered_ref, basis_ref, held_ref, out_ref, natural_ref):
    weights = [widen(c, width) for c in weights_of(gathered_ref)]
    for l in range(2):
        for i in range(deep):
            value = held_ref[l, i]
            for n in range(3):
                value = value + weights[n] * basis_ref[n, l, i, :, pl.ds(0, width)]
            spread(natural_ref, l, i, deep, value)
    settle(natural_ref, out_ref)


def last_step(gathered, basis, held, rows):
    deep = held.shape[1]
    width = held.shape[-1]
    return pl.pallas_call(
        functools.partial(last_kernel, deep, rows, width),
        out_shape=jax.ShapeDtypeStruct((2, rows, width), jnp.float32),
        in_specs=[vmem()] * 3,
        out_specs=vmem(),
        scratch_shapes=[
            pltpu.VMEM((2, width // LANES, deep * GROUP, LANES), jnp.float32),
        ],
        compiler_params=params(12),
        name="last_step",
    )(gathered, basis, held)


def shift(block, axis, up):
    count = lax.axis_size(axis)
    pairs = [(i, i + 1) for i in range(count - 1)]
    return lax.ppermute(block, axis, pairs if up else [(b, a) for a, b in pairs])


def exchange(block):
    return lax.all_to_all(block, BOTH, 0, 0, tiled=True)


def gather_tables(block):
    outer, inner = lax.axis_size("gx"), lax.axis_size("gy")
    groups = [
        [x * inner + y for x in range(parity, outer, 2) for y in range(inner)] for parity in range(2)
    ]
    own = lax.all_to_all(block, BOTH, 0, 0, tiled=True, axis_index_groups=groups)
    own = own.reshape(-1, LANES)
    return own, lax.ppermute(own, "gx", [(i, i ^ 1) for i in range(outer)])


def shards(tables, table_index, toggle, tap_code, capacitance, prior_drop):
    rows, cols = table_index.shape
    count = lax.axis_size("gx") * lax.axis_size("gy")
    inner = lax.axis_size("gy")
    many = tables.shape[0], inner
    outer = HALO
    block, codes = address(tables, tap_code, table_index, toggle, count // 2)
    table = gather_tables(block)
    field = jnp.concatenate([capacitance, prior_drop, codes])
    field = field.reshape(-1, rows, cols // LANES, LANES).transpose(0, 2, 1, 3)
    left = shift(field[:, -1], "gy", True)
    right = shift(field[:, 0], "gy", False)
    def ends_of(array):
        return jnp.concatenate([array[:outer], array[-outer:]])

    ends, pieces = lookup(ends_of(table_index), ends_of(toggle), table, many)
    edge = edge_lookup(left, right, pieces, many)

    def late(far):
        cut = slice(-HALO, None) if far else slice(0, HALO)
        charge, lower = [a[:, :, cut].reshape(-1, HALO, LANES) for a in (ends, field[:5])]
        return jnp.concatenate([lower, charge, edge[:, cut]])

    above = shift(late(True), "gx", True)
    below = shift(late(False), "gx", False)
    pieces, edge = lax.optimization_barrier((pieces, edge))
    middle = lookup(table_index[outer:-outer], toggle[outer:-outer], (pieces,), many)
    basis, *state, part = first_step(field, edge, above, below, ends, middle, count)
    first, basis, held, part = second_step(exchange(part), basis, *state, rows)
    return first, last_step(exchange(part), basis, held, rows)


def solution(mesh):
    in_specs = (
        P(BOTH, None),
        P("gx", "gy"),
        P("gx", "gy"),
        P("gx", "gy"),
        P(None, "gx", "gy"),
        P(None, "gx", "gy"),
    )
    out_specs = (P(None, "gx", "gy"), P(None, "gx", "gy"))
    return jax.shard_map(shards, mesh=mesh, in_specs=in_specs, out_specs=out_specs, check_vma=False)
```

```python
import functools
import math

import jax
import jax.numpy as jnp
from jax import lax
from jax.experimental import pallas as pl
from jax.experimental.pallas import tpu as pltpu
from jax.sharding import PartitionSpec as P

SUBSTEPS = 32
STEPS = 2
BOTH = ("gx", "gy")
LANES = 128
HALO = 20
GROUP = 8
LO = 4
CONDUCT = (1.0, 4.0)


def chebyshev_taus():
    theta = 1.05
    delta = 0.95
    return [1.0 / (theta + delta * math.cos((2 * i - 1) * math.pi / 6.0)) for i in (1, 2, 3)]


TAU = chebyshev_taus()
ALPHA = TAU[1] + (1.0 - TAU[1]) * TAU[0]
BETA = TAU[0] * TAU[1]
KEEP = (1.0 - TAU[2]) * BETA / TAU[2]
SHIFT = 0.75
RADIUS = 0.7
BACK = SHIFT / TAU[2]
FORMER = 0.5 * (RADIUS / TAU[2]) ** 2


def params(mib):
    return pltpu.CompilerParams(vmem_limit_bytes=mib * 2**20)


def vmem():
    return pl.BlockSpec(memory_space=pltpu.VMEM)


def address_kernel(
    table_in, tap_in, index_in, toggle_in, out_ref, codes_ref, table_ref, cells_ref, arrived
):
    copies = [pltpu.make_async_copy(table_in, table_ref, arrived.at[3])]
    for n, source in enumerate((tap_in, index_in, toggle_in)):
        copies.append(pltpu.make_async_copy(source, cells_ref.at[n], arrived.at[n]))
    for copy in copies:
        copy.start()
    copies[0].wait()
    table = table_ref[...]
    many = table.shape[0] // LO
    block = jnp.concatenate([table[a * many : (a + 1) * many] for a in range(LO)], axis=1)
    out_ref[...] = jnp.broadcast_to(block[None], out_ref.shape)
    for n in range(3):
        copies[1 + n].wait()
        codes_ref[n] = cells_ref[n].astype(jnp.float32)


def address(table, tap, index, toggle, count):
    many = table.shape[0] // LO
    return pl.pallas_call(
        address_kernel,
        out_shape=[
            jax.ShapeDtypeStruct((count, many, LANES), jnp.float32),
            jax.ShapeDtypeStruct((3, *tap.shape), jnp.float32),
        ],
        in_specs=[pl.BlockSpec(memory_space=pl.ANY)] * 4,
        out_specs=[vmem()] * 2,
        scratch_shapes=[
            pltpu.VMEM(table.shape, jnp.float32),
            pltpu.VMEM((3, *tap.shape), jnp.int32),
            pltpu.SemaphoreType.DMA((4,)),
        ],
        compiler_params=params(62),
        name="address",
    )(table, tap, index, toggle)


MANY = 8
CHUNK = 256


def split_kernel(table_refs, pieces_ref):
    for b, ref in enumerate(table_refs):
        across = ref[...].T
        high = across.astype(jnp.bfloat16)
        low = (across - high.astype(jnp.float32)).astype(jnp.bfloat16)
        for p, piece in enumerate((high, low)):
            pieces_ref[pl.ds((2 * p + b) * LANES, LANES), :] = piece


def charges(many, index, toggle, pieces_ref):
    many, inner = many
    cols = index.shape[1]
    groups = pieces_ref.shape[1]
    quarter = many // LO
    held = index & (many - 1)
    device = index // many
    half = (device // inner + lax.axis_index("gx")) & 1
    place = device // (2 * inner) * inner + (device & (inner - 1))
    row = place * quarter + (held & (quarter - 1))
    which = held // quarter + LO * half
    hot = []
    for k in range(groups // CHUNK):
        local = (row - CHUNK * k).astype(jnp.float32).astype(jnp.bfloat16)
        count = lax.broadcasted_iota(jnp.int32, (CHUNK, cols), 0)
        count = count.astype(jnp.float32).astype(jnp.bfloat16)
        same = jnp.broadcast_to(local, (CHUNK, cols)) == count
        hot.append(jnp.where(same, jnp.bfloat16(1), jnp.bfloat16(0)))
    got = jnp.dot(pieces_ref[...], jnp.concatenate(hot, 0), preferred_element_type=jnp.float32)
    half = got.shape[0] // 2
    value = (got[:half] + got[half:]).reshape(MANY, SUBSTEPS, cols)
    chosen = value[0]
    for a in range(1, MANY):
        chosen = jnp.where(which == a, value[a], chosen)
    moment = lax.broadcasted_iota(jnp.int32, (SUBSTEPS, cols), 0) + toggle
    share = SUBSTEPS // STEPS
    means = []
    for k in range(STEPS):
        inside = moment < (k + 1) * share
        if k:
            inside &= moment >= k * share
        total = jnp.sum(jnp.where(inside, chosen, 0.0), axis=0, keepdims=True)
        means.append(total * (1.0 / share))
    return means


def lookup_rows(many, index_ref, toggle_ref, pieces_ref, out_ref):
    rows, cols = index_ref.shape
    for r in range(rows):
        row = pl.ds(r, 1)
        means = charges(many, index_ref[row, :], toggle_ref[row, :], pieces_ref)
        for k, mean in enumerate(means):
            for b in range(cols // LANES):
                out_ref[k, b, row, :] = mean[:, b * LANES : (b + 1) * LANES]


def first_lookup_kernel(many, index_ref, toggle_ref, own_ref, other_ref, out_ref, pieces_ref):
    split_kernel((own_ref, other_ref), pieces_ref)
    lookup_rows(many, index_ref, toggle_ref, pieces_ref, out_ref)


def lookup_cost(cells, pieces):
    flops = 2 * cells * pieces.shape[0] * pieces.shape[1]
    return pl.CostEstimate(flops=flops, bytes_accessed=0, transcendentals=0)


def lookup(index, toggle, table, many):
    rows, cols = index.shape
    charge = jax.ShapeDtypeStruct((STEPS, cols // LANES, rows, LANES), jnp.float32)
    fresh = len(table) == 2
    pieces = table[0]
    if fresh:
        pieces = jax.ShapeDtypeStruct((2 * MANY * SUBSTEPS, pieces.shape[0]), jnp.bfloat16)
    return pl.pallas_call(
        functools.partial(first_lookup_kernel if fresh else lookup_rows, many),
        out_shape=[charge, pieces] if fresh else charge,
        in_specs=[vmem()] * (2 + len(table)),
        out_specs=[vmem()] * 2 if fresh else vmem(),
        compiler_params=params(20),
        cost_estimate=lookup_cost(rows * cols, pieces),
        name="lookup",
    )(index, toggle, *table)


def edge_lookup_kernel(many, left_ref, right_ref, pieces_ref, out_ref, cells_ref, got_ref):
    rows = left_ref.shape[1]
    lane = lax.broadcasted_iota(jnp.int32, (rows, LANES), 1)

    def merge(right, left):
        return jnp.where(lane < HALO, right, jnp.where(lane >= LANES - HALO, left, 0.0))

    for f in range(5):
        out_ref[f] = merge(right_ref[f], left_ref[f])
    pair = lax.broadcasted_iota(jnp.int32, (HALO, LANES), 1)
    for n in range(2):
        near = pltpu.roll(merge(right_ref[5 + n], left_ref[5 + n]), HALO, axis=1)
        turned = jnp.concatenate([near, jnp.zeros_like(near)], axis=0).T
        high = pltpu.roll(turned[HALO : 2 * HALO], LANES - rows, axis=1)
        cells_ref[n] = jnp.where(pair < rows, turned[:HALO], high).astype(jnp.int32)
    got_ref[...] = jnp.zeros_like(got_ref)
    step = 4
    for u in range(HALO // step):
        index, toggle = [
            jnp.concatenate([cells_ref[n, pl.ds(step * u + r, 1), :] for r in range(step)], axis=1)
            for n in range(2)
        ]
        for k, mean in enumerate(charges(many, index, toggle, pieces_ref)):
            for r in range(step):
                got_ref[k, pl.ds(step * u + r, 1), :] = mean[:, r * LANES : (r + 1) * LANES]
    inside = out_ref[0] > 0.0
    for k in range(STEPS):
        back = got_ref[k].T
        left = pltpu.roll(back[:rows], LANES - HALO, axis=1)
        out_ref[5 + k] = jnp.where(inside, merge(back[rows:], left), 0.0)


def edge_lookup(left, right, pieces, many):
    rows = left.shape[1]
    assert 2 * rows == LANES
    return pl.pallas_call(
        functools.partial(edge_lookup_kernel, many),
        out_shape=jax.ShapeDtypeStruct(left.shape, jnp.float32),
        in_specs=[vmem()] * 3,
        out_specs=vmem(),
        scratch_shapes=[
            pltpu.VMEM((2, HALO, LANES), jnp.int32),
            pltpu.VMEM((STEPS, LANES, LANES), jnp.float32),
        ],
        compiler_params=params(20),
        cost_estimate=lookup_cost(2 * HALO * rows, pieces),
        name="edge_lookup",
    )(left, right, pieces)


def sweep(deep, fetch, use):
    def load(i):
        if i < 0:
            return [pltpu.roll(fetch(l, deep - 1), 1, axis=0) for l in range(2)]
        if i >= deep:
            return [pltpu.roll(fetch(l, 0), GROUP - 1, axis=0) for l in range(2)]
        return [fetch(l, i) for l in range(2)]

    held = {}
    for i in range(deep):
        held = {k: v for k, v in held.items() if k in (i - 1, i, i + 1)}
        for k in (i - 1, i, i + 1):
            if k not in held:
                held[k] = load(k)
        for l in range(2):
            center = held[i][l]
            width = center.shape[-1]
            beside = pltpu.roll(center, 1, axis=1) + pltpu.roll(center, width - 1, axis=1)
            around = (held[i - 1][l] + held[i + 1][l]) + beside
            use(l, i, center, around, held[i][1 - l])


def weigh(cap_ref, deep, grid_ref, cross_ref):
    for l in range(2):
        for i in range(deep):
            cap = cap_ref[l, i]
            inverse = jnp.where(cap > 0.0, 1.0 / (cap + (4.0 * CONDUCT[l] + 2.0)), 0.0)
            grid_ref[l, i] = CONDUCT[l] * inverse
            cross_ref[l, i] = 2.0 * inverse


def residual(deep, drop_ref, current, cross_ref, width, start_ref, scaled_ref):
    def use(l, i, center, around, other):
        value = CONDUCT[l] * around + 2.0 * other - (4.0 * CONDUCT[l] + 2.0) * center
        if l == 0:
            value = value + current(i)
        start_ref[l, i] = value[:, :width]
        scaled_ref[l, i] = value * (cross_ref[l, i] * 0.5)

    sweep(deep, lambda l, i: drop_ref[l, i], use)


def krylov(deep, width, cap_ref, grid_ref, cross_ref, scaled_ref, second_ref, basis_ref, image_ref):
    def coupled(l, i, around, other):
        return grid_ref[l, i] * around + cross_ref[l, i] * other

    def use_second(l, i, center, around, other):
        second_ref[l, i] = (ALPHA / BETA) * center + coupled(l, i, around, other)

    for n in range(3):

        def use_basis(l, i, center, around, other, n=n):
            value = KEEP * center + (
                scaled_ref[l, i] + BETA * coupled(l, i, around, other)
            )
            if n == 1:
                value = value - BACK * basis_ref[0, l, i]
            if n == 2:
                value = value - BACK * basis_ref[1, l, i] - FORMER * basis_ref[0, l, i]
            basis_ref[n, l, i] = value

        def use_image(l, i, center, around, other, n=n):
            value = center - coupled(l, i, around, other)
            if n < 2:
                scaled_ref[l, i] = value
            diagonal = cap_ref[l, i][:, :width] + (4.0 * CONDUCT[l] + 2.0)
            image_ref[n, l, i] = value[:, :width] * diagonal

        sweep(deep, lambda l, i: scaled_ref[l, i], use_second)
        sweep(deep, lambda l, i: second_ref[l, i], use_basis)
        sweep(deep, lambda l, i, n=n: basis_ref[n, l, i], use_image)


PAIRS = ((0, 0), (1, 0), (2, 0), (1, 1), (2, 1), (2, 2))


def moments(deep, rows, width, start_ref, basis_ref, image_ref, sums_ref, out_ref):
    sub = lax.broadcasted_iota(jnp.int32, (GROUP, LANES), 0)

    def body(i, totals):
        inside = sub * deep + i < rows
        part = [None] * 9
        for l in range(2):
            for b in range(width // LANES):
                lanes = pl.ds(b * LANES, LANES)
                start = start_ref[l, i, :, lanes]
                basis = [basis_ref[n, l, i, :, lanes] for n in range(3)]
                image = [image_ref[n, l, i, :, lanes] for n in range(3)]
                terms = [start * v for v in basis] + [basis[p] * image[q] for p, q in PAIRS]
                part = [t if p is None else p + t for p, t in zip(part, terms)]
        return [t + jnp.where(inside, p, 0.0) for t, p in zip(totals, part)]

    totals = lax.fori_loop(0, deep, body, [jnp.zeros((GROUP, LANES), jnp.float32)] * 9)
    sums_ref[...] = jnp.zeros_like(sums_ref)
    for k, total in enumerate(totals):
        sums_ref[pl.ds(k, 1), :] = jnp.sum(total, axis=0, keepdims=True)
    across = jnp.sum(sums_ref[...], axis=1, keepdims=True)
    row = lax.broadcasted_iota(jnp.int32, sums_ref.shape, 0)
    lane = lax.broadcasted_iota(jnp.int32, sums_ref.shape, 1)
    row = jnp.sum(jnp.where(row == lane, across, 0.0), axis=0, keepdims=True)
    out_ref[...] = jnp.broadcast_to(row, out_ref.shape)


def weights_of(gathered_ref):
    total = jnp.sum(gathered_ref[...], axis=0, keepdims=True)
    b1, b2, b3, h11, h21, h31, h22, h32, h33 = [
        jnp.broadcast_to(total[:, k : k + 1], (GROUP, LANES)) for k in range(9)
    ]
    l21 = h21 / h11
    l31 = h31 / h11
    d2 = h22 - l21 * h21
    e32 = h32 - l31 * h21
    l32 = e32 / d2
    d3 = h33 - l31 * h31 - l32 * e32
    y2 = b2 - l21 * b1
    y3 = b3 - l31 * b1 - l32 * y2
    c3 = y3 / d3
    c2 = y2 / d2 - l32 * c3
    c1 = b1 / h11 - l21 * c2 - l31 * c3
    return c1, c2, c3


def widen(value, width):
    return jnp.concatenate([value] * (width // LANES), axis=1)


def spread(natural_ref, l, i, deep, value):
    for b in range(value.shape[1] // LANES):
        natural_ref[l, b, pl.ds(i, GROUP, stride=deep), :] = value[:, b * LANES : (b + 1) * LANES]


def settle(natural_ref, out_ref):
    for b in range(natural_ref.shape[1]):
        out_ref[:, :, pl.ds(b * LANES, LANES)] = natural_ref[:, b, : out_ref.shape[1], :]


def first_kernel(
    deep, rows, width, outer,
    field_ref, edge_ref, above_ref, below_ref, ends_ref, middle_ref,
    basis_ref, drop_ref, cap_ref, later_ref, out_ref,
    whole_ref, grid_ref, cross_ref, start_ref, scaled_ref, second_ref, image_ref, inject_ref, sums_ref,
):
    wide = width + LANES
    blocks = wide // LANES
    inner = pl.ds(0, rows)
    for f in range(7):
        whole_ref[f, blocks - 1, inner, :] = edge_ref[f]
        for b in range(blocks - 1):
            if f < 5:
                whole_ref[f, b, inner, :] = field_ref[f, b]
            else:
                end, middle = ends_ref.at[f - 5, b], middle_ref.at[f - 5, b]
                whole_ref[f, b, pl.ds(0, outer), :] = end[pl.ds(0, outer), :]
                whole_ref[f, b, pl.ds(outer, rows - 2 * outer), :] = middle[...]
                whole_ref[f, b, pl.ds(rows - outer, outer), :] = end[pl.ds(outer, outer), :]
        for ref, place in ((below_ref, pl.ds(rows, HALO)), (above_ref, pl.ds(rows + HALO, HALO))):
            for b in range(blocks - 1):
                whole_ref[f, b, place, :] = ref[f * (blocks - 1) + b]
            whole_ref[f, blocks - 1, place, :] = ref[7 * (blocks - 1) + f]

    def slab(f, i):
        pick = pl.ds(i, GROUP, stride=deep)
        return jnp.concatenate([whole_ref[f, b, pick, :] for b in range(blocks)], axis=1)

    for l in range(2):
        for i in range(deep):
            cap_ref[l, i] = slab(l, i)
            drop_ref[l, i] = slab(2 + l, i)
    weigh(cap_ref, deep, grid_ref, cross_ref)
    for i in range(deep):
        tap = slab(4, i)
        for k in range(STEPS):
            charge = slab(5 + k, i)
            for a in range(3):
                sent = [jnp.where(tap == float(3 * a + b), charge, 0.0) for b in range(3)]
                value = pltpu.roll(sent[0], wide - 1, axis=1) + sent[1] + pltpu.roll(sent[2], 1, axis=1)
                inject_ref[k, a, i] = value

    def current(k, i):
        if i == deep - 1:
            upward = pltpu.roll(inject_ref[k, 0, 0], GROUP - 1, axis=0)
        else:
            upward = inject_ref[k, 0, i + 1]
        if i == 0:
            downward = pltpu.roll(inject_ref[k, 2, deep - 1], 1, axis=0)
        else:
            downward = inject_ref[k, 2, i - 1]
        return upward + inject_ref[k, 1, i] + downward

    for i in range(deep):
        later_ref[i] = current(1, i)
    residual(deep, drop_ref, lambda i: current(0, i), cross_ref, width, start_ref, scaled_ref)
    krylov(deep, width, cap_ref, grid_ref, cross_ref, scaled_ref, second_ref, basis_ref, image_ref)
    moments(deep, rows, width, start_ref, basis_ref, image_ref, sums_ref, out_ref)


def first_step(field, edge, above, below, ends, middle, count):
    rows = field.shape[2]
    width = field.shape[1] * LANES
    wide = width + LANES
    deep = (rows + 2 * HALO) // GROUP
    full = (2, deep, GROUP, wide)
    shapes = [(3, *full), full, full, full[1:], (count, LANES)]
    return pl.pallas_call(
        functools.partial(first_kernel, deep, rows, width, ends.shape[2] // 2),
        out_shape=[jax.ShapeDtypeStruct(s, jnp.float32) for s in shapes],
        in_specs=[vmem()] * 6,
        out_specs=[vmem()] * len(shapes),
        scratch_shapes=[
            pltpu.VMEM((7, wide // LANES, deep * GROUP, LANES), jnp.float32),
            pltpu.VMEM(full, jnp.float32),
            pltpu.VMEM(full, jnp.float32),
            pltpu.VMEM((2, deep, GROUP, width), jnp.float32),
            pltpu.VMEM(full, jnp.float32),
            pltpu.VMEM(full, jnp.float32),
            pltpu.VMEM((3, 2, deep, GROUP, width), jnp.float32),
            pltpu.VMEM((STEPS, 3, *full[1:]), jnp.float32),
            pltpu.VMEM((2 * GROUP, LANES), jnp.float32),
        ],
        compiler_params=params(20),
        name="first_step",
    )(field, edge, above, below, ends, middle)


def second_kernel(
    deep, rows, width,
    gathered_ref, basis_ref, drop_ref, cap_ref, later_ref,
    first_ref, next_ref, held_ref, out_ref,
    now_ref, grid_ref, cross_ref, start_ref, scaled_ref, second_ref, image_ref, natural_ref, sums_ref,
):
    wide = width + LANES
    weigh(cap_ref, deep, grid_ref, cross_ref)
    weights = [widen(c, wide) for c in weights_of(gathered_ref)]
    for l in range(2):
        for i in range(deep):
            value = drop_ref[l, i]
            for n in range(3):
                value = value + weights[n] * basis_ref[n, l, i]
            now_ref[l, i] = value
            held_ref[l, i] = value[:, :width]
            spread(natural_ref, l, i, deep, value[:, :width])
    settle(natural_ref, first_ref)
    residual(deep, now_ref, lambda i: later_ref[i], cross_ref, width, start_ref, scaled_ref)
    krylov(deep, width, cap_ref, grid_ref, cross_ref, scaled_ref, second_ref, next_ref, image_ref)
    moments(deep, rows, width, start_ref, next_ref, image_ref, sums_ref, out_ref)


def second_step(gathered, basis, drop, cap, later, rows):
    deep = cap.shape[1]
    wide = cap.shape[-1]
    width = wide - LANES
    full = (2, deep, GROUP, wide)
    shapes = [(2, rows, width), (3, *full), (2, deep, GROUP, width), gathered.shape]
    return pl.pallas_call(
        functools.partial(second_kernel, deep, rows, width),
        out_shape=[jax.ShapeDtypeStruct(s, jnp.float32) for s in shapes],
        in_specs=[vmem()] * 5,
        out_specs=[vmem()] * len(shapes),
        scratch_shapes=[
            pltpu.VMEM(full, jnp.float32),
            pltpu.VMEM(full, jnp.float32),
            pltpu.VMEM(full, jnp.float32),
            pltpu.VMEM((2, deep, GROUP, width), jnp.float32),
            pltpu.VMEM(full, jnp.float32),
            pltpu.VMEM(full, jnp.float32),
            pltpu.VMEM((3, 2, deep, GROUP, width), jnp.float32),
            pltpu.VMEM((2, width // LANES, deep * GROUP, LANES), jnp.float32),
            pltpu.VMEM((2 * GROUP, LANES), jnp.float32),
        ],
        compiler_params=params(20),
        name="second_step",
    )(gathered, basis, drop, cap, later)


def last_kernel(deep, rows, width, gathered_ref, basis_ref, held_ref, out_ref, natural_ref):
    weights = [widen(c, width) for c in weights_of(gathered_ref)]
    for l in range(2):
        for i in range(deep):
            value = held_ref[l, i]
            for n in range(3):
                value = value + weights[n] * basis_ref[n, l, i, :, pl.ds(0, width)]
            spread(natural_ref, l, i, deep, value)
    settle(natural_ref, out_ref)


def last_step(gathered, basis, held, rows):
    deep = held.shape[1]
    width = held.shape[-1]
    return pl.pallas_call(
        functools.partial(last_kernel, deep, rows, width),
        out_shape=jax.ShapeDtypeStruct((2, rows, width), jnp.float32),
        in_specs=[vmem()] * 3,
        out_specs=vmem(),
        scratch_shapes=[
            pltpu.VMEM((2, width // LANES, deep * GROUP, LANES), jnp.float32),
        ],
        compiler_params=params(12),
        name="last_step",
    )(gathered, basis, held)


def shift(block, axis, up):
    count = lax.axis_size(axis)
    pairs = [(i, i + 1) for i in range(count - 1)]
    return lax.ppermute(block, axis, pairs if up else [(b, a) for a, b in pairs])


def exchange(block):
    return lax.all_to_all(block, BOTH, 0, 0, tiled=True)


def gather_tables(block):
    outer, inner = lax.axis_size("gx"), lax.axis_size("gy")
    groups = [
        [x * inner + y for x in range(parity, outer, 2) for y in range(inner)] for parity in range(2)
    ]
    own = lax.all_to_all(block, BOTH, 0, 0, tiled=True, axis_index_groups=groups)
    own = own.reshape(-1, LANES)
    return own, lax.ppermute(own, "gx", [(i, i ^ 1) for i in range(outer)])


def shards(tables, table_index, toggle, tap_code, capacitance, prior_drop):
    rows, cols = table_index.shape
    count = lax.axis_size("gx") * lax.axis_size("gy")
    inner = lax.axis_size("gy")
    many = tables.shape[0], inner
    outer = HALO
    block, codes = address(tables, tap_code, table_index, toggle, count // 2)
    table = gather_tables(block)
    field = jnp.concatenate([capacitance, prior_drop, codes])
    field = field.reshape(-1, rows, cols // LANES, LANES).transpose(0, 2, 1, 3)
    left = shift(field[:, -1], "gy", True)
    right = shift(field[:, 0], "gy", False)
    def ends_of(array):
        return jnp.concatenate([array[:outer], array[-outer:]])

    ends, pieces = lookup(ends_of(table_index), ends_of(toggle), table, many)
    edge = edge_lookup(left, right, pieces, many)

    def late(far):
        cut = slice(-HALO, None) if far else slice(0, HALO)
        charge, lower = [a[:, :, cut].reshape(-1, HALO, LANES) for a in (ends, field[:5])]
        return jnp.concatenate([lower, charge, edge[:, cut]])

    above = shift(late(True), "gx", True)
    below = shift(late(False), "gx", False)
    pieces, edge = lax.optimization_barrier((pieces, edge))
    middle = lookup(table_index[outer:-outer], toggle[outer:-outer], (pieces,), many)
    basis, drop, cap, later, part = first_step(field, edge, above, below, ends, middle, count)
    first, basis, held, part = second_step(exchange(part), basis, drop, cap, later, rows)
    return first, last_step(exchange(part), basis, held, rows)


def solution(mesh):
    in_specs = (
        P(BOTH, None),
        P("gx", "gy"),
        P("gx", "gy"),
        P("gx", "gy"),
        P(None, "gx", "gy"),
        P(None, "gx", "gy"),
    )
    out_specs = (P(None, "gx", "gy"), P(None, "gx", "gy"))
    return jax.shard_map(shards, mesh=mesh, in_specs=in_specs, out_specs=out_specs, check_vma=False)
```
